256 devices in a mesh: ctx: 16 (over y, x_hi, core), exp: 16 (over z, x_lo).
Axes of the slice: x: 4 (x_hi: 2, x_lo: 2; x = x_hi * 2 + x_lo), y: 4, z: 8, core: 2. Of those that a mesh axis runs over, the one named last changes fastest.
Arguments:
- queries: bfloat16 [32768, 16, 128], P(('ctx', 'exp')), may hold values from -6 to 6
- key_tensor: bfloat16 [32768, 2, 128], P(('ctx', 'exp')), may hold values from -6 to 6
- value_tensor: bfloat16 [32768, 2, 128], P(('ctx', 'exp')), may hold values from -6 to 6
- out_grad: bfloat16 [32768, 16, 128], P(('ctx', 'exp')), may hold values from -120 to 120
- log_norm: float32 [32768, 16], P(('ctx', 'exp')), may hold values from 6.5 to 8
- out_dot: float32 [32768, 16], P(('ctx', 'exp')), may hold values from -1200 to 1200
- span_order: int32 [32], replicated, may hold values from 0 to 31, each once
- moe_input: bfloat16 [32768, 2048], P(('ctx', 'exp')), may hold values from -6 to 6
- moe_grad: bfloat16 [32768, 2048], P(('ctx', 'exp')), may hold values from -60 to 60
- expert_ids: int32 [32768, 8], P(('ctx', 'exp')), may hold values from 0 to 127, all different within a row; in each aligned block of 128 rows (0 to 127, 128 to 255, ...) at most 10 rows name the same one
- keep_mask: int32 [32768, 8], P(('ctx', 'exp')), may hold values 0 or 1
- route_weight: float32 [32768, 8], P(('ctx', 'exp')), may hold values from 0.03 to 0.5
- w_gate: bfloat16 [16, 2048, 768], P('exp'), may hold values from -0.125 to 0.125
- w_up: bfloat16 [16, 2048, 768], P('exp'), may hold values from -0.125 to 0.125
- w_down: bfloat16 [16, 768, 2048], P('exp'), may hold values from -0.21875 to 0.21875
Outputs:
- grad_queries: bfloat16 [32768, 16, 128], P(('ctx', 'exp'))
- grad_keys: bfloat16 [32768, 2, 128], P(('ctx', 'exp'))
- grad_values: bfloat16 [32768, 2, 128], P(('ctx', 'exp'))
- grad_moe_input: bfloat16 [32768, 2048], P(('ctx', 'exp'))
The draws below stay inside these ranges and needn't reach their ends.
Inputs may be any that keep to these rules, and one draw needn't show every extreme that they name: `span_order`: each span number appears once. `expert_ids`: the 8 ids of a row differ; within the rows of one device (aligned blocks of 128 rows) no expert is named by more than 10 rows, a bound that some block reaches.
All inputs are finite; a program needn't handle non-finite values. No bound on the sum of `keep_mask` on one device may be relied on, other than what follows from the above.
Results may differ from the reference program's by a relative error of at most 0.0058.
Values may be sent and summed in bfloat16 or wider, within the bound.
No kernel may reach another device: no remote copies, remote signals or barrier semaphores. Data moves between devices by JAX's collectives and lax.ppermute only.
A program may use at most 128 MiB of HBM per device.

```python
import math
import jax
import jax.numpy as jnp
import numpy as np
from jax import lax

D = 2048
QUERY_HEADS = 16
KEY_VALUE_HEADS = 2
HEAD_DIMENSION = 128
EXPERTS = 128
TOPK = 8
FFE = 768
T_DEV = 128
SLOT = 10
TOKEN_TOTAL = 32768
N_CTX = 16
N_EXP = 16


def touch_ends(values, own_key, least, largest):
    spot = [jax.random.randint(jax.random.fold_in(own_key, axis), (), 0, length) for axis, length in enumerate(values.shape)]
    main_axis = values.shape.index(max(values.shape))
    neighbour = spot[:main_axis] + [(spot[main_axis] + 1) % values.shape[main_axis]] + spot[main_axis + 1:]
    return values.at[tuple(spot)].set(least).at[tuple(neighbour)].set(largest)


def levels(key, dims, split, least, top_value):
    level = 1.0
    for dim, parts in split:
        steps = jax.random.uniform(jax.random.fold_in(jax.random.fold_in(key, 6), dim), (parts,), jnp.float32, least / len(split), top_value / len(split))
        level = level * jnp.repeat(jnp.exp(steps), dims[dim] // parts).reshape((-1,) + (1,) * (len(dims) - 1 - dim))
    return level


def shared_out(rng, own, number, rows, number_of, top, bound, lean):
    sequence = jax.random.permutation(rng, number_of)
    heavy_load, ordinary = portions_of(number_of, rows * top, bound, lean, True), portions_of(number_of, rows * top, bound, lean, False)
    places = jnp.arange(number_of)

    def named(tallies, rotation):
        used = int((tallies > 0).sum())
        fixed = max(1, used // 4)
        passed = fixed + (places - fixed + rotation * (used - fixed)) % max(1, number_of - fixed)
        return jnp.zeros((number_of,), jnp.int32).at[sequence[jnp.where(places < fixed, places, passed)]].set(jnp.asarray(tallies, jnp.int32))

    tallies = jnp.where(number % 4 == 0, named(heavy_load, number // 4), named(ordinary, number - number // 4 - 1))
    mixed = jax.random.permutation(jax.random.fold_in(own, 3), number_of)
    donor, sink = mixed[0:number_of // 2 * 2:2], mixed[1:number_of // 2 * 2:2]
    room = jnp.minimum(tallies[donor] - 1, bound - tallies[sink]) // 2
    room = jnp.where((donor == sequence[0]) | (sink == sequence[0]) | (tallies[sink] == 0), 0, jnp.maximum(room, 0))
    passed = jax.random.randint(jax.random.fold_in(own, 4), (number_of // 2,), 0, 1 << 20) % (room + 1)
    tallies = tallies.at[donor].add(-passed).at[sink].add(passed)
    members = jnp.searchsorted(jnp.cumsum(tallies), jnp.arange(rows * top), side="right").astype(jnp.int32)
    table = members.reshape(top, rows).T
    table = table[jax.random.permutation(jax.random.fold_in(own, 1), rows)]
    rotation = jax.random.randint(jax.random.fold_in(own, 2), (rows, 1), 0, top)
    return jnp.take_along_axis(table, (jnp.arange(top)[None, :] + rotation) % top, axis=1)


def portions_of(amount, total, reach, slope, full):
    loads = [(1 << 20) // math.isqrt(standing ** slope) + 1 for standing in range(1, amount + 1)]
    largest = reach if full else min(reach, max(-(-total // amount), total * loads[0] // sum(loads)))
    least = 1 if total - largest >= amount - 1 else 0
    holding, spare = [largest] + [least] * (amount - 1), total - largest - least * (amount - 1)
    while spare > 0:
        candidates = [i for i in range(1, amount) if holding[i] < largest] or [i for i in range(1, amount) if holding[i] < reach]
        whole, left = sum([loads[i] for i in candidates]), spare
        for i in candidates:
            addition = min(reach - holding[i], max(1, left * loads[i] // whole), spare)
            holding[i] = holding[i] + addition
            spare = spare - addition
    return np.array(holding)


def noise(stream_key, extent, scale, bound, split=(), held_as=jnp.bfloat16):
    values = jax.random.normal(stream_key, extent, jnp.float32) * scale
    if len(split) > 0:
        values = levels(stream_key, extent, split, -0.22, 0.18) * values
    return jnp.clip(values, min=-bound, max=bound).astype(held_as)


def setup_inputs(seed: int = 0) -> dict:
    key_list = jax.random.split(jax.random.key(seed), 16)
    queries = noise(key_list[0], (TOKEN_TOTAL, QUERY_HEADS, HEAD_DIMENSION), 1.0, 6.0, ((0, 256),))
    key_tensor = noise(key_list[1], (TOKEN_TOTAL, KEY_VALUE_HEADS, HEAD_DIMENSION), 1.0, 6.0, ((0, 256),))
    value_tensor = noise(key_list[2], (TOKEN_TOTAL, KEY_VALUE_HEADS, HEAD_DIMENSION), 1.0, 6.0, ((0, 256),))
    out_grad = noise(key_list[3], (TOKEN_TOTAL, QUERY_HEADS, HEAD_DIMENSION), 20.0, 120.0, ((0, 256),))
    log_norm = jnp.clip(6.5 + 1.5 * jax.random.uniform(key_list[4], (TOKEN_TOTAL, QUERY_HEADS), jnp.float32) ** levels(key_list[4], (TOKEN_TOTAL, QUERY_HEADS), ((0, 256),), -0.2, 0.2), 6.5, 8.0)
    out_dot = noise(key_list[5], (TOKEN_TOTAL, QUERY_HEADS), 200.0, 1200.0, ((0, 256),), jnp.float32)
    span_order = jax.random.permutation(key_list[6], 2 * N_CTX).astype(jnp.int32)
    moe_input = noise(key_list[7], (TOKEN_TOTAL, D), 1.0, 6.0, ((0, 256),))
    moe_grad = noise(key_list[8], (TOKEN_TOTAL, D), 10.0, 60.0, ((0, 256),))
    expert_ids_keys = jax.random.split(jax.random.fold_in(key_list[9], 1), TOKEN_TOTAL // T_DEV)
    expert_ids_turns = jax.random.permutation(jax.random.fold_in(key_list[9], 3), TOKEN_TOTAL // T_DEV)
    expert_ids = jax.vmap(lambda own, number: shared_out(jax.random.fold_in(key_list[9], 2), own, number, T_DEV, EXPERTS, TOPK, SLOT, 2))(expert_ids_keys, expert_ids_turns).reshape((TOKEN_TOTAL, TOPK))
    keep_mask = touch_ends((jax.random.randint(key_list[10], (TOKEN_TOTAL, TOPK), 0, 8) < 7).astype(jnp.int32), jax.random.fold_in(key_list[10], 1), 0, 1)
    route_weight = jnp.clip(jnp.exp(math.log(0.5) - 2.8134107 * jax.random.uniform(key_list[11], (TOKEN_TOTAL, TOPK), jnp.float32) ** levels(key_list[11], (TOKEN_TOTAL, TOPK), ((0, 256),), -0.2, 0.2)), 0.03, 0.5)
    w_gate = noise(key_list[12], (N_EXP, D, FFE), D ** -0.5, 0.125, ((0, 16),))
    w_up = noise(key_list[13], (N_EXP, D, FFE), D ** -0.5, 0.125, ((0, 16),))
    w_down = noise(key_list[14], (N_EXP, FFE, D), FFE ** -0.5, 0.21875, ((0, 16),))
    return dict(queries=queries, key_tensor=key_tensor, value_tensor=value_tensor, out_grad=out_grad, log_norm=log_norm, out_dot=out_dot, span_order=span_order, moe_input=moe_input, moe_grad=moe_grad, expert_ids=expert_ids, keep_mask=keep_mask, route_weight=route_weight, w_gate=w_gate, w_up=w_up, w_down=w_down)


def span_positions(span_order):
    ctx_ids = jnp.arange(N_CTX, dtype=jnp.int32)[:, None, None]
    exp_ids = jnp.zeros((1, N_EXP, 1), dtype=jnp.int32)
    local_rows = jnp.arange(T_DEV, dtype=jnp.int32)[None, None, :]
    half_rows = T_DEV // 2
    slot_index = jnp.where(local_rows < half_rows, ctx_ids, 2 * N_CTX - 1 - ctx_ids)
    span_number = span_order[slot_index + exp_ids]
    return span_number * half_rows + local_rows % half_rows + exp_ids

def by_slice(array):
    rest = array.shape[1:]
    shaped = array.reshape((N_CTX, N_EXP, T_DEV) + rest)
    return jnp.swapaxes(shaped, 0, 1).reshape((N_EXP, N_CTX * T_DEV) + rest)

def from_slice(array):
    rest = array.shape[2:]
    shaped = array.reshape((N_EXP, N_CTX, T_DEV) + rest)
    return jnp.swapaxes(shaped, 0, 1).reshape((TOKEN_TOTAL,) + rest)

def kv_group(operands, positions):
    query_grp, key_one, value_one, grad_grp, norm_grp, dot_grp = operands
    score_scale = 1.0 / math.sqrt(HEAD_DIMENSION)
    query_f = query_grp.astype(jnp.float32)
    key_f = key_one.astype(jnp.float32)
    value_f = value_one.astype(jnp.float32)
    grad_f = grad_grp.astype(jnp.float32)
    scores = jnp.einsum('mgd,nd->mgn', query_f, key_f) * score_scale
    visible = positions[None, None, :] <= positions[:, None, None]
    probs = jnp.where(visible, jnp.exp(scores - norm_grp[:, :, None]), 0.0)
    dprobs = jnp.einsum('mgd,nd->mgn', grad_f, value_f)
    dscores = probs * (dprobs - dot_grp[:, :, None])
    probs_b = lax.optimization_barrier(probs.astype(jnp.bfloat16)).astype(jnp.float32)
    dscores_b = lax.optimization_barrier(dscores.astype(jnp.bfloat16)).astype(jnp.float32)
    grad_query = jnp.einsum('mgn,nd->mgd', dscores_b, key_f) * score_scale
    grad_key = jnp.einsum('mgn,mgd->nd', dscores_b, query_f) * score_scale
    grad_value = jnp.einsum('mgn,mgd->nd', probs_b, grad_f)
    return (grad_query.astype(jnp.bfloat16), grad_key.astype(jnp.bfloat16), grad_value.astype(jnp.bfloat16))

def slice_pass(operands):
    query_second, key_s, value_s, gradient_second, norm_second, product_second, positions = operands
    every_row = query_second.shape[0]
    group_width = QUERY_HEADS // KEY_VALUE_HEADS
    query_high = jnp.moveaxis(query_second.reshape(every_row, KEY_VALUE_HEADS, group_width, HEAD_DIMENSION), 1, 0)
    gradient_high = jnp.moveaxis(gradient_second.reshape(every_row, KEY_VALUE_HEADS, group_width, HEAD_DIMENSION), 1, 0)
    norm_high = jnp.moveaxis(norm_second.reshape(every_row, KEY_VALUE_HEADS, group_width), 1, 0)
    product_high = jnp.moveaxis(product_second.reshape(every_row, KEY_VALUE_HEADS, group_width), 1, 0)
    key_h = jnp.moveaxis(key_s, 1, 0)
    value_h = jnp.moveaxis(value_s, 1, 0)
    grad_query, grad_key, grad_value = lax.map(lambda group_ops: kv_group(group_ops, positions), (query_high, key_h, value_h, gradient_high, norm_high, product_high))
    grad_query = jnp.moveaxis(grad_query, 0, 1).reshape(every_row, QUERY_HEADS, HEAD_DIMENSION)
    return (grad_query, jnp.moveaxis(grad_key, 0, 1), jnp.moveaxis(grad_value, 0, 1))

def expert_rows(input_rows, grad_rows, gate_mat, up_mat, down_mat):
    gate_pre = jnp.dot(input_rows, gate_mat, preferred_element_type=jnp.float32)
    up_pre = jnp.dot(input_rows, up_mat, preferred_element_type=jnp.float32)
    hidden_grad = jnp.dot(grad_rows, down_mat.T, preferred_element_type=jnp.float32)
    sigmoid_gate = jax.nn.sigmoid(gate_pre)
    gate_grad = (hidden_grad * up_pre * sigmoid_gate * (1.0 + gate_pre * (1.0 - sigmoid_gate))).astype(jnp.bfloat16)
    up_grad = (hidden_grad * gate_pre * sigmoid_gate).astype(jnp.bfloat16)
    slot_grad = jnp.dot(gate_grad, gate_mat.T, preferred_element_type=jnp.float32)
    slot_grad = slot_grad + jnp.dot(up_grad, up_mat.T, preferred_element_type=jnp.float32)
    return slot_grad.astype(jnp.bfloat16)

def reference(queries, key_tensor, value_tensor, out_grad, log_norm, out_dot, span_order, moe_input, moe_grad, expert_ids, keep_mask, route_weight, w_gate, w_up, w_down):
    positions = jnp.swapaxes(span_positions(span_order), 0, 1).reshape(N_EXP, N_CTX * T_DEV)
    grad_query, grad_key, grad_value = lax.map(slice_pass, (by_slice(queries), by_slice(key_tensor), by_slice(value_tensor), by_slice(out_grad), by_slice(log_norm), by_slice(out_dot), positions))
    grad_queries = from_slice(grad_query)
    grad_keys = from_slice(grad_key)
    grad_values = from_slice(grad_value)
    live_all = (expert_ids < N_EXP) & (keep_mask == 1)
    capacity_rows = N_CTX * N_EXP * SLOT

    def add_expert(total, expert):
        live = live_all & (expert_ids == expert)
        chosen = jnp.any(live, axis=1)
        weight = lax.optimization_barrier(jnp.sum(jnp.where(live, route_weight, 0.0), axis=1))
        order = jnp.argsort(1 - chosen.astype(jnp.int32), stable=True)[:capacity_rows].astype(jnp.int32)
        slot_grad = expert_rows(moe_input[order], moe_grad[order], w_gate[expert], w_up[expert], w_down[expert])
        slot_f = lax.optimization_barrier(slot_grad).astype(jnp.float32)
        contrib = weight[order][:, None] * slot_f
        return (total.at[order].add(contrib), None)
    initial = jnp.zeros((TOKEN_TOTAL, D), jnp.float32)
    total, ignored = lax.scan(add_expert, initial, jnp.arange(N_EXP, dtype=jnp.int32))
    grad_moe_input = total.astype(jnp.bfloat16)
    return (grad_queries, grad_keys, grad_values, grad_moe_input)
```

```python
import functools
import math

import jax
import jax.numpy as jnp
from jax import lax
from jax.experimental import pallas as pl
from jax.experimental.pallas import tpu as pltpu
from jax.sharding import PartitionSpec as P

SLOT = 10
LANES = 128
CHUNK = 256
VMEM = pl.BlockSpec(memory_space=pltpu.VMEM)
SMEM = pl.BlockSpec(memory_space=pltpu.SMEM)
F32 = jnp.float32
BF16 = jnp.bfloat16


def dot(left, right):
    return jnp.dot(left, right, preferred_element_type=F32)


def dot_rows(left, right):
    return lax.dot_general(left, right, (((1,), (1,)), ((), ())), preferred_element_type=F32)


def dot_cols(left, right):
    return lax.dot_general(left, right, (((0,), (0,)), ((), ())), preferred_element_type=F32)


def attention_kernel(
    scale,
    kv_blocks,
    span_ref,
    chip_ref,
    q_own,
    q_got,
    d_own,
    d_got,
    stat_own,
    stat_got,
    *rest,
):
    kv_refs = rest[:kv_blocks]
    dq_own, dq_got, own_ref, part_ref = rest[kv_blocks : kv_blocks + 4]
    keys, values, keys_t, dk_acc, dv_acc, dq_acc = rest[kv_blocks + 4 :]
    chip = chip_ref[0]
    core = chip_ref[1]
    slots = span_ref.shape[0]
    half = keys.shape[0] // slots
    width = q_own.shape[1]
    repeat = width // half

    def span_of(chip_index, core_index, upper):
        place = chip_index * 2 + core_index
        return span_ref[slots - 1 - place if upper else place]

    for block in range(kv_blocks):
        for part in range(4):
            span = span_of(chip ^ block, part // 2, part % 2)
            at = pl.ds(pl.multiple_of(span * half, half), half)
            rows = kv_refs[block][part * half : (part + 1) * half, :]
            keys[at, :] = rows[:, :LANES]
            values[at, :] = rows[:, LANES:]
    chunks = keys.shape[0] // CHUNK
    for chunk in range(chunks):
        at = slice(chunk * CHUNK, (chunk + 1) * CHUNK)
        keys_t[chunk] = keys[at, :].T
    dk_acc[...] = jnp.zeros_like(dk_acc)
    dv_acc[...] = jnp.zeros_like(dv_acc)
    factor = scale / math.log(2.0)
    spans_in_chunk = CHUNK // half

    for index in range(4):
        upper = index % 2
        if index < 2:
            q_ref, d_ref, stat_ref, dq_ref, who = q_own, d_own, stat_own, dq_own, core
        else:
            q_ref, d_ref, stat_ref, dq_ref, who = q_got, d_got, stat_got, dq_got, 1 - core
        span = span_of(chip, who, upper)
        queries = q_ref[upper]
        grads = d_ref[upper]
        norm = stat_ref[0:1, upper * width : (upper + 1) * width] * (1.0 / math.log(2.0))
        inner = stat_ref[1:2, upper * width : (upper + 1) * width]
        dq_acc[...] = jnp.zeros_like(dq_acc)
        last = span // spans_in_chunk

        def one(chunk, masked):
            at = pl.ds(pl.multiple_of(chunk * CHUNK, CHUNK), CHUNK)
            key = keys[at, :]
            scores = dot_rows(key, queries)
            probs = jnp.exp2(scores * factor - norm)
            if masked:
                key_pos = chunk * CHUNK + lax.broadcasted_iota(jnp.int32, scores.shape, 0)
                query_pos = span * half + lax.broadcasted_iota(jnp.int32, scores.shape, 1) // repeat
                probs = jnp.where(key_pos <= query_pos, probs, 0.0)
            dprobs = dot_rows(values[at, :], grads)
            dscores = (probs * (dprobs - inner)).astype(BF16)
            dv_acc[at, :] += dot(probs.astype(BF16), grads)
            dk_acc[at, :] += dot(dscores, queries)
            dq_acc[...] += dot(keys_t[chunk], dscores)

        lax.fori_loop(0, last, lambda chunk, none: (one(chunk, False), none)[1], 0)
        one(last, True)
        dq_ref[upper] = (dq_acc[...].T * scale).astype(BF16)

    for block in range(kv_blocks):
        for part in range(4):
            span = span_of(chip ^ block, part // 2, part % 2)
            at = pl.ds(pl.multiple_of(span * half, half), half)
            rows = slice(part * half, (part + 1) * half)
            if block == 0:
                own_ref[rows, :LANES] = dk_acc[at, :] * scale
                own_ref[rows, LANES:] = dv_acc[at, :]
            else:
                part_ref[block - 1, rows, :LANES] = (dk_acc[at, :] * scale).astype(BF16)
                part_ref[block - 1, rows, LANES:] = dv_acc[at, :].astype(BF16)


def attention(span_order, place, q_own, q_got, d_own, d_got, stat_own, stat_got, kv_list, scale):
    blocks = len(kv_list)
    rows = kv_list[0].shape[0]
    total = blocks * rows
    spans, width, _ = q_own.shape
    return pl.pallas_call(
        functools.partial(attention_kernel, scale, blocks),
        out_shape=(
            jax.ShapeDtypeStruct(q_own.shape, BF16),
            jax.ShapeDtypeStruct(q_own.shape, BF16),
            jax.ShapeDtypeStruct((rows, 2 * LANES), F32),
            jax.ShapeDtypeStruct((blocks - 1, rows, 2 * LANES), BF16),
        ),
        in_specs=[SMEM, SMEM] + [VMEM] * (6 + blocks),
        out_specs=(VMEM,) * 4,
        scratch_shapes=[
            pltpu.VMEM((total, LANES), BF16),
            pltpu.VMEM((total, LANES), BF16),
            pltpu.VMEM((total // CHUNK, LANES, CHUNK), BF16),
            pltpu.VMEM((total, LANES), F32),
            pltpu.VMEM((total, LANES), F32),
            pltpu.VMEM((LANES, width), F32),
        ],
        compiler_params=pltpu.CompilerParams(vmem_limit_bytes=40 * 1024 * 1024),
        cost_estimate=pl.CostEstimate(
            flops=6 * spans * width * total * LANES * 2,
            bytes_accessed=6 * 1024 * 1024,
            transcendentals=spans * width * total,
        ),
        name="attention",
    )(span_order, place, q_own, q_got, d_own, d_got, stat_own, stat_got, *kv_list)


def slots_to_chunks(tiles, experts, blocks, chunk_ref, first):
    for expert in range(experts):
        for block in range(blocks):
            at = first + block * SLOT
            chunk_ref[expert, at : at + SLOT, :] = tiles[block, expert * SLOT : (expert + 1) * SLOT, :]


def dispatch_kernel(ids_ref, keep_ref, weight_ref, x_ref, g_ref, send_ref, combine_ref, tiles, chunks):
    rows, top = ids_ref.shape
    experts = send_ref.shape[0]
    blocks = x_ref.shape[1] // LANES
    slots = experts * SLOT
    column = lax.broadcasted_iota(jnp.int32, (rows, slots), 1)
    expert_of = column // SLOT
    slot_of = column - expert_of * SLOT
    ids = jnp.where(keep_ref[...] == 1, ids_ref[...], -1)
    weights = weight_ref[...]
    hit = jnp.zeros((rows, slots), F32)
    weight = jnp.zeros((rows, slots), F32)
    for k in range(top):
        match = ids[:, k : k + 1] == expert_of
        hit = jnp.where(match, 1.0, hit)
        weight = jnp.where(match, weights[:, k : k + 1], weight)
    earlier = (
        lax.broadcasted_iota(jnp.int32, (rows, rows), 1)
        < lax.broadcasted_iota(jnp.int32, (rows, rows), 0)
    ).astype(F32).astype(BF16)
    rank = dot(earlier, hit.astype(BF16))
    chosen = jnp.where(rank == slot_of.astype(F32), hit, 0.0)
    combine_ref[...] = chosen * weight
    pick = chosen.T.astype(BF16)
    for source, first in ((x_ref, 0), (g_ref, blocks * SLOT)):
        for pair in range(blocks // 2):
            both = dot(pick, source[:, pair * 2 * LANES : (pair + 1) * 2 * LANES])
            tiles[2 * pair] = both[:, :LANES]
            tiles[2 * pair + 1] = both[:, LANES:]
        slots_to_chunks(tiles, experts, blocks, chunks, first)
    send_ref[...] = chunks[...].astype(BF16)


def dispatch(ids, keep, weight, x, g, experts):
    rows = ids.shape[0]
    blocks = x.shape[1] // LANES
    slots = experts * SLOT
    return pl.pallas_call(
        dispatch_kernel,
        out_shape=(
            jax.ShapeDtypeStruct((experts, 2 * blocks * SLOT, LANES), BF16),
            jax.ShapeDtypeStruct((rows, slots), F32),
        ),
        in_specs=[VMEM] * 5,
        out_specs=(VMEM, VMEM),
        scratch_shapes=[
            pltpu.VMEM((blocks, slots, LANES), F32),
            pltpu.VMEM((experts, 2 * blocks * SLOT, LANES), F32),
        ],
        compiler_params=pltpu.CompilerParams(vmem_limit_bytes=32 * 1024 * 1024),
        name="dispatch",
    )(ids, keep, weight, x, g)


def mlp_kernel(in_ref, gate_ref, up_ref, down_ref, out_ref, chunks, tiles, x_rows, g_rows, total):
    sources = in_ref.shape[0]
    blocks = x_rows.shape[1] // LANES
    step = pl.program_id(0)

    @pl.when(step == 0)
    def _():
        chunks[...] = in_ref[...].astype(F32)
        for rows_ref, first in ((x_rows, 0), (g_rows, blocks * SLOT)):
            for block in range(blocks):
                for source in range(sources):
                    at = first + block * SLOT
                    tiles[block, source * SLOT : (source + 1) * SLOT, :] = chunks[source, at : at + SLOT, :]
                rows_ref[:, block * LANES : (block + 1) * LANES] = tiles[block].astype(BF16)
        total[...] = jnp.zeros_like(total)

    gate_w, up_w = gate_ref[0], up_ref[0]
    gate_pre = dot(x_rows[...], gate_w)
    up_pre = dot(x_rows[...], up_w)
    hidden = dot_rows(g_rows[...], down_ref[0])
    sig = jax.nn.sigmoid(gate_pre)
    gate_grad = (hidden * up_pre * sig * (1.0 + gate_pre * (1.0 - sig))).astype(BF16)
    up_grad = (hidden * gate_pre * sig).astype(BF16)
    total[...] += dot_rows(gate_grad, gate_w) + dot_rows(up_grad, up_w)

    @pl.when(step == pl.num_programs(0) - 1)
    def _():
        for block in range(blocks):
            tiles[block] = total[:, block * LANES : (block + 1) * LANES]
        slots_to_chunks(tiles, sources, blocks, chunks, 0)
        out_ref[...] = chunks[:, : blocks * SLOT, :].astype(BF16)


def mlp(received, w_gate, w_up, w_down):
    sources, chunk_rows, _ = received.shape
    _, width, hidden = w_gate.shape
    blocks = width // LANES
    tile = 256
    slots = sources * SLOT
    whole = lambda *shape: pl.BlockSpec(shape, lambda i: (0,) * len(shape))
    return pl.pallas_call(
        mlp_kernel,
        grid=(hidden // tile,),
        out_shape=jax.ShapeDtypeStruct((sources, blocks * SLOT, LANES), BF16),
        in_specs=[
            whole(sources, chunk_rows, LANES),
            pl.BlockSpec((1, width, tile), lambda i: (0, 0, i)),
            pl.BlockSpec((1, width, tile), lambda i: (0, 0, i)),
            pl.BlockSpec((1, tile, width), lambda i: (0, i, 0)),
        ],
        out_specs=whole(sources, blocks * SLOT, LANES),
        scratch_shapes=[
            pltpu.VMEM((sources, chunk_rows, LANES), F32),
            pltpu.VMEM((blocks, slots, LANES), F32),
            pltpu.VMEM((slots, width), BF16),
            pltpu.VMEM((slots, width), BF16),
            pltpu.VMEM((slots, width), F32),
        ],
        compiler_params=pltpu.CompilerParams(vmem_limit_bytes=40 * 1024 * 1024),
        cost_estimate=pl.CostEstimate(
            flops=10 * slots * width * hidden, bytes_accessed=11 * 1024 * 1024, transcendentals=slots * hidden
        ),
        name="experts",
    )(received, w_gate, w_up, w_down)


def combine_kernel(weight_ref, back_ref, out_ref, chunks, tiles):
    experts = back_ref.shape[0]
    blocks = out_ref.shape[1] // LANES
    chunks[...] = back_ref[...].astype(F32)
    weight = weight_ref[...]
    high = weight.astype(BF16)
    rest = weight - high.astype(F32)
    middle = rest.astype(BF16)
    low = (rest - middle.astype(F32)).astype(BF16)
    for block in range(blocks):
        for expert in range(experts):
            at = block * SLOT
            tiles[block, expert * SLOT : (expert + 1) * SLOT, :] = chunks[expert, at : at + SLOT, :]
    for pair in range(blocks // 2):
        rows = jnp.concatenate([tiles[2 * pair], tiles[2 * pair + 1]], axis=1).astype(BF16)
        out = dot(high, rows) + (dot(middle, rows) + dot(low, rows))
        out_ref[:, pair * 2 * LANES : (pair + 1) * 2 * LANES] = out.astype(BF16)


def combine(weight, back):
    experts, chunk_rows, _ = back.shape
    rows, slots = weight.shape
    blocks = chunk_rows // SLOT
    return pl.pallas_call(
        combine_kernel,
        out_shape=jax.ShapeDtypeStruct((rows, blocks * LANES), BF16),
        in_specs=[VMEM, VMEM],
        out_specs=VMEM,
        scratch_shapes=[
            pltpu.VMEM((experts, chunk_rows, LANES), F32),
            pltpu.VMEM((blocks, slots, LANES), F32),
        ],
        compiler_params=pltpu.CompilerParams(vmem_limit_bytes=32 * 1024 * 1024),
        name="combine",
    )(weight, back)


def on_device(
    queries,
    key_tensor,
    value_tensor,
    out_grad,
    log_norm,
    out_dot,
    span_order,
    moe_input,
    moe_grad,
    expert_ids,
    keep_mask,
    route_weight,
    w_gate,
    w_up,
    w_down,
):
    rows, heads, size = queries.shape
    group = heads // 2
    scale = 1.0 / math.sqrt(size)
    members = lax.axis_size("ctx")
    experts = lax.axis_size("exp")
    me = lax.axis_index("ctx")
    core = me % 2
    first = core == 0
    chips = members // 2
    swap = [(i, i ^ 1) for i in range(members)]

    send, weight = dispatch(expert_ids, keep_mask, route_weight, moe_input, moe_grad, experts)

    def halves(array):
        low, high = array[:, :group], array[:, group:]
        return jnp.where(first, low, high), jnp.where(first, high, low)

    q_own, q_away = halves(queries)
    d_own, d_away = halves(out_grad)
    stat_own, stat_away = halves(jnp.stack([log_norm, out_dot]).reshape(2 * rows, heads))
    kv = jnp.concatenate([key_tensor, value_tensor], axis=2)
    kv_own = jnp.where(first, kv[:, 0], kv[:, 1])
    kv_away = jnp.where(first, kv[:, 1], kv[:, 0])
    trade = lambda array: lax.ppermute(array, "ctx", swap)
    kv_got = trade(kv_away)
    q_got, d_got = trade(q_away), trade(d_away)
    stat_got = trade(stat_away.reshape(2, rows * group))
    kv_chip = jnp.concatenate([jnp.where(first, kv_own, kv_got), jnp.where(first, kv_got, kv_own)], axis=0)

    received = lax.all_to_all(send, "exp", split_axis=0, concat_axis=0, tiled=True)
    to_chip = lambda array, k: lax.ppermute(array, "ctx", [(i, i ^ (2 * k)) for i in range(members)])
    kv_list = [kv_chip] + [to_chip(kv_chip, k) for k in range(1, chips)]

    spans = lambda array: array.reshape(2, rows // 2 * group, size)
    place = jnp.stack([me // 2, core]).astype(jnp.int32)
    dq_own, dq_got, own_sum, parts = attention(
        span_order,
        place,
        spans(q_own),
        spans(q_got),
        spans(d_own),
        spans(d_got),
        stat_own.reshape(2, rows * group),
        stat_got,
        kv_list,
        scale,
    )
    slot_grad = mlp(received, w_gate, w_up, w_down)
    returned = lax.all_to_all(slot_grad, "exp", split_axis=0, concat_axis=0, tiled=True)

    total = own_sum
    for k in range(1, chips):
        total = total + to_chip(parts[k - 1], k).astype(F32)
    total = total.astype(BF16)
    low, high = total[:rows], total[rows:]
    kv_mine = jnp.where(first, low, high)
    kv_theirs = trade(jnp.where(first, high, low))
    dq_back = trade(dq_got)

    def joined(mine, theirs):
        return jnp.concatenate([jnp.where(first, mine, theirs), jnp.where(first, theirs, mine)], axis=1)

    grad_queries = joined(dq_own.reshape(rows, group, size), dq_back.reshape(rows, group, size))
    kv_grads = joined(kv_mine[:, None, :], kv_theirs[:, None, :])
    grad_moe = combine(weight, returned)
    return grad_queries, kv_grads[:, :, :size], kv_grads[:, :, size:], grad_moe


def solution(mesh):
    rows = P(("ctx", "exp"))
    in_specs = (rows,) * 6 + (P(),) + (rows,) * 5 + (P("exp"),) * 3
    return jax.shard_map(
        on_device, mesh=mesh, in_specs=in_specs, out_specs=(rows,) * 4, check_vma=False
    )
```

```python
import functools
import math

import jax
import jax.numpy as jnp
from jax import lax
from jax.experimental import pallas as pl
from jax.experimental.pallas import tpu as pltpu
from jax.sharding import PartitionSpec as P

SLOT = 10
LANES = 128
CHUNK = 256
VMEM = pl.BlockSpec(memory_space=pltpu.VMEM)
SMEM = pl.BlockSpec(memory_space=pltpu.SMEM)
ANY = pl.BlockSpec(memory_space=pl.ANY)
F32 = jnp.float32
BF16 = jnp.bfloat16


def dot(left, right):
    return jnp.dot(left, right, preferred_element_type=F32)


def dot_rows(left, right):
    return lax.dot_general(left, right, (((1,), (1,)), ((), ())), preferred_element_type=F32)


def dot_cols(left, right):
    return lax.dot_general(left, right, (((0,), (0,)), ((), ())), preferred_element_type=F32)


def attention_kernel(
    scale,
    kv_blocks,
    span_ref,
    chip_ref,
    q_own,
    q_got,
    d_own,
    d_got,
    stat_own,
    stat_got,
    *rest,
):
    kv_refs = rest[:kv_blocks]
    dq_own, dq_got, own_ref, part_ref = rest[kv_blocks : kv_blocks + 4]
    keys, values, keys_t, dk_acc, dv_acc, dq_acc = rest[kv_blocks + 4 :]
    chip = chip_ref[0]
    core = chip_ref[1]
    slots = span_ref.shape[0]
    half = keys.shape[0] // slots
    width = q_own.shape[1]
    repeat = width // half

    def span_of(chip_index, core_index, upper):
        place = chip_index * 2 + core_index
        return span_ref[slots - 1 - place if upper else place]

    for block in range(kv_blocks):
        for part in range(8):
            span = span_of(chip ^ (2 * block + part // 4), part // 2 % 2, part % 2)
            at = pl.ds(pl.multiple_of(span * half, half), half)
            rows = kv_refs[block][part * half : (part + 1) * half, :]
            keys[at, :] = rows[:, :LANES]
            values[at, :] = rows[:, LANES:]
    chunks = keys.shape[0] // CHUNK
    for chunk in range(chunks):
        at = slice(chunk * CHUNK, (chunk + 1) * CHUNK)
        keys_t[chunk] = keys[at, :].T
    dk_acc[...] = jnp.zeros_like(dk_acc)
    dv_acc[...] = jnp.zeros_like(dv_acc)
    factor = scale / math.log(2.0)
    spans_in_chunk = CHUNK // half

    for index in range(4):
        upper = index % 2
        if index < 2:
            q_ref, d_ref, stat_ref, dq_ref, who = q_own, d_own, stat_own, dq_own, core
        else:
            q_ref, d_ref, stat_ref, dq_ref, who = q_got, d_got, stat_got, dq_got, 1 - core
        span = span_of(chip, who, upper)
        queries = q_ref[upper]
        grads = d_ref[upper]
        norm = stat_ref[0:1, upper * width : (upper + 1) * width] * (1.0 / math.log(2.0))
        inner = stat_ref[1:2, upper * width : (upper + 1) * width]
        dq_acc[...] = jnp.zeros_like(dq_acc)
        last = span // spans_in_chunk

        def one(chunk, masked):
            at = pl.ds(pl.multiple_of(chunk * CHUNK, CHUNK), CHUNK)
            key = keys[at, :]
            scores = dot_rows(key, queries)
            probs = jnp.exp2(scores * factor - norm)
            if masked:
                key_pos = chunk * CHUNK + lax.broadcasted_iota(jnp.int32, scores.shape, 0)
                query_pos = span * half + lax.broadcasted_iota(jnp.int32, scores.shape, 1) // repeat
                probs = jnp.where(key_pos <= query_pos, probs, 0.0)
            dprobs = dot_rows(values[at, :], grads)
            dscores = (probs * (dprobs - inner)).astype(BF16)
            dv_acc[at, :] += dot(probs.astype(BF16), grads)
            dk_acc[at, :] += dot(dscores, queries)
            dq_acc[...] += dot(keys_t[chunk], dscores)

        lax.fori_loop(0, last, lambda chunk, none: (one(chunk, False), none)[1], 0)
        one(last, True)
        dq_ref[upper] = (dq_acc[...].T * scale).astype(BF16)

    for block in range(kv_blocks):
        for part in range(8):
            span = span_of(chip ^ (2 * block + part // 4), part // 2 % 2, part % 2)
            at = pl.ds(pl.multiple_of(span * half, half), half)
            rows = slice(part * half, (part + 1) * half)
            if block == 0:
                own_ref[rows, :LANES] = dk_acc[at, :] * scale
                own_ref[rows, LANES:] = dv_acc[at, :]
            else:
                part_ref[block - 1, rows, :LANES] = (dk_acc[at, :] * scale).astype(BF16)
                part_ref[block - 1, rows, LANES:] = dv_acc[at, :].astype(BF16)


def attention(span_order, place, q_own, q_got, d_own, d_got, stat_own, stat_got, kv_list, scale):
    blocks = len(kv_list)
    rows = kv_list[0].shape[0]
    total = blocks * rows
    spans, width, _ = q_own.shape
    return pl.pallas_call(
        functools.partial(attention_kernel, scale, blocks),
        out_shape=(
            jax.ShapeDtypeStruct(q_own.shape, BF16),
            jax.ShapeDtypeStruct(q_own.shape, BF16),
            jax.ShapeDtypeStruct((rows, 2 * LANES), F32),
            jax.ShapeDtypeStruct((blocks - 1, rows, 2 * LANES), BF16),
        ),
        in_specs=[SMEM, SMEM] + [VMEM] * (6 + blocks),
        out_specs=(VMEM,) * 4,
        scratch_shapes=[
            pltpu.VMEM((total, LANES), BF16),
            pltpu.VMEM((total, LANES), BF16),
            pltpu.VMEM((total // CHUNK, LANES, CHUNK), BF16),
            pltpu.VMEM((total, LANES), F32),
            pltpu.VMEM((total, LANES), F32),
            pltpu.VMEM((LANES, width), F32),
        ],
        compiler_params=pltpu.CompilerParams(vmem_limit_bytes=16 * 1024 * 1024),
        cost_estimate=pl.CostEstimate(
            flops=6 * spans * width * total * LANES * 2,
            bytes_accessed=6 * 1024 * 1024,
            transcendentals=spans * width * total,
        ),
        name="attention",
    )(span_order, place, q_own, q_got, d_own, d_got, stat_own, stat_got, *kv_list)


def slots_to_chunks(tiles, experts, blocks, chunk_ref, first):
    for expert in range(experts):
        for block in range(blocks):
            at = first + block * SLOT
            chunk_ref[expert, at : at + SLOT, :] = tiles[block, expert * SLOT : (expert + 1) * SLOT, :]


def dispatch_kernel(ids_ref, keep_ref, weight_ref, x_hbm, g_hbm, send_ref, combine_ref, x_ref, g_ref, tiles, chunks, sems):
    loads = [
        pltpu.make_async_copy(source, target, sems.at[i])
        for i, (source, target) in enumerate(((x_hbm, x_ref), (g_hbm, g_ref)))
    ]
    for load in loads:
        load.start()
    top, rows = ids_ref.shape
    experts = send_ref.shape[0]
    blocks = x_ref.shape[1] // LANES
    slots = experts * SLOT
    line = lax.broadcasted_iota(jnp.int32, (slots, rows), 0)
    expert_of = line // SLOT
    slot_of = line - expert_of * SLOT
    ids = jnp.where(keep_ref[...] == 1, ids_ref[...], -1)
    weights = weight_ref[...]
    hit = jnp.zeros((slots, rows), F32)
    weight = jnp.zeros((slots, rows), F32)
    for k in range(top):
        match = ids[k : k + 1, :] == expert_of
        hit = jnp.where(match, 1.0, hit)
        weight = jnp.where(match, weights[k : k + 1, :], weight)
    earlier = (
        lax.broadcasted_iota(jnp.int32, (rows, rows), 0)
        < lax.broadcasted_iota(jnp.int32, (rows, rows), 1)
    ).astype(F32).astype(BF16)
    rank = dot(hit.astype(BF16), earlier)
    chosen = jnp.where(rank == slot_of.astype(F32), hit, 0.0)
    combine_ref[...] = chosen * weight
    pick = chosen.astype(BF16)
    for load, source, first in ((loads[0], x_ref, 0), (loads[1], g_ref, blocks * SLOT)):
        load.wait()
        for pair in range(blocks // 2):
            both = dot(pick, source[:, pair * 2 * LANES : (pair + 1) * 2 * LANES])
            tiles[2 * pair] = both[:, :LANES]
            tiles[2 * pair + 1] = both[:, LANES:]
        slots_to_chunks(tiles, experts, blocks, chunks, first)
    send_ref[...] = chunks[...].astype(BF16)


def dispatch(ids, keep, weight, x, g, experts):
    rows = ids.shape[0]
    blocks = x.shape[1] // LANES
    slots = experts * SLOT
    return pl.pallas_call(
        dispatch_kernel,
        out_shape=(
            jax.ShapeDtypeStruct((experts, 2 * blocks * SLOT, LANES), BF16),
            jax.ShapeDtypeStruct((slots, rows), F32),
        ),
        in_specs=[VMEM] * 3 + [ANY] * 2,
        out_specs=(VMEM, VMEM),
        scratch_shapes=[
            pltpu.VMEM(x.shape, BF16),
            pltpu.VMEM(g.shape, BF16),
            pltpu.VMEM((blocks, slots, LANES), F32),
            pltpu.VMEM((experts, 2 * blocks * SLOT, LANES), F32),
            pltpu.SemaphoreType.DMA((2,)),
        ],
        compiler_params=pltpu.CompilerParams(vmem_limit_bytes=12 * 1024 * 1024),
        name="dispatch",
    )(ids.T, keep.T, weight.T, x, g)


def mlp_kernel(in_ref, *rest):
    weights_hbm = rest[:3]
    out_ref = rest[3]
    weights = rest[4:7]
    chunks, tiles, x_rows, g_rows, sems = rest[7:]
    sources = in_ref.shape[0]
    blocks = x_rows.shape[1] // LANES
    hidden = weights[0].shape[1]
    tile = 256
    loads = []
    for step in range(hidden // tile):
        part = slice(step * tile, (step + 1) * tile)
        for i in range(3):
            at = (slice(None), part) if i < 2 else (part, slice(None))
            load = pltpu.make_async_copy(weights_hbm[i].at[(0,) + at], weights[i].at[at], sems.at[3 * step + i])
            load.start()
            loads.append(load)
    chunks[...] = in_ref[...].astype(F32)
    for rows_ref, first in ((x_rows, 0), (g_rows, blocks * SLOT)):
        for block in range(blocks):
            for source in range(sources):
                at = first + block * SLOT
                tiles[block, source * SLOT : (source + 1) * SLOT, :] = chunks[source, at : at + SLOT, :]
            rows_ref[:, block * LANES : (block + 1) * LANES] = tiles[block].astype(BF16)
    total = None
    for step in range(hidden // tile):
        for i in range(3):
            loads[3 * step + i].wait()
        part = slice(step * tile, (step + 1) * tile)
        gate_w, up_w = weights[0][:, part], weights[1][:, part]
        gate_pre = dot(x_rows[...], gate_w)
        up_pre = dot(x_rows[...], up_w)
        hidden_grad = dot_rows(g_rows[...], weights[2][part, :])
        sig = jax.nn.sigmoid(gate_pre)
        gate_grad = (hidden_grad * up_pre * sig * (1.0 + gate_pre * (1.0 - sig))).astype(BF16)
        up_grad = (hidden_grad * gate_pre * sig).astype(BF16)
        term = dot_rows(gate_grad, gate_w) + dot_rows(up_grad, up_w)
        for block in range(blocks):
            piece = term[:, block * LANES : (block + 1) * LANES]
            tiles[block] = piece if step == 0 else tiles[block] + piece
    slots_to_chunks(tiles, sources, blocks, chunks, 0)
    out_ref[...] = chunks[:, : blocks * SLOT, :].astype(BF16)


def mlp(received, w_gate, w_up, w_down):
    sources, chunk_rows, _ = received.shape
    _, width, hidden = w_gate.shape
    blocks = width // LANES
    slots = sources * SLOT
    return pl.pallas_call(
        mlp_kernel,
        out_shape=jax.ShapeDtypeStruct((sources, blocks * SLOT, LANES), BF16),
        in_specs=[VMEM] + [ANY] * 3,
        out_specs=VMEM,
        scratch_shapes=[
            pltpu.VMEM((width, hidden), BF16),
            pltpu.VMEM((width, hidden), BF16),
            pltpu.VMEM((hidden, width), BF16),
            pltpu.VMEM((sources, chunk_rows, LANES), F32),
            pltpu.VMEM((blocks, slots, LANES), F32),
            pltpu.VMEM((slots, width), BF16),
            pltpu.VMEM((slots, width), BF16),
            pltpu.SemaphoreType.DMA((9,)),
        ],
        compiler_params=pltpu.CompilerParams(vmem_limit_bytes=28 * 1024 * 1024),
        cost_estimate=pl.CostEstimate(
            flops=10 * slots * width * hidden, bytes_accessed=11 * 1024 * 1024, transcendentals=slots * hidden
        ),
        name="experts",
    )(received, w_gate, w_up, w_down)


def combine_kernel(weight_ref, back_ref, out_ref, chunks, tiles):
    experts = back_ref.shape[0]
    blocks = out_ref.shape[1] // LANES
    chunks[...] = back_ref[...].astype(F32)
    weight = weight_ref[...].T
    high = weight.astype(BF16)
    rest = weight - high.astype(F32)
    middle = rest.astype(BF16)
    low = (rest - middle.astype(F32)).astype(BF16)
    for block in range(blocks):
        for expert in range(experts):
            at = block * SLOT
            tiles[block, expert * SLOT : (expert + 1) * SLOT, :] = chunks[expert, at : at + SLOT, :]
    for pair in range(blocks // 2):
        rows = jnp.concatenate([tiles[2 * pair], tiles[2 * pair + 1]], axis=1).astype(BF16)
        out = dot(high, rows) + (dot(middle, rows) + dot(low, rows))
        out_ref[:, pair * 2 * LANES : (pair + 1) * 2 * LANES] = out.astype(BF16)


def combine(weight, back):
    experts, chunk_rows, _ = back.shape
    slots, rows = weight.shape
    blocks = chunk_rows // SLOT
    return pl.pallas_call(
        combine_kernel,
        out_shape=jax.ShapeDtypeStruct((rows, blocks * LANES), BF16),
        in_specs=[VMEM, VMEM],
        out_specs=VMEM,
        scratch_shapes=[
            pltpu.VMEM((experts, chunk_rows, LANES), F32),
            pltpu.VMEM((blocks, slots, LANES), F32),
        ],
        compiler_params=pltpu.CompilerParams(vmem_limit_bytes=12 * 1024 * 1024),
        name="combine",
    )(weight, back)


def on_device(
    queries,
    key_tensor,
    value_tensor,
    out_grad,
    log_norm,
    out_dot,
    span_order,
    moe_input,
    moe_grad,
    expert_ids,
    keep_mask,
    route_weight,
    w_gate,
    w_up,
    w_down,
):
    rows, heads, size = queries.shape
    group = heads // 2
    scale = 1.0 / math.sqrt(size)
    members = lax.axis_size("ctx")
    experts = lax.axis_size("exp")
    me = lax.axis_index("ctx")
    core = me % 2
    first = core == 0
    chips = members // 2
    swap = [(i, i ^ 1) for i in range(members)]

    send, weight = dispatch(expert_ids, keep_mask, route_weight, moe_input, moe_grad, experts)

    def halves(array):
        low, high = array[:, :group], array[:, group:]
        return jnp.where(first, low, high), jnp.where(first, high, low)

    q_own, q_away = halves(queries)
    d_own, d_away = halves(out_grad)
    stat_own, stat_away = halves(jnp.stack([log_norm, out_dot]).reshape(2 * rows, heads))
    kv = jnp.concatenate([key_tensor, value_tensor], axis=2)
    kv_own = jnp.where(first, kv[:, 0], kv[:, 1])
    kv_away = jnp.where(first, kv[:, 1], kv[:, 0])
    trade = lambda array: lax.ppermute(array, "ctx", swap)
    kv_got = trade(kv_away)
    q_got, d_got = trade(q_away), trade(d_away)
    stat_got = trade(stat_away.reshape(2, rows * group))
    kv_chip = jnp.concatenate([jnp.where(first, kv_own, kv_got), jnp.where(first, kv_got, kv_own)], axis=0)

    neighbour = lambda array: lax.ppermute(array, "ctx", [(i, i ^ 2) for i in range(members)])
    along_y = lambda array, k: lax.ppermute(array, "ctx", [(i, i ^ (4 * k)) for i in range(members)])
    kv_pair = jnp.concatenate([kv_chip, neighbour(kv_chip)], axis=0)
    received = lax.all_to_all(send, "exp", split_axis=0, concat_axis=0, tiled=True)
    kv_list = [kv_pair] + [along_y(kv_pair, k) for k in range(1, chips // 2)]

    spans = lambda array: array.reshape(2, rows // 2 * group, size)
    place = jnp.stack([me // 2, core]).astype(jnp.int32)
    dq_own, dq_got, own_sum, parts = attention(
        span_order,
        place,
        spans(q_own),
        spans(q_got),
        spans(d_own),
        spans(d_got),
        stat_own.reshape(2, rows * group),
        stat_got,
        kv_list,
        scale,
    )
    received, parts = lax.optimization_barrier((received, parts))
    slot_grad = mlp(received, w_gate, w_up, w_down)
    returned = lax.all_to_all(slot_grad, "exp", split_axis=0, concat_axis=0, tiled=True)

    total = own_sum
    for k in range(1, chips // 2):
        total = total + along_y(parts[k - 1], k).astype(F32)
    total = total[: 2 * rows] + neighbour(total[2 * rows :].astype(BF16)).astype(F32)
    total = total.astype(BF16)
    low, high = total[:rows], total[rows:]
    kv_mine = jnp.where(first, low, high)
    kv_theirs = trade(jnp.where(first, high, low))
    dq_back = trade(dq_got)

    def joined(mine, theirs):
        return jnp.concatenate([jnp.where(first, mine, theirs), jnp.where(first, theirs, mine)], axis=1)

    grad_queries = joined(dq_own.reshape(rows, group, size), dq_back.reshape(rows, group, size))
    kv_grads = joined(kv_mine[:, None, :], kv_theirs[:, None, :])
    grad_moe = combine(weight, returned)
    return grad_queries, kv_grads[:, :, :size], kv_grads[:, :, size:], grad_moe


def solution(mesh):
    rows = P(("ctx", "exp"))
    in_specs = (rows,) * 6 + (P(),) + (rows,) * 5 + (P("exp"),) * 3
    return jax.shard_map(
        on_device, mesh=mesh, in_specs=in_specs, out_specs=(rows,) * 4, check_vma=False
    )
```

```python
import functools
import math

import jax
import jax.numpy as jnp
from jax import lax
from jax.experimental import pallas as pl
from jax.experimental.pallas import tpu as pltpu
from jax.sharding import PartitionSpec as P

SLOT = 10
LANES = 128
CHUNK = 256
MIB = 1024 * 1024
VMEM = pl.BlockSpec(memory_space=pltpu.VMEM)
SMEM = pl.BlockSpec(memory_space=pltpu.SMEM)
ANY = pl.BlockSpec(memory_space=pl.ANY)
F32 = jnp.float32
BF16 = jnp.bfloat16


def dot(left, right):
    return jnp.dot(left, right, preferred_element_type=F32)


def dot_rows(left, right):
    return lax.dot_general(left, right, (((1,), (1,)), ((), ())), preferred_element_type=F32)


def dot_cols(left, right):
    return lax.dot_general(left, right, (((0,), (0,)), ((), ())), preferred_element_type=F32)


def split3(array):
    high = array.astype(BF16)
    rest = array - high.astype(F32)
    middle = rest.astype(BF16)
    return high, middle, (rest - middle.astype(F32)).astype(BF16)


def attention_kernel(
    scale,
    kv_blocks,
    span_ref,
    q_own,
    q_got,
    d_own,
    d_got,
    stat_own,
    stat_got,
    *rest,
):
    kv_refs = rest[:kv_blocks]
    dq_own, dq_got, own_ref = rest[kv_blocks : kv_blocks + 3]
    part_refs = rest[kv_blocks + 3 : 2 * kv_blocks + 2]
    keys, values, keys_t, dk_acc, dv_acc, dq_acc, stat_acc = rest[2 * kv_blocks + 2 :]
    me = lax.axis_index("ctx")
    chip = me // 2
    core = me % 2
    slots = span_ref.shape[0]
    half = keys.shape[0] // slots
    width = q_own.shape[1]
    repeat = width // half

    def span_of(chip_index, core_index, upper):
        place = chip_index * 2 + core_index
        return span_ref[slots - 1 - place if upper else place]

    stats = jnp.concatenate([stat_own[...], stat_got[...]], axis=0)
    rows = stats.shape[1]
    wide = rows * repeat
    spread = (
        lax.broadcasted_iota(jnp.int32, (rows, wide), 1) // repeat
        == lax.broadcasted_iota(jnp.int32, (rows, wide), 0)
    ).astype(F32).astype(BF16)
    high, middle, low = split3(stats)
    lanes = dot(high, spread) + (dot(middle, spread) + dot(low, spread))
    count = stats.shape[0] // repeat
    lanes = lanes.reshape(count, repeat, wide)
    head = lax.broadcasted_iota(jnp.int32, lanes.shape, 1)
    lane_head = lax.broadcasted_iota(jnp.int32, lanes.shape, 2) % repeat
    stat_acc[...] = jnp.sum(jnp.where(head == lane_head, lanes, 0.0), axis=1)

    for block in range(kv_blocks):
        for part in range(8):
            span = span_of(chip ^ (2 * block + part // 4), part // 2 % 2, part % 2)
            at = pl.ds(pl.multiple_of(span * half, half), half)
            rows = kv_refs[block][part * half : (part + 1) * half, :]
            keys[at, :] = rows[:, :LANES]
            values[at, :] = rows[:, LANES:]
    chunks = keys.shape[0] // CHUNK
    for chunk in range(chunks):
        at = slice(chunk * CHUNK, (chunk + 1) * CHUNK)
        keys_t[chunk] = keys[at, :].T
    dk_acc[...] = jnp.zeros_like(dk_acc)
    dv_acc[...] = jnp.zeros_like(dv_acc)
    factor = scale / math.log(2.0)
    spans_in_chunk = CHUNK // half

    for index in range(4):
        upper = index % 2
        if index < 2:
            q_ref, d_ref, dq_ref, who = q_own, d_own, dq_own, core
        else:
            q_ref, d_ref, dq_ref, who = q_got, d_got, dq_got, 1 - core
        line = 2 * (index // 2)
        span = span_of(chip, who, upper)
        queries = q_ref[upper]
        grads = d_ref[upper]
        norm = stat_acc[line : line + 1, upper * width : (upper + 1) * width] * (1.0 / math.log(2.0))
        inner = stat_acc[line + 1 : line + 2, upper * width : (upper + 1) * width]
        dq_acc[...] = jnp.zeros_like(dq_acc)
        last = span // spans_in_chunk

        def one(chunk, masked):
            at = pl.ds(pl.multiple_of(chunk * CHUNK, CHUNK), CHUNK)
            key = keys[at, :]
            scores = dot_rows(key, queries)
            probs = jnp.exp2(scores * factor - norm)
            if masked:
                key_pos = chunk * CHUNK + lax.broadcasted_iota(jnp.int32, scores.shape, 0)
                query_pos = span * half + lax.broadcasted_iota(jnp.int32, scores.shape, 1) // repeat
                probs = jnp.where(key_pos <= query_pos, probs, 0.0)
            dprobs = dot_rows(values[at, :], grads)
            dscores = (probs * (dprobs - inner)).astype(BF16)
            dv_acc[at, :] += dot(probs.astype(BF16), grads)
            dk_acc[at, :] += dot(dscores, queries)
            dq_acc[...] += dot(keys_t[chunk], dscores)

        lax.fori_loop(0, last, lambda chunk, none: (one(chunk, False), none)[1], 0)
        one(last, True)
        dq_ref[upper] = (dq_acc[...].T * scale).astype(BF16)

    for block in range(kv_blocks):
        for part in range(8):
            span = span_of(chip ^ (2 * block + part // 4), part // 2 % 2, part % 2)
            at = pl.ds(pl.multiple_of(span * half, half), half)
            rows = slice(part * half, (part + 1) * half)
            if block == 0:
                own_ref[rows, :LANES] = dk_acc[at, :] * scale
                own_ref[rows, LANES:] = dv_acc[at, :]
            else:
                part_refs[block - 1][rows, :LANES] = (dk_acc[at, :] * scale).astype(BF16)
                part_refs[block - 1][rows, LANES:] = dv_acc[at, :].astype(BF16)


def attention(span_order, q_own, q_got, d_own, d_got, stat_own, stat_got, kv_list, scale):
    blocks = len(kv_list)
    rows = kv_list[0].shape[0]
    total = blocks * rows
    spans, width, _ = q_own.shape
    part = jax.ShapeDtypeStruct((rows, 2 * LANES), BF16)
    return pl.pallas_call(
        functools.partial(attention_kernel, scale, blocks),
        out_shape=(
            jax.ShapeDtypeStruct(q_own.shape, BF16),
            jax.ShapeDtypeStruct(q_own.shape, BF16),
            jax.ShapeDtypeStruct((rows, 2 * LANES), F32),
        )
        + (part,) * (blocks - 1),
        in_specs=[SMEM] + [VMEM] * (6 + blocks),
        out_specs=(VMEM,) * (2 + blocks),
        scratch_shapes=[
            pltpu.VMEM((total, LANES), BF16),
            pltpu.VMEM((total, LANES), BF16),
            pltpu.VMEM((total // CHUNK, LANES, CHUNK), BF16),
            pltpu.VMEM((total, LANES), F32),
            pltpu.VMEM((total, LANES), F32),
            pltpu.VMEM((LANES, width), F32),
            pltpu.VMEM((4, spans * width), F32),
        ],
        compiler_params=pltpu.CompilerParams(vmem_limit_bytes=16 * MIB),
        cost_estimate=pl.CostEstimate(
            flops=6 * spans * width * total * LANES * 2,
            bytes_accessed=6 * 1024 * 1024,
            transcendentals=spans * width * total,
        ),
        name="attention",
    )(span_order, q_own, q_got, d_own, d_got, stat_own, stat_got, *kv_list)


def slots_to_chunks(tiles, experts, blocks, chunk_ref, first):
    for expert in range(experts):
        for block in range(blocks):
            at = first + block * SLOT
            chunk_ref[expert, at : at + SLOT, :] = tiles[block, expert * SLOT : (expert + 1) * SLOT, :]


def dispatch_kernel(ids_ref, keep_ref, weight_ref, x_hbm, g_hbm, send_ref, combine_ref, x_ref, g_ref, tiles, chunks, sems):
    loads = [
        pltpu.make_async_copy(source, target, sems.at[i])
        for i, (source, target) in enumerate(((x_hbm, x_ref), (g_hbm, g_ref)))
    ]
    for load in loads:
        load.start()
    top, rows = ids_ref.shape
    experts = send_ref.shape[0]
    blocks = x_ref.shape[1] // LANES
    slots = experts * SLOT
    line = lax.broadcasted_iota(jnp.int32, (slots, rows), 0)
    expert_of = line // SLOT
    slot_of = line - expert_of * SLOT
    ids = jnp.where(keep_ref[...] == 1, ids_ref[...], -1)
    weights = weight_ref[...]
    hit = jnp.zeros((slots, rows), F32)
    weight = jnp.zeros((slots, rows), F32)
    for k in range(top):
        match = ids[k : k + 1, :] == expert_of
        hit = jnp.where(match, 1.0, hit)
        weight = jnp.where(match, weights[k : k + 1, :], weight)
    earlier = (
        lax.broadcasted_iota(jnp.int32, (rows, rows), 0)
        < lax.broadcasted_iota(jnp.int32, (rows, rows), 1)
    ).astype(F32).astype(BF16)
    rank = dot(hit.astype(BF16), earlier)
    chosen = jnp.where(rank == slot_of.astype(F32), hit, 0.0)
    combine_ref[...] = chosen * weight
    pick = chosen.astype(BF16)
    for load, source, first in ((loads[0], x_ref, 0), (loads[1], g_ref, blocks * SLOT)):
        load.wait()
        for pair in range(blocks // 2):
            both = dot(pick, source[:, pair * 2 * LANES : (pair + 1) * 2 * LANES])
            tiles[2 * pair] = both[:, :LANES]
            tiles[2 * pair + 1] = both[:, LANES:]
        slots_to_chunks(tiles, experts, blocks, chunks, first)
    send_ref[...] = chunks[...].astype(BF16)


def dispatch(ids, keep, weight, x, g, experts):
    rows = ids.shape[0]
    blocks = x.shape[1] // LANES
    slots = experts * SLOT
    return pl.pallas_call(
        dispatch_kernel,
        out_shape=(
            jax.ShapeDtypeStruct((experts, 2 * blocks * SLOT, LANES), BF16),
            jax.ShapeDtypeStruct((slots, rows), F32),
        ),
        in_specs=[VMEM] * 3 + [ANY] * 2,
        out_specs=(VMEM, VMEM),
        scratch_shapes=[
            pltpu.VMEM(x.shape, BF16),
            pltpu.VMEM(g.shape, BF16),
            pltpu.VMEM((blocks, slots, LANES), F32),
            pltpu.VMEM((experts, 2 * blocks * SLOT, LANES), F32),
            pltpu.SemaphoreType.DMA((2,)),
        ],
        compiler_params=pltpu.CompilerParams(vmem_limit_bytes=60 * MIB),
        name="dispatch",
    )(ids.T, keep.T, weight.T, x, g)


def mlp_kernel(in_ref, *rest):
    weights_hbm = rest[:3]
    out_ref = rest[3]
    weights = rest[4:7]
    chunks, tiles, x_rows, g_rows, sems = rest[7:]
    sources = in_ref.shape[0]
    blocks = x_rows.shape[1] // LANES
    hidden = weights[0].shape[1]
    tile = 256
    loads = []
    for step in range(hidden // tile):
        part = slice(step * tile, (step + 1) * tile)
        for i in range(3):
            at = (slice(None), part) if i < 2 else (part, slice(None))
            load = pltpu.make_async_copy(weights_hbm[i].at[(0,) + at], weights[i].at[at], sems.at[3 * step + i])
            load.start()
            loads.append(load)
    chunks[...] = in_ref[...].astype(F32)
    for rows_ref, first in ((x_rows, 0), (g_rows, blocks * SLOT)):
        for block in range(blocks):
            for source in range(sources):
                at = first + block * SLOT
                tiles[block, source * SLOT : (source + 1) * SLOT, :] = chunks[source, at : at + SLOT, :]
            rows_ref[:, block * LANES : (block + 1) * LANES] = tiles[block].astype(BF16)
    total = None
    for step in range(hidden // tile):
        for i in range(3):
            loads[3 * step + i].wait()
        part = slice(step * tile, (step + 1) * tile)
        gate_w, up_w = weights[0][:, part], weights[1][:, part]
        gate_pre = dot(x_rows[...], gate_w)
        up_pre = dot(x_rows[...], up_w)
        hidden_grad = dot_rows(g_rows[...], weights[2][part, :])
        sig = jax.nn.sigmoid(gate_pre)
        gate_grad = (hidden_grad * up_pre * sig * (1.0 + gate_pre * (1.0 - sig))).astype(BF16)
        up_grad = (hidden_grad * gate_pre * sig).astype(BF16)
        term = dot_rows(gate_grad, gate_w) + dot_rows(up_grad, up_w)
        for block in range(blocks):
            piece = term[:, block * LANES : (block + 1) * LANES]
            tiles[block] = piece if step == 0 else tiles[block] + piece
    slots_to_chunks(tiles, sources, blocks, chunks, 0)
    out_ref[...] = chunks[:, : blocks * SLOT, :].astype(BF16)


def mlp(received, w_gate, w_up, w_down):
    sources, chunk_rows, _ = received.shape
    _, width, hidden = w_gate.shape
    blocks = width // LANES
    slots = sources * SLOT
    return pl.pallas_call(
        mlp_kernel,
        out_shape=jax.ShapeDtypeStruct((sources, blocks * SLOT, LANES), BF16),
        in_specs=[VMEM] + [ANY] * 3,
        out_specs=VMEM,
        scratch_shapes=[
            pltpu.VMEM((width, hidden), BF16),
            pltpu.VMEM((width, hidden), BF16),
            pltpu.VMEM((hidden, width), BF16),
            pltpu.VMEM((sources, chunk_rows, LANES), F32),
            pltpu.VMEM((blocks, slots, LANES), F32),
            pltpu.VMEM((slots, width), BF16),
            pltpu.VMEM((slots, width), BF16),
            pltpu.SemaphoreType.DMA((9,)),
        ],
        compiler_params=pltpu.CompilerParams(vmem_limit_bytes=58 * MIB),
        cost_estimate=pl.CostEstimate(
            flops=10 * slots * width * hidden, bytes_accessed=11 * 1024 * 1024, transcendentals=slots * hidden
        ),
        name="experts",
    )(received, w_gate, w_up, w_down)


def combine_kernel(weight_ref, back_ref, out_ref, chunks, tiles):
    experts = back_ref.shape[0]
    blocks = out_ref.shape[1] // LANES
    chunks[...] = back_ref[...].astype(F32)
    weight = weight_ref[...].T
    high = weight.astype(BF16)
    rest = weight - high.astype(F32)
    middle = rest.astype(BF16)
    low = (rest - middle.astype(F32)).astype(BF16)
    for block in range(blocks):
        for expert in range(experts):
            at = block * SLOT
            tiles[block, expert * SLOT : (expert + 1) * SLOT, :] = chunks[expert, at : at + SLOT, :]
    for pair in range(blocks // 2):
        rows = jnp.concatenate([tiles[2 * pair], tiles[2 * pair + 1]], axis=1).astype(BF16)
        out = dot(high, rows) + (dot(middle, rows) + dot(low, rows))
        out_ref[:, pair * 2 * LANES : (pair + 1) * 2 * LANES] = out.astype(BF16)


def combine(weight, back):
    experts, chunk_rows, _ = back.shape
    slots, rows = weight.shape
    blocks = chunk_rows // SLOT
    return pl.pallas_call(
        combine_kernel,
        out_shape=jax.ShapeDtypeStruct((rows, blocks * LANES), BF16),
        in_specs=[VMEM, VMEM],
        out_specs=VMEM,
        scratch_shapes=[
            pltpu.VMEM((experts, chunk_rows, LANES), F32),
            pltpu.VMEM((blocks, slots, LANES), F32),
        ],
        compiler_params=pltpu.CompilerParams(vmem_limit_bytes=12 * MIB),
        name="combine",
    )(weight, back)


def on_device(
    queries,
    key_tensor,
    value_tensor,
    out_grad,
    log_norm,
    out_dot,
    span_order,
    moe_input,
    moe_grad,
    expert_ids,
    keep_mask,
    route_weight,
    w_gate,
    w_up,
    w_down,
):
    rows, heads, size = queries.shape
    group = heads // 2
    scale = 1.0 / math.sqrt(size)
    members = lax.axis_size("ctx")
    experts = lax.axis_size("exp")
    first = lax.axis_index("ctx") & 1 == 0
    chips = members // 2
    trade = lambda array, k: lax.ppermute(array, "ctx", [(i, i ^ k) for i in range(members)])

    kv = jnp.concatenate([key_tensor, value_tensor], axis=2)
    kv_own = jnp.where(first, kv[:, 0], kv[:, 1])
    kv_away = jnp.where(first, kv[:, 1], kv[:, 0])
    kv_own, kv_away, expert_ids = lax.optimization_barrier((kv_own, kv_away, expert_ids))
    kv_got = trade(kv_away, 1)
    kv_near, kv_cross = trade(kv_own, 2), trade(kv_away, 3)
    send, weight = dispatch(expert_ids, keep_mask, route_weight, moe_input, moe_grad, experts)
    ordered = lambda mine, other: [jnp.where(first, mine, other), jnp.where(first, other, mine)]
    kv_pair = jnp.concatenate(ordered(kv_own, kv_got) + ordered(kv_near, kv_cross), axis=0)
    send, kv_pair = lax.optimization_barrier((send, kv_pair))
    received = lax.all_to_all(send, "exp", split_axis=0, concat_axis=0, tiled=True)
    kv_list = [kv_pair] + [trade(kv_pair, 4 * k) for k in range(1, chips // 2)]

    def halves(array, axis):
        low, high = jnp.split(array, 2, axis=axis)
        return jnp.where(first, low, high), jnp.where(first, high, low)

    q_own, q_away = halves(queries, 1)
    d_own, d_away = halves(out_grad, 1)
    stat_own, stat_away = halves(jnp.stack([log_norm.T, out_dot.T]), 1)
    q_got, d_got = trade(q_away, 1), trade(d_away, 1)
    stat_got = trade(stat_away, 1)

    spans = lambda array: array.reshape(2, rows // 2 * group, size)
    dq_own, dq_got, own_sum, *parts = attention(
        span_order,
        spans(q_own),
        spans(q_got),
        spans(d_own),
        spans(d_got),
        stat_own.reshape(2 * group, rows),
        stat_got.reshape(2 * group, rows),
        kv_list,
        scale,
    )
    received, *parts = lax.optimization_barrier((received, *parts))
    slot_grad = mlp(received, w_gate, w_up, w_down)
    returned = lax.all_to_all(slot_grad, "exp", split_axis=0, concat_axis=0, tiled=True)

    total = own_sum
    for k in range(1, chips // 2):
        total = total + trade(parts[k - 1], 4 * k).astype(F32)
    total = total[: 2 * rows] + trade(total[2 * rows :].astype(BF16), 2).astype(F32)
    total = total.astype(BF16)
    low, high = total[:rows], total[rows:]
    kv_mine = jnp.where(first, low, high)
    kv_theirs = trade(jnp.where(first, high, low), 1)
    dq_back = trade(dq_got, 1)

    def joined(mine, theirs):
        return jnp.concatenate([jnp.where(first, mine, theirs), jnp.where(first, theirs, mine)], axis=1)

    grad_queries = joined(dq_own.reshape(rows, group, size), dq_back.reshape(rows, group, size))
    kv_grads = joined(kv_mine[:, None, :], kv_theirs[:, None, :])
    grad_moe = combine(weight, returned)
    return grad_queries, kv_grads[:, :, :size], kv_grads[:, :, size:], grad_moe


def solution(mesh):
    rows = P(("ctx", "exp"))
    in_specs = (rows,) * 6 + (P(),) + (rows,) * 5 + (P("exp"),) * 3
    return jax.shard_map(
        on_device, mesh=mesh, in_specs=in_specs, out_specs=(rows,) * 4, check_vma=False
    )
```

```python
import functools
import math

import jax
import jax.numpy as jnp
from jax import lax
from jax.experimental import pallas as pl
from jax.experimental.pallas import tpu as pltpu
from jax.sharding import PartitionSpec as P

SLOT = 10
LANES = 128
CHUNK = 256
LONG = 1024
MIB = 1024 * 1024
VMEM = pl.BlockSpec(memory_space=pltpu.VMEM)
SMEM = pl.BlockSpec(memory_space=pltpu.SMEM)
ANY = pl.BlockSpec(memory_space=pl.ANY)
F32 = jnp.float32
BF16 = jnp.bfloat16


def dot(left, right):
    return jnp.dot(left, right, preferred_element_type=F32)


def dot_rows(left, right):
    return lax.dot_general(left, right, (((1,), (1,)), ((), ())), preferred_element_type=F32)


def dot_cols(left, right):
    return lax.dot_general(left, right, (((0,), (0,)), ((), ())), preferred_element_type=F32)


def split3(array):
    high = array.astype(BF16)
    rest = array - high.astype(F32)
    middle = rest.astype(BF16)
    return high, middle, (rest - middle.astype(F32)).astype(BF16)


def attention_kernel(
    scale,
    kv_blocks,
    span_ref,
    q_own,
    q_got,
    d_own,
    d_got,
    stat_own,
    stat_got,
    *rest,
):
    kv_refs = rest[:kv_blocks]
    dq_own, dq_got, own_ref = rest[kv_blocks : kv_blocks + 3]
    part_refs = rest[kv_blocks + 3 : 2 * kv_blocks + 2]
    keys, values, keys_t, dk_acc, dv_acc, dq_acc, stat_acc = rest[2 * kv_blocks + 2 :]
    me = lax.axis_index("ctx")
    chip = me // 2
    core = me % 2
    slots = span_ref.shape[0]
    half = keys.shape[0] // slots
    width = q_own.shape[1]
    repeat = width // half

    def span_of(chip_index, core_index, upper):
        place = chip_index * 2 + core_index
        return span_ref[slots - 1 - place if upper else place]

    stats = jnp.concatenate([stat_own[...], stat_got[...]], axis=0)
    rows = stats.shape[1]
    wide = rows * repeat
    spread = (
        lax.broadcasted_iota(jnp.int32, (rows, wide), 1) // repeat
        == lax.broadcasted_iota(jnp.int32, (rows, wide), 0)
    ).astype(F32).astype(BF16)
    high, middle, low = split3(stats)
    lanes = dot(high, spread) + (dot(middle, spread) + dot(low, spread))
    count = stats.shape[0] // repeat
    lanes = lanes.reshape(count, repeat, wide)
    head = lax.broadcasted_iota(jnp.int32, lanes.shape, 1)
    lane_head = lax.broadcasted_iota(jnp.int32, lanes.shape, 2) % repeat
    stat_acc[...] = jnp.sum(jnp.where(head == lane_head, lanes, 0.0), axis=1)

    for block in range(kv_blocks):
        for part in range(8):
            span = span_of(chip ^ (2 * block + part // 4), part // 2 % 2, part % 2)
            at = pl.ds(pl.multiple_of(span * half, half), half)
            rows = kv_refs[block][part * half : (part + 1) * half, :]
            keys[at, :] = rows[:, :LANES]
            values[at, :] = rows[:, LANES:]
    chunks = keys.shape[0] // CHUNK
    for chunk in range(chunks):
        at = slice(chunk * CHUNK, (chunk + 1) * CHUNK)
        keys_t[:, at] = keys[at, :].T
    dk_acc[...] = jnp.zeros_like(dk_acc)
    dv_acc[...] = jnp.zeros_like(dv_acc)
    factor = scale / math.log(2.0)

    for index in range(4):
        upper = index % 2
        if index < 2:
            q_ref, d_ref, dq_ref, who = q_own, d_own, dq_own, core
        else:
            q_ref, d_ref, dq_ref, who = q_got, d_got, dq_got, 1 - core
        line = 2 * (index // 2)
        span = span_of(chip, who, upper)
        queries = q_ref[upper]
        grads = d_ref[upper]
        norm = stat_acc[line : line + 1, upper * width : (upper + 1) * width] * (1.0 / math.log(2.0))
        inner = stat_acc[line + 1 : line + 2, upper * width : (upper + 1) * width]
        dq_acc[...] = jnp.zeros_like(dq_acc)

        def one(start, count, masked):
            at = pl.ds(pl.multiple_of(start, CHUNK), count)
            scores = dot_rows(keys[at, :], queries)
            probs = jnp.exp2(scores * factor - norm)
            if masked:
                key_pos = start + lax.broadcasted_iota(jnp.int32, scores.shape, 0)
                query_pos = span * half + lax.broadcasted_iota(jnp.int32, scores.shape, 1) // repeat
                probs = jnp.where(key_pos <= query_pos, probs, 0.0)
            dprobs = dot_rows(values[at, :], grads)
            dscores = (probs * (dprobs - inner)).astype(BF16)
            dv_acc[at, :] += dot(probs.astype(BF16), grads)
            dk_acc[at, :] += dot(dscores, queries)
            dq_acc[...] += dot(keys_t[:, at], dscores)

        ahead = span * half
        lax.fori_loop(0, ahead // LONG, lambda i, none: (one(i * LONG, LONG, False), none)[1], 0)
        rest_start = ahead // LONG * LONG

        @pl.when(ahead - rest_start >= LONG // 2)
        def _():
            one(rest_start, LONG // 2, False)

        tail = ahead // (LONG // 2) * (LONG // 2)

        @pl.when(ahead - tail >= CHUNK)
        def _():
            one(tail, LONG // 2, True)

        @pl.when(ahead - tail < CHUNK)
        def _():
            one(tail, CHUNK, True)

        dq_ref[upper] = (dq_acc[...].T * scale).astype(BF16)

    for block in range(kv_blocks):
        for part in range(8):
            span = span_of(chip ^ (2 * block + part // 4), part // 2 % 2, part % 2)
            at = pl.ds(pl.multiple_of(span * half, half), half)
            rows = slice(part * half, (part + 1) * half)
            if block == 0:
                own_ref[rows, :LANES] = dk_acc[at, :] * scale
                own_ref[rows, LANES:] = dv_acc[at, :]
            else:
                part_refs[block - 1][rows, :LANES] = (dk_acc[at, :] * scale).astype(BF16)
                part_refs[block - 1][rows, LANES:] = dv_acc[at, :].astype(BF16)


def attention(span_order, q_own, q_got, d_own, d_got, stat_own, stat_got, kv_list, scale):
    blocks = len(kv_list)
    rows = kv_list[0].shape[0]
    total = blocks * rows
    spans, width, _ = q_own.shape
    part = jax.ShapeDtypeStruct((rows, 2 * LANES), BF16)
    return pl.pallas_call(
        functools.partial(attention_kernel, scale, blocks),
        out_shape=(
            jax.ShapeDtypeStruct(q_own.shape, BF16),
            jax.ShapeDtypeStruct(q_own.shape, BF16),
            jax.ShapeDtypeStruct((rows, 2 * LANES), F32),
        )
        + (part,) * (blocks - 1),
        in_specs=[SMEM] + [VMEM] * (6 + blocks),
        out_specs=(VMEM,) * (2 + blocks),
        scratch_shapes=[
            pltpu.VMEM((total, LANES), BF16),
            pltpu.VMEM((total, LANES), BF16),
            pltpu.VMEM((LANES, total), BF16),
            pltpu.VMEM((total, LANES), F32),
            pltpu.VMEM((total, LANES), F32),
            pltpu.VMEM((LANES, width), F32),
            pltpu.VMEM((4, spans * width), F32),
        ],
        compiler_params=pltpu.CompilerParams(vmem_limit_bytes=16 * MIB),
        cost_estimate=pl.CostEstimate(
            flops=6 * spans * width * total * LANES * 2,
            bytes_accessed=6 * 1024 * 1024,
            transcendentals=spans * width * total,
        ),
        name="attention",
    )(span_order, q_own, q_got, d_own, d_got, stat_own, stat_got, *kv_list)


def slots_to_chunks(tiles, experts, blocks, chunk_ref, first):
    for expert in range(experts):
        for block in range(blocks):
            at = first + block * SLOT
            chunk_ref[expert, at : at + SLOT, :] = tiles[block, expert * SLOT : (expert + 1) * SLOT, :]


def dispatch_kernel(ids_ref, keep_ref, weight_ref, x_hbm, g_hbm, send_ref, combine_ref, x_ref, g_ref, tiles, chunks, sems):
    loads = [
        pltpu.make_async_copy(source, target, sems.at[i])
        for i, (source, target) in enumerate(((x_hbm, x_ref), (g_hbm, g_ref)))
    ]
    for load in loads:
        load.start()
    top, rows = ids_ref.shape
    experts = send_ref.shape[0]
    blocks = x_ref.shape[1] // LANES
    slots = experts * SLOT
    line = lax.broadcasted_iota(jnp.int32, (slots, rows), 0)
    expert_of = line // SLOT
    slot_of = line - expert_of * SLOT
    ids = jnp.where(keep_ref[...] == 1, ids_ref[...], -1)
    weights = weight_ref[...]
    hit = jnp.zeros((slots, rows), F32)
    weight = jnp.zeros((slots, rows), F32)
    for k in range(top):
        match = ids[k : k + 1, :] == expert_of
        hit = jnp.where(match, 1.0, hit)
        weight = jnp.where(match, weights[k : k + 1, :], weight)
    earlier = (
        lax.broadcasted_iota(jnp.int32, (rows, rows), 0)
        < lax.broadcasted_iota(jnp.int32, (rows, rows), 1)
    ).astype(F32).astype(BF16)
    rank = dot(hit.astype(BF16), earlier)
    chosen = jnp.where(rank == slot_of.astype(F32), hit, 0.0)
    combine_ref[...] = chosen * weight
    pick = chosen.astype(BF16)
    for load, source, first in ((loads[0], x_ref, 0), (loads[1], g_ref, blocks * SLOT)):
        load.wait()
        for pair in range(blocks // 2):
            both = dot(pick, source[:, pair * 2 * LANES : (pair + 1) * 2 * LANES])
            tiles[2 * pair] = both[:, :LANES]
            tiles[2 * pair + 1] = both[:, LANES:]
        slots_to_chunks(tiles, experts, blocks, chunks, first)
    send_ref[...] = chunks[...].astype(BF16)


def dispatch(ids, keep, weight, x, g, experts):
    rows = ids.shape[0]
    blocks = x.shape[1] // LANES
    slots = experts * SLOT
    return pl.pallas_call(
        dispatch_kernel,
        out_shape=(
            jax.ShapeDtypeStruct((experts, 2 * blocks * SLOT, LANES), BF16),
            jax.ShapeDtypeStruct((slots, rows), F32),
        ),
        in_specs=[VMEM] * 3 + [ANY] * 2,
        out_specs=(VMEM, VMEM),
        scratch_shapes=[
            pltpu.VMEM(x.shape, BF16),
            pltpu.VMEM(g.shape, BF16),
            pltpu.VMEM((blocks, slots, LANES), F32),
            pltpu.VMEM((experts, 2 * blocks * SLOT, LANES), F32),
            pltpu.SemaphoreType.DMA((2,)),
        ],
        compiler_params=pltpu.CompilerParams(vmem_limit_bytes=60 * MIB),
        name="dispatch",
    )(ids.T, keep.T, weight.T, x, g)


def mlp_kernel(in_ref, *rest):
    weights_hbm = rest[:3]
    out_ref = rest[3]
    weights = rest[4:7]
    chunks, tiles, x_rows, g_rows, sems = rest[7:]
    sources = in_ref.shape[0]
    blocks = x_rows.shape[1] // LANES
    hidden = weights[0].shape[1]
    tile = 256
    loads = []
    for step in range(hidden // tile):
        part = slice(step * tile, (step + 1) * tile)
        for i in range(3):
            at = (slice(None), part) if i < 2 else (part, slice(None))
            load = pltpu.make_async_copy(weights_hbm[i].at[(0,) + at], weights[i].at[at], sems.at[3 * step + i])
            load.start()
            loads.append(load)
    chunks[...] = in_ref[...].astype(F32)
    for rows_ref, first in ((x_rows, 0), (g_rows, blocks * SLOT)):
        for block in range(blocks):
            for source in range(sources):
                at = first + block * SLOT
                tiles[block, source * SLOT : (source + 1) * SLOT, :] = chunks[source, at : at + SLOT, :]
            rows_ref[:, block * LANES : (block + 1) * LANES] = tiles[block].astype(BF16)
    total = None
    for step in range(hidden // tile):
        for i in range(3):
            loads[3 * step + i].wait()
        part = slice(step * tile, (step + 1) * tile)
        gate_w, up_w = weights[0][:, part], weights[1][:, part]
        gate_pre = dot(x_rows[...], gate_w)
        up_pre = dot(x_rows[...], up_w)
        hidden_grad = dot_rows(g_rows[...], weights[2][part, :])
        sig = jax.nn.sigmoid(gate_pre)
        gate_grad = (hidden_grad * up_pre * sig * (1.0 + gate_pre * (1.0 - sig))).astype(BF16)
        up_grad = (hidden_grad * gate_pre * sig).astype(BF16)
        term = dot_rows(gate_grad, gate_w) + dot_rows(up_grad, up_w)
        for block in range(blocks):
            piece = term[:, block * LANES : (block + 1) * LANES]
            tiles[block] = piece if step == 0 else tiles[block] + piece
    slots_to_chunks(tiles, sources, blocks, chunks, 0)
    out_ref[...] = chunks[:, : blocks * SLOT, :].astype(BF16)


def mlp(received, w_gate, w_up, w_down):
    sources, chunk_rows, _ = received.shape
    _, width, hidden = w_gate.shape
    blocks = width // LANES
    slots = sources * SLOT
    return pl.pallas_call(
        mlp_kernel,
        out_shape=jax.ShapeDtypeStruct((sources, blocks * SLOT, LANES), BF16),
        in_specs=[VMEM] + [ANY] * 3,
        out_specs=VMEM,
        scratch_shapes=[
            pltpu.VMEM((width, hidden), BF16),
            pltpu.VMEM((width, hidden), BF16),
            pltpu.VMEM((hidden, width), BF16),
            pltpu.VMEM((sources, chunk_rows, LANES), F32),
            pltpu.VMEM((blocks, slots, LANES), F32),
            pltpu.VMEM((slots, width), BF16),
            pltpu.VMEM((slots, width), BF16),
            pltpu.SemaphoreType.DMA((9,)),
        ],
        compiler_params=pltpu.CompilerParams(vmem_limit_bytes=58 * MIB),
        cost_estimate=pl.CostEstimate(
            flops=10 * slots * width * hidden, bytes_accessed=11 * 1024 * 1024, transcendentals=slots * hidden
        ),
        name="experts",
    )(received, w_gate, w_up, w_down)


def combine_kernel(weight_ref, back_ref, out_ref, chunks, tiles):
    experts = back_ref.shape[0]
    blocks = out_ref.shape[1] // LANES
    chunks[...] = back_ref[...].astype(F32)
    weight = weight_ref[...].T
    high = weight.astype(BF16)
    rest = weight - high.astype(F32)
    middle = rest.astype(BF16)
    low = (rest - middle.astype(F32)).astype(BF16)
    for block in range(blocks):
        for expert in range(experts):
            at = block * SLOT
            tiles[block, expert * SLOT : (expert + 1) * SLOT, :] = chunks[expert, at : at + SLOT, :]
    for pair in range(blocks // 2):
        rows = jnp.concatenate([tiles[2 * pair], tiles[2 * pair + 1]], axis=1).astype(BF16)
        out = dot(high, rows) + (dot(middle, rows) + dot(low, rows))
        out_ref[:, pair * 2 * LANES : (pair + 1) * 2 * LANES] = out.astype(BF16)


def combine(weight, back):
    experts, chunk_rows, _ = back.shape
    slots, rows = weight.shape
    blocks = chunk_rows // SLOT
    return pl.pallas_call(
        combine_kernel,
        out_shape=jax.ShapeDtypeStruct((rows, blocks * LANES), BF16),
        in_specs=[VMEM, VMEM],
        out_specs=VMEM,
        scratch_shapes=[
            pltpu.VMEM((experts, chunk_rows, LANES), F32),
            pltpu.VMEM((blocks, slots, LANES), F32),
        ],
        compiler_params=pltpu.CompilerParams(vmem_limit_bytes=12 * MIB),
        name="combine",
    )(weight, back)


def on_device(
    queries,
    key_tensor,
    value_tensor,
    out_grad,
    log_norm,
    out_dot,
    span_order,
    moe_input,
    moe_grad,
    expert_ids,
    keep_mask,
    route_weight,
    w_gate,
    w_up,
    w_down,
):
    rows, heads, size = queries.shape
    group = heads // 2
    scale = 1.0 / math.sqrt(size)
    members = lax.axis_size("ctx")
    experts = lax.axis_size("exp")
    first = lax.axis_index("ctx") & 1 == 0
    chips = members // 2
    trade = lambda array, k: lax.ppermute(array, "ctx", [(i, i ^ k) for i in range(members)])

    kv = jnp.concatenate([key_tensor, value_tensor], axis=2)
    kv_own = jnp.where(first, kv[:, 0], kv[:, 1])
    kv_away = jnp.where(first, kv[:, 1], kv[:, 0])
    kv_own, kv_away, expert_ids = lax.optimization_barrier((kv_own, kv_away, expert_ids))
    kv_got = trade(kv_away, 1)
    kv_near, kv_cross = trade(kv_own, 2), trade(kv_away, 3)
    send, weight = dispatch(expert_ids, keep_mask, route_weight, moe_input, moe_grad, experts)
    ordered = lambda mine, other: [jnp.where(first, mine, other), jnp.where(first, other, mine)]
    kv_pair = jnp.concatenate(ordered(kv_own, kv_got) + ordered(kv_near, kv_cross), axis=0)
    send, kv_pair = lax.optimization_barrier((send, kv_pair))
    received = lax.all_to_all(send, "exp", split_axis=0, concat_axis=0, tiled=True)
    kv_list = [kv_pair] + [trade(kv_pair, 4 * k) for k in range(1, chips // 2)]

    def halves(array, axis):
        low, high = jnp.split(array, 2, axis=axis)
        return jnp.where(first, low, high), jnp.where(first, high, low)

    q_own, q_away = halves(queries, 1)
    d_own, d_away = halves(out_grad, 1)
    stat_own, stat_away = halves(jnp.stack([log_norm.T, out_dot.T]), 1)
    q_got, d_got = trade(q_away, 1), trade(d_away, 1)
    stat_got = trade(stat_away, 1)

    spans = lambda array: array.reshape(2, rows // 2 * group, size)
    dq_own, dq_got, own_sum, *parts = attention(
        span_order,
        spans(q_own),
        spans(q_got),
        spans(d_own),
        spans(d_got),
        stat_own.reshape(2 * group, rows),
        stat_got.reshape(2 * group, rows),
        kv_list,
        scale,
    )
    received, _ = lax.optimization_barrier((received, parts[0]))
    slot_grad = mlp(received, w_gate, w_up, w_down)
    returned = lax.all_to_all(slot_grad, "exp", split_axis=0, concat_axis=0, tiled=True)

    total = own_sum
    for k in range(1, chips // 2):
        total = total + trade(parts[k - 1], 4 * k).astype(F32)
    total = total[: 2 * rows] + trade(total[2 * rows :].astype(BF16), 2).astype(F32)
    total = total.astype(BF16)
    low, high = total[:rows], total[rows:]
    kv_mine = jnp.where(first, low, high)
    kv_theirs = trade(jnp.where(first, high, low), 1)
    dq_back = trade(dq_got, 1)

    def joined(mine, theirs):
        return jnp.concatenate([jnp.where(first, mine, theirs), jnp.where(first, theirs, mine)], axis=1)

    grad_queries = joined(dq_own.reshape(rows, group, size), dq_back.reshape(rows, group, size))
    kv_grads = joined(kv_mine[:, None, :], kv_theirs[:, None, :])
    grad_moe = combine(weight, returned)
    return grad_queries, kv_grads[:, :, :size], kv_grads[:, :, size:], grad_moe


def solution(mesh):
    rows = P(("ctx", "exp"))
    in_specs = (rows,) * 6 + (P(),) + (rows,) * 5 + (P("exp"),) * 3
    return jax.shard_map(
        on_device, mesh=mesh, in_specs=in_specs, out_specs=(rows,) * 4, check_vma=False
    )
```

```python
import functools
import math

import jax
import jax.numpy as jnp
from jax import lax
from jax.experimental import pallas as pl
from jax.experimental.pallas import tpu as pltpu
from jax.sharding import PartitionSpec as P

SLOT = 10
LANES = 128
CHUNK = 256
LONG = 1024
MIB = 1024 * 1024
VMEM = pl.BlockSpec(memory_space=pltpu.VMEM)
SMEM = pl.BlockSpec(memory_space=pltpu.SMEM)
ANY = pl.BlockSpec(memory_space=pl.ANY)
F32 = jnp.float32
BF16 = jnp.bfloat16


def dot(left, right):
    return jnp.dot(left, right, preferred_element_type=F32)


def dot_rows(left, right):
    return lax.dot_general(left, right, (((1,), (1,)), ((), ())), preferred_element_type=F32)


def dot_cols(left, right):
    return lax.dot_general(left, right, (((0,), (0,)), ((), ())), preferred_element_type=F32)


def split3(array):
    high = array.astype(BF16)
    rest = array - high.astype(F32)
    middle = rest.astype(BF16)
    return high, middle, (rest - middle.astype(F32)).astype(BF16)


def attention_kernel(
    scale,
    kv_blocks,
    span_ref,
    q_own,
    q_got,
    d_own,
    d_got,
    stat_own,
    stat_got,
    *rest,
):
    kv_refs = rest[:kv_blocks]
    dq_own, dq_got, own_ref = rest[kv_blocks : kv_blocks + 3]
    part_refs = rest[kv_blocks + 3 : 2 * kv_blocks + 2]
    keys, values, keys_t, dk_acc, dv_acc, dq_acc, stat_acc = rest[2 * kv_blocks + 2 :]
    me = lax.axis_index("ctx")
    chip = me // 2
    core = me % 2
    slots = span_ref.shape[0]
    half = keys.shape[0] // slots
    width = q_own.shape[1]
    repeat = width // half

    def span_of(chip_index, core_index, upper):
        place = chip_index * 2 + core_index
        return span_ref[slots - 1 - place if upper else place]

    stats = jnp.concatenate([stat_own[...], stat_got[...]], axis=0)
    rows = stats.shape[1]
    wide = rows * repeat
    spread = (
        lax.broadcasted_iota(jnp.int32, (rows, wide), 1) // repeat
        == lax.broadcasted_iota(jnp.int32, (rows, wide), 0)
    ).astype(F32).astype(BF16)
    high, middle, low = split3(stats)
    lanes = dot(high, spread) + (dot(middle, spread) + dot(low, spread))
    count = stats.shape[0] // repeat
    lanes = lanes.reshape(count, repeat, wide)
    head = lax.broadcasted_iota(jnp.int32, lanes.shape, 1)
    lane_head = lax.broadcasted_iota(jnp.int32, lanes.shape, 2) % repeat
    stat_acc[...] = jnp.sum(jnp.where(head == lane_head, lanes, 0.0), axis=1)

    for block in range(kv_blocks):
        for part in range(8):
            span = span_of(chip ^ (2 * block + part // 4), part // 2 % 2, part % 2)
            at = pl.ds(pl.multiple_of(span * half, half), half)
            rows = kv_refs[block][part * half : (part + 1) * half, :]
            keys[at, :] = rows[:, :LANES]
            values[at, :] = rows[:, LANES:]
    chunks = keys.shape[0] // CHUNK
    for chunk in range(chunks):
        at = slice(chunk * CHUNK, (chunk + 1) * CHUNK)
        keys_t[:, at] = keys[at, :].T
    dk_acc[...] = jnp.zeros_like(dk_acc)
    dv_acc[...] = jnp.zeros_like(dv_acc)
    factor = scale / math.log(2.0)

    for index in range(4):
        upper = index % 2
        if index < 2:
            q_ref, d_ref, dq_ref, who = q_own, d_own, dq_own, core
        else:
            q_ref, d_ref, dq_ref, who = q_got, d_got, dq_got, 1 - core
        line = 2 * (index // 2)
        span = span_of(chip, who, upper)
        queries = q_ref[upper]
        grads = d_ref[upper]
        norm = stat_acc[line : line + 1, upper * width : (upper + 1) * width] * (1.0 / math.log(2.0))
        inner = stat_acc[line + 1 : line + 2, upper * width : (upper + 1) * width]
        dq_acc[...] = jnp.zeros_like(dq_acc)

        def one(start, count, masked):
            at = pl.ds(pl.multiple_of(start, CHUNK), count)
            scores = dot_rows(keys[at, :], queries)
            probs = jnp.exp2(scores * factor - norm)
            if masked:
                key_pos = start + lax.broadcasted_iota(jnp.int32, scores.shape, 0)
                query_pos = span * half + lax.broadcasted_iota(jnp.int32, scores.shape, 1) // repeat
                probs = jnp.where(key_pos <= query_pos, probs, 0.0)
            dprobs = dot_rows(values[at, :], grads)
            dscores = (probs * (dprobs - inner)).astype(BF16)
            dv_acc[at, :] += dot(probs.astype(BF16), grads)
            dk_acc[at, :] += dot(dscores, queries)
            dq_acc[...] += dot(keys_t[:, at], dscores)

        ahead = span * half
        lax.fori_loop(0, ahead // LONG, lambda i, none: (one(i * LONG, LONG, False), none)[1], 0)
        rest_start = ahead // LONG * LONG

        @pl.when(ahead - rest_start >= LONG // 2)
        def _():
            one(rest_start, LONG // 2, False)

        tail = ahead // (LONG // 2) * (LONG // 2)

        @pl.when(ahead - tail >= CHUNK)
        def _():
            one(tail, LONG // 2, True)

        @pl.when(ahead - tail < CHUNK)
        def _():
            one(tail, CHUNK, True)

        dq_ref[upper] = (dq_acc[...].T * scale).astype(BF16)

    for block in range(kv_blocks):
        for part in range(8):
            span = span_of(chip ^ (2 * block + part // 4), part // 2 % 2, part % 2)
            at = pl.ds(pl.multiple_of(span * half, half), half)
            rows = slice(part * half, (part + 1) * half)
            if block == 0:
                own_ref[rows, :LANES] = dk_acc[at, :] * scale
                own_ref[rows, LANES:] = dv_acc[at, :]
            else:
                part_refs[block - 1][rows, :LANES] = (dk_acc[at, :] * scale).astype(BF16)
                part_refs[block - 1][rows, LANES:] = dv_acc[at, :].astype(BF16)


def attention(span_order, q_own, q_got, d_own, d_got, stat_own, stat_got, kv_list, scale):
    blocks = len(kv_list)
    rows = kv_list[0].shape[0]
    total = blocks * rows
    spans, width, _ = q_own.shape
    part = jax.ShapeDtypeStruct((rows, 2 * LANES), BF16)
    return pl.pallas_call(
        functools.partial(attention_kernel, scale, blocks),
        out_shape=(
            jax.ShapeDtypeStruct(q_own.shape, BF16),
            jax.ShapeDtypeStruct(q_own.shape, BF16),
            jax.ShapeDtypeStruct((rows, 2 * LANES), F32),
        )
        + (part,) * (blocks - 1),
        in_specs=[SMEM] + [VMEM] * (6 + blocks),
        out_specs=(VMEM,) * (2 + blocks),
        scratch_shapes=[
            pltpu.VMEM((total, LANES), BF16),
            pltpu.VMEM((total, LANES), BF16),
            pltpu.VMEM((LANES, total), BF16),
            pltpu.VMEM((total, LANES), F32),
            pltpu.VMEM((total, LANES), F32),
            pltpu.VMEM((LANES, width), F32),
            pltpu.VMEM((4, spans * width), F32),
        ],
        compiler_params=pltpu.CompilerParams(vmem_limit_bytes=16 * MIB),
        cost_estimate=pl.CostEstimate(
            flops=60 * spans * width * total * LANES * 2,
            bytes_accessed=6 * 1024 * 1024,
            transcendentals=spans * width * total,
        ),
        name="attention",
    )(span_order, q_own, q_got, d_own, d_got, stat_own, stat_got, *kv_list)


def slots_to_chunks(tiles, experts, blocks, chunk_ref, first):
    for expert in range(experts):
        for block in range(blocks):
            at = first + block * SLOT
            chunk_ref[expert, at : at + SLOT, :] = tiles[block, expert * SLOT : (expert + 1) * SLOT, :]


def dispatch_kernel(ids_ref, keep_ref, weight_ref, x_hbm, g_hbm, send_ref, combine_ref, x_ref, g_ref, tiles, chunks, sems):
    loads = [
        pltpu.make_async_copy(source, target, sems.at[i])
        for i, (source, target) in enumerate(((x_hbm, x_ref), (g_hbm, g_ref)))
    ]
    for load in loads:
        load.start()
    top, rows = ids_ref.shape
    experts = send_ref.shape[0]
    blocks = x_ref.shape[1] // LANES
    slots = experts * SLOT
    line = lax.broadcasted_iota(jnp.int32, (slots, rows), 0)
    expert_of = line // SLOT
    slot_of = line - expert_of * SLOT
    ids = jnp.where(keep_ref[...] == 1, ids_ref[...], -1)
    weights = weight_ref[...]
    hit = jnp.zeros((slots, rows), F32)
    weight = jnp.zeros((slots, rows), F32)
    for k in range(top):
        match = ids[k : k + 1, :] == expert_of
        hit = jnp.where(match, 1.0, hit)
        weight = jnp.where(match, weights[k : k + 1, :], weight)
    earlier = (
        lax.broadcasted_iota(jnp.int32, (rows, rows), 0)
        < lax.broadcasted_iota(jnp.int32, (rows, rows), 1)
    ).astype(F32).astype(BF16)
    rank = dot(hit.astype(BF16), earlier)
    chosen = jnp.where(rank == slot_of.astype(F32), hit, 0.0)
    combine_ref[...] = chosen * weight
    pick = chosen.astype(BF16)
    for load, source, first in ((loads[0], x_ref, 0), (loads[1], g_ref, blocks * SLOT)):
        load.wait()
        for pair in range(blocks // 2):
            both = dot(pick, source[:, pair * 2 * LANES : (pair + 1) * 2 * LANES])
            tiles[2 * pair] = both[:, :LANES]
            tiles[2 * pair + 1] = both[:, LANES:]
        slots_to_chunks(tiles, experts, blocks, chunks, first)
    send_ref[...] = chunks[...].astype(BF16)


def dispatch(ids, keep, weight, x, g, experts):
    rows = ids.shape[0]
    blocks = x.shape[1] // LANES
    slots = experts * SLOT
    return pl.pallas_call(
        dispatch_kernel,
        out_shape=(
            jax.ShapeDtypeStruct((experts, 2 * blocks * SLOT, LANES), BF16),
            jax.ShapeDtypeStruct((slots, rows), F32),
        ),
        in_specs=[VMEM] * 3 + [ANY] * 2,
        out_specs=(VMEM, VMEM),
        scratch_shapes=[
            pltpu.VMEM(x.shape, BF16),
            pltpu.VMEM(g.shape, BF16),
            pltpu.VMEM((blocks, slots, LANES), F32),
            pltpu.VMEM((experts, 2 * blocks * SLOT, LANES), F32),
            pltpu.SemaphoreType.DMA((2,)),
        ],
        compiler_params=pltpu.CompilerParams(vmem_limit_bytes=60 * MIB),
        name="dispatch",
    )(ids.T, keep.T, weight.T, x, g)


def mlp_kernel(in_ref, *rest):
    weights_hbm = rest[:3]
    out_ref = rest[3]
    weights = rest[4:7]
    chunks, tiles, x_rows, g_rows, sems = rest[7:]
    sources = in_ref.shape[0]
    blocks = x_rows.shape[1] // LANES
    hidden = weights[0].shape[1]
    tile = 256
    loads = []
    for step in range(hidden // tile):
        part = slice(step * tile, (step + 1) * tile)
        for i in range(3):
            at = (slice(None), part) if i < 2 else (part, slice(None))
            load = pltpu.make_async_copy(weights_hbm[i].at[(0,) + at], weights[i].at[at], sems.at[3 * step + i])
            load.start()
            loads.append(load)
    chunks[...] = in_ref[...].astype(F32)
    for rows_ref, first in ((x_rows, 0), (g_rows, blocks * SLOT)):
        for block in range(blocks):
            for source in range(sources):
                at = first + block * SLOT
                tiles[block, source * SLOT : (source + 1) * SLOT, :] = chunks[source, at : at + SLOT, :]
            rows_ref[:, block * LANES : (block + 1) * LANES] = tiles[block].astype(BF16)
    total = None
    for step in range(hidden // tile):
        for i in range(3):
            loads[3 * step + i].wait()
        part = slice(step * tile, (step + 1) * tile)
        gate_w, up_w = weights[0][:, part], weights[1][:, part]
        gate_pre = dot(x_rows[...], gate_w)
        up_pre = dot(x_rows[...], up_w)
        hidden_grad = dot_rows(g_rows[...], weights[2][part, :])
        sig = jax.nn.sigmoid(gate_pre)
        gate_grad = (hidden_grad * up_pre * sig * (1.0 + gate_pre * (1.0 - sig))).astype(BF16)
        up_grad = (hidden_grad * gate_pre * sig).astype(BF16)
        term = dot_rows(gate_grad, gate_w) + dot_rows(up_grad, up_w)
        for block in range(blocks):
            piece = term[:, block * LANES : (block + 1) * LANES]
            tiles[block] = piece if step == 0 else tiles[block] + piece
    slots_to_chunks(tiles, sources, blocks, chunks, 0)
    out_ref[...] = chunks[:, : blocks * SLOT, :].astype(BF16)


def mlp(received, w_gate, w_up, w_down):
    sources, chunk_rows, _ = received.shape
    _, width, hidden = w_gate.shape
    blocks = width // LANES
    slots = sources * SLOT
    return pl.pallas_call(
        mlp_kernel,
        out_shape=jax.ShapeDtypeStruct((sources, blocks * SLOT, LANES), BF16),
        in_specs=[VMEM] + [ANY] * 3,
        out_specs=VMEM,
        scratch_shapes=[
            pltpu.VMEM((width, hidden), BF16),
            pltpu.VMEM((width, hidden), BF16),
            pltpu.VMEM((hidden, width), BF16),
            pltpu.VMEM((sources, chunk_rows, LANES), F32),
            pltpu.VMEM((blocks, slots, LANES), F32),
            pltpu.VMEM((slots, width), BF16),
            pltpu.VMEM((slots, width), BF16),
            pltpu.SemaphoreType.DMA((9,)),
        ],
        compiler_params=pltpu.CompilerParams(vmem_limit_bytes=58 * MIB),
        cost_estimate=pl.CostEstimate(
            flops=10 * slots * width * hidden, bytes_accessed=11 * 1024 * 1024, transcendentals=slots * hidden
        ),
        name="experts",
    )(received, w_gate, w_up, w_down)


def combine_kernel(weight_ref, back_ref, out_ref, chunks, tiles):
    experts = back_ref.shape[0]
    blocks = out_ref.shape[1] // LANES
    chunks[...] = back_ref[...].astype(F32)
    weight = weight_ref[...].T
    high = weight.astype(BF16)
    rest = weight - high.astype(F32)
    middle = rest.astype(BF16)
    low = (rest - middle.astype(F32)).astype(BF16)
    for block in range(blocks):
        for expert in range(experts):
            at = block * SLOT
            tiles[block, expert * SLOT : (expert + 1) * SLOT, :] = chunks[expert, at : at + SLOT, :]
    for pair in range(blocks // 2):
        rows = jnp.concatenate([tiles[2 * pair], tiles[2 * pair + 1]], axis=1).astype(BF16)
        out = dot(high, rows) + (dot(middle, rows) + dot(low, rows))
        out_ref[:, pair * 2 * LANES : (pair + 1) * 2 * LANES] = out.astype(BF16)


def combine(weight, back):
    experts, chunk_rows, _ = back.shape
    slots, rows = weight.shape
    blocks = chunk_rows // SLOT
    return pl.pallas_call(
        combine_kernel,
        out_shape=jax.ShapeDtypeStruct((rows, blocks * LANES), BF16),
        in_specs=[VMEM, VMEM],
        out_specs=VMEM,
        scratch_shapes=[
            pltpu.VMEM((experts, chunk_rows, LANES), F32),
            pltpu.VMEM((blocks, slots, LANES), F32),
        ],
        compiler_params=pltpu.CompilerParams(vmem_limit_bytes=12 * MIB),
        name="combine",
    )(weight, back)


def on_device(
    queries,
    key_tensor,
    value_tensor,
    out_grad,
    log_norm,
    out_dot,
    span_order,
    moe_input,
    moe_grad,
    expert_ids,
    keep_mask,
    route_weight,
    w_gate,
    w_up,
    w_down,
):
    rows, heads, size = queries.shape
    group = heads // 2
    scale = 1.0 / math.sqrt(size)
    members = lax.axis_size("ctx")
    experts = lax.axis_size("exp")
    first = lax.axis_index("ctx") & 1 == 0
    chips = members // 2
    trade = lambda array, k: lax.ppermute(array, "ctx", [(i, i ^ k) for i in range(members)])

    kv = jnp.concatenate([key_tensor, value_tensor], axis=2)
    kv_own = jnp.where(first, kv[:, 0], kv[:, 1])
    kv_away = jnp.where(first, kv[:, 1], kv[:, 0])
    kv_own, kv_away, expert_ids = lax.optimization_barrier((kv_own, kv_away, expert_ids))
    kv_got = trade(kv_away, 1)
    kv_near, kv_cross = trade(kv_own, 2), trade(kv_away, 3)
    send, weight = dispatch(expert_ids, keep_mask, route_weight, moe_input, moe_grad, experts)
    ordered = lambda mine, other: [jnp.where(first, mine, other), jnp.where(first, other, mine)]
    kv_pair = jnp.concatenate(ordered(kv_own, kv_got) + ordered(kv_near, kv_cross), axis=0)
    send, kv_pair = lax.optimization_barrier((send, kv_pair))
    received = lax.all_to_all(send, "exp", split_axis=0, concat_axis=0, tiled=True)
    kv_list = [kv_pair] + [trade(kv_pair, 4 * k) for k in range(1, chips // 2)]

    def halves(array, axis):
        low, high = jnp.split(array, 2, axis=axis)
        return jnp.where(first, low, high), jnp.where(first, high, low)

    q_own, q_away = halves(queries, 1)
    d_own, d_away = halves(out_grad, 1)
    stat_own, stat_away = halves(jnp.stack([log_norm.T, out_dot.T]), 1)
    q_got, d_got = trade(q_away, 1), trade(d_away, 1)
    stat_got = trade(stat_away, 1)

    spans = lambda array: array.reshape(2, rows // 2 * group, size)
    dq_own, dq_got, own_sum, *parts = attention(
        span_order,
        spans(q_own),
        spans(q_got),
        spans(d_own),
        spans(d_got),
        stat_own.reshape(2 * group, rows),
        stat_got.reshape(2 * group, rows),
        kv_list,
        scale,
    )
    received, _ = lax.optimization_barrier((received, parts[0]))
    slot_grad = mlp(received, w_gate, w_up, w_down)
    returned = lax.all_to_all(slot_grad, "exp", split_axis=0, concat_axis=0, tiled=True)

    total = own_sum
    for k in range(1, chips // 2):
        total = total + trade(parts[k - 1], 4 * k).astype(F32)
    total = total[: 2 * rows] + trade(total[2 * rows :].astype(BF16), 2).astype(F32)
    total = total.astype(BF16)
    low, high = total[:rows], total[rows:]
    kv_mine = jnp.where(first, low, high)
    kv_theirs = trade(jnp.where(first, high, low), 1)
    dq_back = trade(dq_got, 1)

    def joined(mine, theirs):
        return jnp.concatenate([jnp.where(first, mine, theirs), jnp.where(first, theirs, mine)], axis=1)

    grad_queries = joined(dq_own.reshape(rows, group, size), dq_back.reshape(rows, group, size))
    kv_grads = joined(kv_mine[:, None, :], kv_theirs[:, None, :])
    grad_moe = combine(weight, returned)
    return grad_queries, kv_grads[:, :, :size], kv_grads[:, :, size:], grad_moe


def solution(mesh):
    rows = P(("ctx", "exp"))
    in_specs = (rows,) * 6 + (P(),) + (rows,) * 5 + (P("exp"),) * 3
    return jax.shard_map(
        on_device, mesh=mesh, in_specs=in_specs, out_specs=(rows,) * 4, check_vma=False
    )
```

```python
import functools
import math

import jax
import jax.numpy as jnp
from jax import lax
from jax.experimental import pallas as pl
from jax.experimental.pallas import tpu as pltpu
from jax.sharding import PartitionSpec as P

SLOT = 10
LANES = 128
CHUNK = 256
LONG = 1024
MIB = 1024 * 1024
VMEM = pl.BlockSpec(memory_space=pltpu.VMEM)
SMEM = pl.BlockSpec(memory_space=pltpu.SMEM)
ANY = pl.BlockSpec(memory_space=pl.ANY)
F32 = jnp.float32
BF16 = jnp.bfloat16


def dot(left, right):
    return jnp.dot(left, right, preferred_element_type=F32)


def dot_rows(left, right):
    return lax.dot_general(left, right, (((1,), (1,)), ((), ())), preferred_element_type=F32)


def dot_cols(left, right):
    return lax.dot_general(left, right, (((0,), (0,)), ((), ())), preferred_element_type=F32)


def split3(array):
    high = array.astype(BF16)
    rest = array - high.astype(F32)
    middle = rest.astype(BF16)
    return high, middle, (rest - middle.astype(F32)).astype(BF16)


def attention_kernel(
    scale,
    kv_blocks,
    span_ref,
    q_own,
    q_got,
    d_own,
    d_got,
    stat_own,
    stat_got,
    *rest,
):
    kv_refs = rest[:kv_blocks]
    dq_own, dq_got, own_ref = rest[kv_blocks : kv_blocks + 3]
    part_refs = rest[kv_blocks + 3 : 2 * kv_blocks + 2]
    keys, values, keys_t, dk_acc, dv_acc, dq_acc, stat_acc = rest[2 * kv_blocks + 2 :]
    me = lax.axis_index("ctx")
    chip = me // 2
    core = me % 2
    slots = span_ref.shape[0]
    half = keys.shape[0] // slots
    width = q_own.shape[1]
    repeat = width // half

    def span_of(chip_index, core_index, upper):
        place = chip_index * 2 + core_index
        return span_ref[slots - 1 - place if upper else place]

    stats = jnp.concatenate([stat_own[...], stat_got[...]], axis=0)
    rows = stats.shape[1]
    wide = rows * repeat
    spread = (
        lax.broadcasted_iota(jnp.int32, (rows, wide), 1) // repeat
        == lax.broadcasted_iota(jnp.int32, (rows, wide), 0)
    ).astype(F32).astype(BF16)
    high, middle, low = split3(stats)
    lanes = dot(high, spread) + (dot(middle, spread) + dot(low, spread))
    count = stats.shape[0] // repeat
    lanes = lanes.reshape(count, repeat, wide)
    head = lax.broadcasted_iota(jnp.int32, lanes.shape, 1)
    lane_head = lax.broadcasted_iota(jnp.int32, lanes.shape, 2) % repeat
    stat_acc[...] = jnp.sum(jnp.where(head == lane_head, lanes, 0.0), axis=1)

    for block in range(kv_blocks):
        for part in range(8):
            span = span_of(chip ^ (2 * block + part // 4), part // 2 % 2, part % 2)
            at = pl.ds(pl.multiple_of(span * half, half), half)
            rows = kv_refs[block][part * half : (part + 1) * half, :]
            keys[at, :] = rows[:, :LANES]
            values[at, :] = rows[:, LANES:]
    chunks = keys.shape[0] // CHUNK
    for chunk in range(chunks):
        at = slice(chunk * CHUNK, (chunk + 1) * CHUNK)
        keys_t[:, at] = keys[at, :].T
    dk_acc[...] = jnp.zeros_like(dk_acc)
    dv_acc[...] = jnp.zeros_like(dv_acc)
    factor = scale / math.log(2.0)

    for index in range(4):
        upper = index % 2
        if index < 2:
            q_ref, d_ref, dq_ref, who = q_own, d_own, dq_own, core
        else:
            q_ref, d_ref, dq_ref, who = q_got, d_got, dq_got, 1 - core
        line = 2 * (index // 2)
        span = span_of(chip, who, upper)
        queries = q_ref[upper]
        grads = d_ref[upper]
        norm = stat_acc[line : line + 1, upper * width : (upper + 1) * width] * (1.0 / math.log(2.0))
        inner = stat_acc[line + 1 : line + 2, upper * width : (upper + 1) * width]
        dq_acc[...] = jnp.zeros_like(dq_acc)

        def one(start, count, masked):
            at = pl.ds(pl.multiple_of(start, CHUNK), count)
            scores = dot_rows(keys[at, :], queries)
            probs = jnp.exp2(scores * factor - norm)
            if masked:
                key_pos = start + lax.broadcasted_iota(jnp.int32, scores.shape, 0)
                query_pos = span * half + lax.broadcasted_iota(jnp.int32, scores.shape, 1) // repeat
                probs = jnp.where(key_pos <= query_pos, probs, 0.0)
            dprobs = dot_rows(values[at, :], grads)
            dscores = (probs * (dprobs - inner)).astype(BF16)
            dv_acc[at, :] += dot(probs.astype(BF16), grads)
            dk_acc[at, :] += dot(dscores, queries)
            dq_acc[...] += dot(keys_t[:, at], dscores)

        ahead = span * half
        lax.fori_loop(0, ahead // LONG, lambda i, none: (one(i * LONG, LONG, False), none)[1], 0)
        rest_start = ahead // LONG * LONG

        @pl.when(ahead - rest_start >= LONG // 2)
        def _():
            one(rest_start, LONG // 2, False)

        tail = ahead // (LONG // 2) * (LONG // 2)

        @pl.when(ahead - tail >= CHUNK)
        def _():
            one(tail, LONG // 2, True)

        @pl.when(ahead - tail < CHUNK)
        def _():
            one(tail, CHUNK, True)

        dq_ref[upper] = (dq_acc[...].T * scale).astype(BF16)

    for block in range(kv_blocks):
        for part in range(8):
            span = span_of(chip ^ (2 * block + part // 4), part // 2 % 2, part % 2)
            at = pl.ds(pl.multiple_of(span * half, half), half)
            rows = slice(part * half, (part + 1) * half)
            if block == 0:
                own_ref[rows, :LANES] = dk_acc[at, :] * scale
                own_ref[rows, LANES:] = dv_acc[at, :]
            else:
                part_refs[block - 1][rows, :LANES] = (dk_acc[at, :] * scale).astype(BF16)
                part_refs[block - 1][rows, LANES:] = dv_acc[at, :].astype(BF16)


def attention(span_order, q_own, q_got, d_own, d_got, stat_own, stat_got, kv_list, scale):
    blocks = len(kv_list)
    rows = kv_list[0].shape[0]
    total = blocks * rows
    spans, width, _ = q_own.shape
    part = jax.ShapeDtypeStruct((rows, 2 * LANES), BF16)
    return pl.pallas_call(
        functools.partial(attention_kernel, scale, blocks),
        out_shape=(
            jax.ShapeDtypeStruct(q_own.shape, BF16),
            jax.ShapeDtypeStruct(q_own.shape, BF16),
            jax.ShapeDtypeStruct((rows, 2 * LANES), F32),
        )
        + (part,) * (blocks - 1),
        in_specs=[SMEM] + [VMEM] * (6 + blocks),
        out_specs=(VMEM,) * (2 + blocks),
        scratch_shapes=[
            pltpu.VMEM((total, LANES), BF16),
            pltpu.VMEM((total, LANES), BF16),
            pltpu.VMEM((LANES, total), BF16),
            pltpu.VMEM((total, LANES), F32),
            pltpu.VMEM((total, LANES), F32),
            pltpu.VMEM((LANES, width), F32),
            pltpu.VMEM((4, spans * width), F32),
        ],
        compiler_params=pltpu.CompilerParams(vmem_limit_bytes=16 * MIB),
        cost_estimate=pl.CostEstimate(
            flops=6 * spans * width * total * LANES * 2,
            bytes_accessed=6 * 1024 * 1024,
            transcendentals=spans * width * total // 12,
        ),
        name="attention",
    )(span_order, q_own, q_got, d_own, d_got, stat_own, stat_got, *kv_list)


def slots_to_chunks(tiles, experts, blocks, chunk_ref, first):
    for expert in range(experts):
        for block in range(blocks):
            at = first + block * SLOT
            chunk_ref[expert, at : at + SLOT, :] = tiles[block, expert * SLOT : (expert + 1) * SLOT, :]


def dispatch_kernel(ids_ref, keep_ref, weight_ref, x_hbm, g_hbm, send_ref, combine_ref, x_ref, g_ref, tiles, chunks, sems):
    loads = [
        pltpu.make_async_copy(source, target, sems.at[i])
        for i, (source, target) in enumerate(((x_hbm, x_ref), (g_hbm, g_ref)))
    ]
    for load in loads:
        load.start()
    top, rows = ids_ref.shape
    experts = send_ref.shape[0]
    blocks = x_ref.shape[1] // LANES
    slots = experts * SLOT
    line = lax.broadcasted_iota(jnp.int32, (slots, rows), 0)
    expert_of = line // SLOT
    slot_of = line - expert_of * SLOT
    ids = jnp.where(keep_ref[...] == 1, ids_ref[...], -1)
    weights = weight_ref[...]
    hit = jnp.zeros((slots, rows), F32)
    weight = jnp.zeros((slots, rows), F32)
    for k in range(top):
        match = ids[k : k + 1, :] == expert_of
        hit = jnp.where(match, 1.0, hit)
        weight = jnp.where(match, weights[k : k + 1, :], weight)
    earlier = (
        lax.broadcasted_iota(jnp.int32, (rows, rows), 0)
        < lax.broadcasted_iota(jnp.int32, (rows, rows), 1)
    ).astype(F32).astype(BF16)
    rank = dot(hit.astype(BF16), earlier)
    chosen = jnp.where(rank == slot_of.astype(F32), hit, 0.0)
    combine_ref[...] = chosen * weight
    pick = chosen.astype(BF16)
    for load, source, first in ((loads[0], x_ref, 0), (loads[1], g_ref, blocks * SLOT)):
        load.wait()
        for pair in range(blocks // 2):
            both = dot(pick, source[:, pair * 2 * LANES : (pair + 1) * 2 * LANES])
            tiles[2 * pair] = both[:, :LANES]
            tiles[2 * pair + 1] = both[:, LANES:]
        slots_to_chunks(tiles, experts, blocks, chunks, first)
    send_ref[...] = chunks[...].astype(BF16)


def dispatch(ids, keep, weight, x, g, experts):
    rows = ids.shape[0]
    blocks = x.shape[1] // LANES
    slots = experts * SLOT
    return pl.pallas_call(
        dispatch_kernel,
        out_shape=(
            jax.ShapeDtypeStruct((experts, 2 * blocks * SLOT, LANES), BF16),
            jax.ShapeDtypeStruct((slots, rows), F32),
        ),
        in_specs=[VMEM] * 3 + [ANY] * 2,
        out_specs=(VMEM, VMEM),
        scratch_shapes=[
            pltpu.VMEM(x.shape, BF16),
            pltpu.VMEM(g.shape, BF16),
            pltpu.VMEM((blocks, slots, LANES), F32),
            pltpu.VMEM((experts, 2 * blocks * SLOT, LANES), F32),
            pltpu.SemaphoreType.DMA((2,)),
        ],
        compiler_params=pltpu.CompilerParams(vmem_limit_bytes=60 * MIB),
        name="dispatch",
    )(ids.T, keep.T, weight.T, x, g)


def mlp_kernel(in_ref, *rest):
    weights_hbm = rest[:3]
    out_ref = rest[3]
    weights = rest[4:7]
    chunks, tiles, x_rows, g_rows, sems = rest[7:]
    sources = in_ref.shape[0]
    blocks = x_rows.shape[1] // LANES
    hidden = weights[0].shape[1]
    tile = 256
    loads = []
    for step in range(hidden // tile):
        part = slice(step * tile, (step + 1) * tile)
        for i in range(3):
            at = (slice(None), part) if i < 2 else (part, slice(None))
            load = pltpu.make_async_copy(weights_hbm[i].at[(0,) + at], weights[i].at[at], sems.at[3 * step + i])
            load.start()
            loads.append(load)
    chunks[...] = in_ref[...].astype(F32)
    for rows_ref, first in ((x_rows, 0), (g_rows, blocks * SLOT)):
        for block in range(blocks):
            for source in range(sources):
                at = first + block * SLOT
                tiles[block, source * SLOT : (source + 1) * SLOT, :] = chunks[source, at : at + SLOT, :]
            rows_ref[:, block * LANES : (block + 1) * LANES] = tiles[block].astype(BF16)
    total = None
    for step in range(hidden // tile):
        for i in range(3):
            loads[3 * step + i].wait()
        part = slice(step * tile, (step + 1) * tile)
        gate_w, up_w = weights[0][:, part], weights[1][:, part]
        gate_pre = dot(x_rows[...], gate_w)
        up_pre = dot(x_rows[...], up_w)
        hidden_grad = dot_rows(g_rows[...], weights[2][part, :])
        sig = jax.nn.sigmoid(gate_pre)
        gate_grad = (hidden_grad * up_pre * sig * (1.0 + gate_pre * (1.0 - sig))).astype(BF16)
        up_grad = (hidden_grad * gate_pre * sig).astype(BF16)
        term = dot_rows(gate_grad, gate_w) + dot_rows(up_grad, up_w)
        for block in range(blocks):
            piece = term[:, block * LANES : (block + 1) * LANES]
            tiles[block] = piece if step == 0 else tiles[block] + piece
    slots_to_chunks(tiles, sources, blocks, chunks, 0)
    out_ref[...] = chunks[:, : blocks * SLOT, :].astype(BF16)


def mlp(received, w_gate, w_up, w_down):
    sources, chunk_rows, _ = received.shape
    _, width, hidden = w_gate.shape
    blocks = width // LANES
    slots = sources * SLOT
    return pl.pallas_call(
        mlp_kernel,
        out_shape=jax.ShapeDtypeStruct((sources, blocks * SLOT, LANES), BF16),
        in_specs=[VMEM] + [ANY] * 3,
        out_specs=VMEM,
        scratch_shapes=[
            pltpu.VMEM((width, hidden), BF16),
            pltpu.VMEM((width, hidden), BF16),
            pltpu.VMEM((hidden, width), BF16),
            pltpu.VMEM((sources, chunk_rows, LANES), F32),
            pltpu.VMEM((blocks, slots, LANES), F32),
            pltpu.VMEM((slots, width), BF16),
            pltpu.VMEM((slots, width), BF16),
            pltpu.SemaphoreType.DMA((9,)),
        ],
        compiler_params=pltpu.CompilerParams(vmem_limit_bytes=58 * MIB),
        cost_estimate=pl.CostEstimate(
            flops=10 * slots * width * hidden, bytes_accessed=11 * 1024 * 1024, transcendentals=slots * hidden
        ),
        name="experts",
    )(received, w_gate, w_up, w_down)


def combine_kernel(weight_ref, back_ref, out_ref, chunks, tiles):
    experts = back_ref.shape[0]
    blocks = out_ref.shape[1] // LANES
    chunks[...] = back_ref[...].astype(F32)
    weight = weight_ref[...].T
    high = weight.astype(BF16)
    rest = weight - high.astype(F32)
    middle = rest.astype(BF16)
    low = (rest - middle.astype(F32)).astype(BF16)
    for block in range(blocks):
        for expert in range(experts):
            at = block * SLOT
            tiles[block, expert * SLOT : (expert + 1) * SLOT, :] = chunks[expert, at : at + SLOT, :]
    for pair in range(blocks // 2):
        rows = jnp.concatenate([tiles[2 * pair], tiles[2 * pair + 1]], axis=1).astype(BF16)
        out = dot(high, rows) + (dot(middle, rows) + dot(low, rows))
        out_ref[:, pair * 2 * LANES : (pair + 1) * 2 * LANES] = out.astype(BF16)


def combine(weight, back):
    experts, chunk_rows, _ = back.shape
    slots, rows = weight.shape
    blocks = chunk_rows // SLOT
    return pl.pallas_call(
        combine_kernel,
        out_shape=jax.ShapeDtypeStruct((rows, blocks * LANES), BF16),
        in_specs=[VMEM, VMEM],
        out_specs=VMEM,
        scratch_shapes=[
            pltpu.VMEM((experts, chunk_rows, LANES), F32),
            pltpu.VMEM((blocks, slots, LANES), F32),
        ],
        compiler_params=pltpu.CompilerParams(vmem_limit_bytes=12 * MIB),
        name="combine",
    )(weight, back)


def on_device(
    queries,
    key_tensor,
    value_tensor,
    out_grad,
    log_norm,
    out_dot,
    span_order,
    moe_input,
    moe_grad,
    expert_ids,
    keep_mask,
    route_weight,
    w_gate,
    w_up,
    w_down,
):
    rows, heads, size = queries.shape
    group = heads // 2
    scale = 1.0 / math.sqrt(size)
    members = lax.axis_size("ctx")
    experts = lax.axis_size("exp")
    first = lax.axis_index("ctx") & 1 == 0
    chips = members // 2
    trade = lambda array, k: lax.ppermute(array, "ctx", [(i, i ^ k) for i in range(members)])

    send, weight = dispatch(expert_ids, keep_mask, route_weight, moe_input, moe_grad, experts)
    send, key_tensor, value_tensor = lax.optimization_barrier((send, key_tensor, value_tensor))
    kv = jnp.concatenate([key_tensor, value_tensor], axis=2)
    kv_own = jnp.where(first, kv[:, 0], kv[:, 1])
    kv_away = jnp.where(first, kv[:, 1], kv[:, 0])
    kv_got = trade(kv_away, 1)
    kv_near, kv_cross = trade(kv_own, 2), trade(kv_away, 3)
    ordered = lambda mine, other: [jnp.where(first, mine, other), jnp.where(first, other, mine)]
    kv_pair = jnp.concatenate(ordered(kv_own, kv_got) + ordered(kv_near, kv_cross), axis=0)
    received = lax.all_to_all(send, "exp", split_axis=0, concat_axis=0, tiled=True)
    kv_list = [kv_pair] + [trade(kv_pair, 4 * k) for k in range(1, chips // 2)]

    kv_near, queries, out_grad, log_norm, out_dot = lax.optimization_barrier(
        (kv_near, queries, out_grad, log_norm, out_dot)
    )

    def halves(array, axis):
        low, high = jnp.split(array, 2, axis=axis)
        return jnp.where(first, low, high), jnp.where(first, high, low)

    q_own, q_away = halves(queries, 1)
    d_own, d_away = halves(out_grad, 1)
    stat_own, stat_away = halves(jnp.stack([log_norm.T, out_dot.T]), 1)
    q_got, d_got = trade(q_away, 1), trade(d_away, 1)
    stat_got = trade(stat_away, 1)

    spans = lambda array: array.reshape(2, rows // 2 * group, size)
    dq_own, dq_got, own_sum, *parts = attention(
        span_order,
        spans(q_own),
        spans(q_got),
        spans(d_own),
        spans(d_got),
        stat_own.reshape(2 * group, rows),
        stat_got.reshape(2 * group, rows),
        kv_list,
        scale,
    )
    received, _ = lax.optimization_barrier((received, parts[0]))
    slot_grad = mlp(received, w_gate, w_up, w_down)
    returned = lax.all_to_all(slot_grad, "exp", split_axis=0, concat_axis=0, tiled=True)

    total, _ = lax.optimization_barrier((own_sum, slot_grad))
    for k in range(1, chips // 2):
        total = total + trade(parts[k - 1], 4 * k).astype(F32)
    blocks = [total[i * rows : (i + 1) * rows] for i in range(4)]
    mine, near = ordered(blocks[0], blocks[1]), ordered(blocks[2], blocks[3])
    own_head = mine[0] + trade(near[0].astype(BF16), 2).astype(F32)
    other_head = trade(mine[1].astype(BF16), 1).astype(F32) + trade(near[1].astype(BF16), 3).astype(F32)
    dq_got, _ = lax.optimization_barrier((dq_got, slot_grad))
    dq_back = trade(dq_got, 1)

    def joined(own, other):
        return jnp.concatenate(ordered(own, other), axis=1)

    grad_queries = joined(dq_own.reshape(rows, group, size), dq_back.reshape(rows, group, size))
    kv_grads = joined(own_head.astype(BF16)[:, None, :], other_head.astype(BF16)[:, None, :])
    grad_moe = combine(weight, returned)
    return grad_queries, kv_grads[:, :, :size], kv_grads[:, :, size:], grad_moe


def solution(mesh):
    rows = P(("ctx", "exp"))
    in_specs = (rows,) * 6 + (P(),) + (rows,) * 5 + (P("exp"),) * 3
    return jax.shard_map(
        on_device, mesh=mesh, in_specs=in_specs, out_specs=(rows,) * 4, check_vma=False
    )
```

```python
import functools
import math

import jax
import jax.numpy as jnp
from jax import lax
from jax.experimental import pallas as pl
from jax.experimental.pallas import tpu as pltpu
from jax.sharding import PartitionSpec as P

SLOT = 10
LANES = 128
CHUNK = 256
LONG = 1024
MIB = 1024 * 1024
VMEM = pl.BlockSpec(memory_space=pltpu.VMEM)
SMEM = pl.BlockSpec(memory_space=pltpu.SMEM)
ANY = pl.BlockSpec(memory_space=pl.ANY)
F32 = jnp.float32
BF16 = jnp.bfloat16


def dot(left, right):
    return jnp.dot(left, right, preferred_element_type=F32)


def dot_rows(left, right):
    return lax.dot_general(left, right, (((1,), (1,)), ((), ())), preferred_element_type=F32)


def dot_cols(left, right):
    return lax.dot_general(left, right, (((0,), (0,)), ((), ())), preferred_element_type=F32)


def split3(array):
    high = array.astype(BF16)
    rest = array - high.astype(F32)
    middle = rest.astype(BF16)
    return high, middle, (rest - middle.astype(F32)).astype(BF16)


def span_finder(span_ref):
    slots = span_ref.shape[0]

    def span_of(chip, core, upper):
        place = chip * 2 + core
        return span_ref[slots - 1 - place if upper else place]

    return span_of


def pair_gradients(scale, queries, grads, norm, inner, keys, values, keys_t, visible):
    scores = dot_rows(keys, queries)
    probs = jnp.exp2(scores * (scale / math.log(2.0)) - norm)
    if visible is not None:
        probs = jnp.where(visible(scores.shape), probs, 0.0)
    dprobs = dot_rows(values, grads)
    dscores = (probs * (dprobs - inner)).astype(BF16)
    return dot(dscores, queries), dot(probs.astype(BF16), grads), dot(keys_t, dscores)


def near_kernel(
    scale, span_ref, q_own, q_got, d_own, d_got, stat_own, stat_got, kv_ref, dq_ref, sum_ref, stat_ref, keys_t, key_pos
):
    me = lax.axis_index("ctx")
    chip, core = me // 2, me % 2
    span_of = span_finder(span_ref)
    width = q_own.shape[1]
    count = kv_ref.shape[0]
    half = count // 8
    repeat = width // half

    stats = jnp.concatenate([stat_own[...], stat_got[...]], axis=0)
    rows = stats.shape[1]
    wide = rows * repeat
    spread = (
        lax.broadcasted_iota(jnp.int32, (rows, wide), 1) // repeat
        == lax.broadcasted_iota(jnp.int32, (rows, wide), 0)
    ).astype(F32).astype(BF16)
    high, middle, low = split3(stats)
    lanes = dot(high, spread) + (dot(middle, spread) + dot(low, spread))
    lanes = lanes.reshape(stats.shape[0] // repeat, repeat, wide)
    head = lax.broadcasted_iota(jnp.int32, lanes.shape, 1)
    lane_head = lax.broadcasted_iota(jnp.int32, lanes.shape, 2) % repeat
    lanes = jnp.sum(jnp.where(head == lane_head, lanes, 0.0), axis=1)
    is_norm = lax.broadcasted_iota(jnp.int32, lanes.shape, 0) % 2 == 0
    stat_ref[...] = jnp.where(is_norm, lanes * (1.0 / math.log(2.0)), lanes)

    keys_t[...] = kv_ref[:, :LANES].T
    for part in range(8):
        span = span_of(chip ^ (part // 4), part // 2 % 2, part % 2)
        at = slice(part * half, (part + 1) * half)
        key_pos[at, :] = span * half + lax.broadcasted_iota(jnp.int32, (half, LANES), 0)

    for index in range(4):
        upper = index % 2
        q_ref, d_ref, who = (q_own, d_own, core) if index < 2 else (q_got, d_got, 1 - core)
        line = 2 * (index // 2)
        span = span_of(chip, who, upper)

        def visible(shape):
            query_pos = span * half + lax.broadcasted_iota(jnp.int32, shape, 1) // repeat
            return jnp.concatenate([key_pos[...]] * (width // LANES), axis=1) <= query_pos

        at = slice(upper * width, (upper + 1) * width)
        dk, dv, dq = pair_gradients(
            scale,
            q_ref[upper],
            d_ref[upper],
            stat_ref[line : line + 1, at],
            stat_ref[line + 1 : line + 2, at],
            kv_ref[:, :LANES],
            kv_ref[:, LANES:],
            keys_t[...],
            visible,
        )
        dq_ref[index] = dq
        dk = dk * scale
        sum_ref[:, :LANES] = dk if index == 0 else sum_ref[:, :LANES] + dk
        sum_ref[:, LANES:] = dv if index == 0 else sum_ref[:, LANES:] + dv


def far_kernel(scale, kv_blocks, span_ref, q_own, q_got, d_own, d_got, stat_ref, dq_ref, *rest):
    kv_refs = rest[:kv_blocks]
    dq_own, dq_got = rest[kv_blocks : kv_blocks + 2]
    part_refs = rest[kv_blocks + 2 : 2 * kv_blocks + 2]
    keys, values, keys_t, dk_acc, dv_acc, dq_acc, before = rest[2 * kv_blocks + 2 :]
    me = lax.axis_index("ctx")
    chip, core = me // 2, me % 2
    span_of = span_finder(span_ref)
    slots = span_ref.shape[0]
    width = q_own.shape[1]
    half = kv_refs[0].shape[0] // 8

    for n in range(slots):
        before[n] = 0
    spans = [
        [span_of(chip ^ (2 * (block + 1) + part // 4), part // 2 % 2, part % 2) for part in range(8)]
        for block in range(kv_blocks)
    ]
    for line in spans:
        for span in line:
            before[span] = 1
    running = 0
    for n in range(slots):
        here = before[n]
        before[n] = running
        running = running + here

    def place(block, part):
        return pl.ds(pl.multiple_of(before[spans[block][part]] * half, half), half)

    for block in range(kv_blocks):
        for part in range(8):
            at = place(block, part)
            rows = kv_refs[block][part * half : (part + 1) * half, :]
            keys[at, :] = rows[:, :LANES]
            values[at, :] = rows[:, LANES:]
    for chunk in range(keys.shape[0] // CHUNK):
        at = slice(chunk * CHUNK, (chunk + 1) * CHUNK)
        keys_t[:, at] = keys[at, :].T
    dk_acc[...] = jnp.zeros_like(dk_acc)
    dv_acc[...] = jnp.zeros_like(dv_acc)

    for index in range(4):
        upper = index % 2
        q_ref, d_ref, out_ref, who = (q_own, d_own, dq_own, core) if index < 2 else (q_got, d_got, dq_got, 1 - core)
        line = 2 * (index // 2)
        lanes = slice(upper * width, (upper + 1) * width)
        queries = q_ref[upper]
        grads = d_ref[upper]
        norm = stat_ref[line : line + 1, lanes]
        inner = stat_ref[line + 1 : line + 2, lanes]
        dq_acc[...] = dq_ref[index]
        ahead = before[span_of(chip, who, upper)] * half

        def one(start, count, masked):
            at = pl.ds(pl.multiple_of(start, CHUNK), count)
            seen = lambda shape: start + lax.broadcasted_iota(jnp.int32, shape, 0) < ahead
            dk, dv, dq = pair_gradients(
                scale, queries, grads, norm, inner, keys[at, :], values[at, :], keys_t[:, at], seen if masked else None
            )
            dk_acc[at, :] += dk
            dv_acc[at, :] += dv
            dq_acc[...] += dq

        long = ahead // LONG * LONG
        tail = ahead // (LONG // 2) * (LONG // 2)

        @pl.when(long > 0)
        def _():
            one(0, LONG, False)

        @pl.when(tail > long)
        def _():
            one(long, LONG // 2, False)

        @pl.when(ahead - tail > CHUNK)
        def _():
            one(tail, LONG // 2, True)

        @pl.when((ahead > tail) & (ahead - tail <= CHUNK))
        def _():
            one(tail, CHUNK, True)

        out_ref[upper] = (dq_acc[...].T * scale).astype(BF16)

    for block in range(kv_blocks):
        for part in range(8):
            at = place(block, part)
            rows = slice(part * half, (part + 1) * half)
            part_refs[block][rows, :LANES] = (dk_acc[at, :] * scale).astype(BF16)
            part_refs[block][rows, LANES:] = dv_acc[at, :].astype(BF16)


def attention_near(span_order, q_own, q_got, d_own, d_got, stat_own, stat_got, kv, scale):
    count = kv.shape[0]
    halves, width, size = q_own.shape
    assert count * 2 == LONG
    return pl.pallas_call(
        functools.partial(near_kernel, scale),
        out_shape=(
            jax.ShapeDtypeStruct((2 * halves, size, width), F32),
            jax.ShapeDtypeStruct((count, 2 * LANES), F32),
            jax.ShapeDtypeStruct((4, halves * width), F32),
        ),
        in_specs=[SMEM] + [VMEM] * 7,
        out_specs=(VMEM,) * 3,
        scratch_shapes=[pltpu.VMEM((LANES, count), BF16), pltpu.VMEM((count, LANES), jnp.int32)],
        compiler_params=pltpu.CompilerParams(vmem_limit_bytes=16 * MIB),
        cost_estimate=pl.CostEstimate(
            flops=20 * halves * width * count * size,
            bytes_accessed=3 * MIB,
            transcendentals=2 * halves * width * count,
        ),
        name="attention_near",
    )(span_order, q_own, q_got, d_own, d_got, stat_own, stat_got, kv)


def attention_far(span_order, q_own, q_got, d_own, d_got, stats, dq_near, kv_list, scale):
    blocks = len(kv_list)
    rows = kv_list[0].shape[0]
    total = blocks * rows
    halves, width, size = q_own.shape
    assert total % LONG == LONG // 2
    part = jax.ShapeDtypeStruct((rows, 2 * LANES), BF16)
    return pl.pallas_call(
        functools.partial(far_kernel, scale, blocks),
        out_shape=(jax.ShapeDtypeStruct(q_own.shape, BF16),) * 2 + (part,) * blocks,
        in_specs=[SMEM] + [VMEM] * (6 + blocks),
        out_specs=(VMEM,) * (2 + blocks),
        scratch_shapes=[
            pltpu.VMEM((total, LANES), BF16),
            pltpu.VMEM((total, LANES), BF16),
            pltpu.VMEM((LANES, total), BF16),
            pltpu.VMEM((total, LANES), F32),
            pltpu.VMEM((total, LANES), F32),
            pltpu.VMEM((LANES, width), F32),
            pltpu.SMEM(span_order.shape, jnp.int32),
        ],
        compiler_params=pltpu.CompilerParams(vmem_limit_bytes=16 * MIB),
        cost_estimate=pl.CostEstimate(
            flops=20 * halves * width * total * size,
            bytes_accessed=6 * MIB,
            transcendentals=2 * halves * width * total,
        ),
        name="attention_far",
    )(span_order, q_own, q_got, d_own, d_got, stats, dq_near, *kv_list)


def slots_to_chunks(tiles, experts, blocks, chunk_ref, first):
    for expert in range(experts):
        for block in range(blocks):
            at = first + block * SLOT
            chunk_ref[expert, at : at + SLOT, :] = tiles[block, expert * SLOT : (expert + 1) * SLOT, :]


def dispatch_kernel(ids_ref, keep_ref, weight_ref, x_hbm, g_hbm, send_ref, combine_ref, x_ref, g_ref, tiles, chunks, sems):
    loads = [
        pltpu.make_async_copy(source, target, sems.at[i])
        for i, (source, target) in enumerate(((x_hbm, x_ref), (g_hbm, g_ref)))
    ]
    for load in loads:
        load.start()
    top, rows = ids_ref.shape
    experts = send_ref.shape[0]
    blocks = x_ref.shape[1] // LANES
    slots = experts * SLOT
    line = lax.broadcasted_iota(jnp.int32, (slots, rows), 0)
    expert_of = line // SLOT
    slot_of = line - expert_of * SLOT
    ids = jnp.where(keep_ref[...] == 1, ids_ref[...], -1)
    weights = weight_ref[...]
    hit = jnp.zeros((slots, rows), F32)
    weight = jnp.zeros((slots, rows), F32)
    for k in range(top):
        match = ids[k : k + 1, :] == expert_of
        hit = jnp.where(match, 1.0, hit)
        weight = jnp.where(match, weights[k : k + 1, :], weight)
    earlier = (
        lax.broadcasted_iota(jnp.int32, (rows, rows), 0)
        < lax.broadcasted_iota(jnp.int32, (rows, rows), 1)
    ).astype(F32).astype(BF16)
    rank = dot(hit.astype(BF16), earlier)
    chosen = jnp.where(rank == slot_of.astype(F32), hit, 0.0)
    combine_ref[...] = chosen * weight
    pick = chosen.astype(BF16)
    for load, source, first in ((loads[0], x_ref, 0), (loads[1], g_ref, blocks * SLOT)):
        load.wait()
        for pair in range(blocks // 2):
            both = dot(pick, source[:, pair * 2 * LANES : (pair + 1) * 2 * LANES])
            tiles[2 * pair] = both[:, :LANES]
            tiles[2 * pair + 1] = both[:, LANES:]
        slots_to_chunks(tiles, experts, blocks, chunks, first)
    send_ref[...] = chunks[...].astype(BF16)


def dispatch(ids, keep, weight, x, g, experts):
    rows = ids.shape[0]
    blocks = x.shape[1] // LANES
    slots = experts * SLOT
    return pl.pallas_call(
        dispatch_kernel,
        out_shape=(
            jax.ShapeDtypeStruct((experts, 2 * blocks * SLOT, LANES), BF16),
            jax.ShapeDtypeStruct((slots, rows), F32),
        ),
        in_specs=[VMEM] * 3 + [ANY] * 2,
        out_specs=(VMEM, VMEM),
        scratch_shapes=[
            pltpu.VMEM(x.shape, BF16),
            pltpu.VMEM(g.shape, BF16),
            pltpu.VMEM((blocks, slots, LANES), F32),
            pltpu.VMEM((experts, 2 * blocks * SLOT, LANES), F32),
            pltpu.SemaphoreType.DMA((2,)),
        ],
        compiler_params=pltpu.CompilerParams(vmem_limit_bytes=60 * MIB),
        name="dispatch",
    )(ids.T, keep.T, weight.T, x, g)


def mlp_kernel(in_ref, *rest):
    weights_hbm = rest[:3]
    out_ref = rest[3]
    weights = rest[4:7]
    chunks, tiles, x_rows, g_rows, sems = rest[7:]
    sources = in_ref.shape[0]
    blocks = x_rows.shape[1] // LANES
    hidden = weights[0].shape[1]
    tile = 256
    loads = []
    for step in range(hidden // tile):
        part = slice(step * tile, (step + 1) * tile)
        for i in range(3):
            at = (slice(None), part) if i < 2 else (part, slice(None))
            load = pltpu.make_async_copy(weights_hbm[i].at[(0,) + at], weights[i].at[at], sems.at[3 * step + i])
            load.start()
            loads.append(load)
    chunks[...] = in_ref[...].astype(F32)
    for rows_ref, first in ((x_rows, 0), (g_rows, blocks * SLOT)):
        for block in range(blocks):
            for source in range(sources):
                at = first + block * SLOT
                tiles[block, source * SLOT : (source + 1) * SLOT, :] = chunks[source, at : at + SLOT, :]
            rows_ref[:, block * LANES : (block + 1) * LANES] = tiles[block].astype(BF16)
    total = None
    for step in range(hidden // tile):
        for i in range(3):
            loads[3 * step + i].wait()
        part = slice(step * tile, (step + 1) * tile)
        gate_w, up_w = weights[0][:, part], weights[1][:, part]
        gate_pre = dot(x_rows[...], gate_w)
        up_pre = dot(x_rows[...], up_w)
        hidden_grad = dot_rows(g_rows[...], weights[2][part, :])
        sig = jax.nn.sigmoid(gate_pre)
        gate_grad = (hidden_grad * up_pre * sig * (1.0 + gate_pre * (1.0 - sig))).astype(BF16)
        up_grad = (hidden_grad * gate_pre * sig).astype(BF16)
        term = dot_rows(gate_grad, gate_w) + dot_rows(up_grad, up_w)
        for block in range(blocks):
            piece = term[:, block * LANES : (block + 1) * LANES]
            tiles[block] = piece if step == 0 else tiles[block] + piece
    slots_to_chunks(tiles, sources, blocks, chunks, 0)
    out_ref[...] = chunks[:, : blocks * SLOT, :].astype(BF16)


def mlp(received, w_gate, w_up, w_down):
    sources, chunk_rows, _ = received.shape
    _, width, hidden = w_gate.shape
    blocks = width // LANES
    slots = sources * SLOT
    return pl.pallas_call(
        mlp_kernel,
        out_shape=jax.ShapeDtypeStruct((sources, blocks * SLOT, LANES), BF16),
        in_specs=[VMEM] + [ANY] * 3,
        out_specs=VMEM,
        scratch_shapes=[
            pltpu.VMEM((width, hidden), BF16),
            pltpu.VMEM((width, hidden), BF16),
            pltpu.VMEM((hidden, width), BF16),
            pltpu.VMEM((sources, chunk_rows, LANES), F32),
            pltpu.VMEM((blocks, slots, LANES), F32),
            pltpu.VMEM((slots, width), BF16),
            pltpu.VMEM((slots, width), BF16),
            pltpu.SemaphoreType.DMA((9,)),
        ],
        compiler_params=pltpu.CompilerParams(vmem_limit_bytes=58 * MIB),
        cost_estimate=pl.CostEstimate(
            flops=10 * slots * width * hidden, bytes_accessed=11 * 1024 * 1024, transcendentals=slots * hidden
        ),
        name="experts",
    )(received, w_gate, w_up, w_down)


def combine_kernel(weight_ref, back_ref, out_ref, chunks, tiles):
    experts = back_ref.shape[0]
    blocks = out_ref.shape[1] // LANES
    chunks[...] = back_ref[...].astype(F32)
    weight = weight_ref[...].T
    high = weight.astype(BF16)
    rest = weight - high.astype(F32)
    middle = rest.astype(BF16)
    low = (rest - middle.astype(F32)).astype(BF16)
    for block in range(blocks):
        for expert in range(experts):
            at = block * SLOT
            tiles[block, expert * SLOT : (expert + 1) * SLOT, :] = chunks[expert, at : at + SLOT, :]
    for pair in range(blocks // 2):
        rows = jnp.concatenate([tiles[2 * pair], tiles[2 * pair + 1]], axis=1).astype(BF16)
        out = dot(high, rows) + (dot(middle, rows) + dot(low, rows))
        out_ref[:, pair * 2 * LANES : (pair + 1) * 2 * LANES] = out.astype(BF16)


def combine(weight, back):
    experts, chunk_rows, _ = back.shape
    slots, rows = weight.shape
    blocks = chunk_rows // SLOT
    return pl.pallas_call(
        combine_kernel,
        out_shape=jax.ShapeDtypeStruct((rows, blocks * LANES), BF16),
        in_specs=[VMEM, VMEM],
        out_specs=VMEM,
        scratch_shapes=[
            pltpu.VMEM((experts, chunk_rows, LANES), F32),
            pltpu.VMEM((blocks, slots, LANES), F32),
        ],
        compiler_params=pltpu.CompilerParams(vmem_limit_bytes=12 * MIB),
        name="combine",
    )(weight, back)


def on_device(
    queries,
    key_tensor,
    value_tensor,
    out_grad,
    log_norm,
    out_dot,
    span_order,
    moe_input,
    moe_grad,
    expert_ids,
    keep_mask,
    route_weight,
    w_gate,
    w_up,
    w_down,
):
    rows, heads, size = queries.shape
    group = heads // 2
    scale = 1.0 / math.sqrt(size)
    members = lax.axis_size("ctx")
    experts = lax.axis_size("exp")
    first = lax.axis_index("ctx") & 1 == 0
    chips = members // 2
    trade = lambda array, k: lax.ppermute(array, "ctx", [(i, i ^ k) for i in range(members)])

    send, weight = dispatch(expert_ids, keep_mask, route_weight, moe_input, moe_grad, experts)
    send, key_tensor, value_tensor = lax.optimization_barrier((send, key_tensor, value_tensor))
    kv = jnp.concatenate([key_tensor, value_tensor], axis=2)
    kv_own = jnp.where(first, kv[:, 0], kv[:, 1])
    kv_away = jnp.where(first, kv[:, 1], kv[:, 0])
    kv_got = trade(kv_away, 1)
    kv_near, kv_cross = trade(kv_own, 2), trade(kv_away, 3)
    ordered = lambda mine, other: [jnp.where(first, mine, other), jnp.where(first, other, mine)]
    kv_pair = jnp.concatenate(ordered(kv_own, kv_got) + ordered(kv_near, kv_cross), axis=0)
    received = lax.all_to_all(send, "exp", split_axis=0, concat_axis=0, tiled=True)
    kv_list = [trade(kv_pair, 4 * k) for k in range(1, chips // 2)]

    kv_near, queries, out_grad, log_norm, out_dot = lax.optimization_barrier(
        (kv_near, queries, out_grad, log_norm, out_dot)
    )

    def halves(array, axis):
        low, high = jnp.split(array, 2, axis=axis)
        return jnp.where(first, low, high), jnp.where(first, high, low)

    q_own, q_away = halves(queries, 1)
    d_own, d_away = halves(out_grad, 1)
    stat_own, stat_away = halves(jnp.stack([log_norm.T, out_dot.T]), 1)
    q_got, d_got = trade(q_away, 1), trade(d_away, 1)
    stat_got = trade(stat_away, 1)

    spans = lambda array: array.reshape(2, rows // 2 * group, size)
    shared = (span_order, spans(q_own), spans(q_got), spans(d_own), spans(d_got))
    dq_near, own_sum, stats = attention_near(
        *shared, stat_own.reshape(2 * group, rows), stat_got.reshape(2 * group, rows), kv_pair, scale
    )
    dq_own, dq_got, *parts = attention_far(*shared, stats, dq_near, kv_list, scale)
    received, _ = lax.optimization_barrier((received, parts[0]))
    slot_grad = mlp(received, w_gate, w_up, w_down)
    returned = lax.all_to_all(slot_grad, "exp", split_axis=0, concat_axis=0, tiled=True)

    total, _ = lax.optimization_barrier((own_sum, slot_grad))
    for k in range(1, chips // 2):
        total = total + trade(parts[k - 1], 4 * k).astype(F32)
    blocks = [total[i * rows : (i + 1) * rows] for i in range(4)]
    mine, near = ordered(blocks[0], blocks[1]), ordered(blocks[2], blocks[3])
    own_head = mine[0] + trade(near[0].astype(BF16), 2).astype(F32)
    other_head = trade(mine[1].astype(BF16), 1).astype(F32) + trade(near[1].astype(BF16), 3).astype(F32)
    dq_got, _ = lax.optimization_barrier((dq_got, slot_grad))
    dq_back = trade(dq_got, 1)

    def joined(own, other):
        return jnp.concatenate(ordered(own, other), axis=1)

    grad_queries = joined(dq_own.reshape(rows, group, size), dq_back.reshape(rows, group, size))
    kv_grads = joined(own_head.astype(BF16)[:, None, :], other_head.astype(BF16)[:, None, :])
    grad_moe = combine(weight, returned)
    return grad_queries, kv_grads[:, :, :size], kv_grads[:, :, size:], grad_moe


def solution(mesh):
    rows = P(("ctx", "exp"))
    in_specs = (rows,) * 6 + (P(),) + (rows,) * 5 + (P("exp"),) * 3
    return jax.shard_map(
        on_device, mesh=mesh, in_specs=in_specs, out_specs=(rows,) * 4, check_vma=False
    )
```

```python
import functools
import math

import jax
import jax.numpy as jnp
from jax import lax
from jax.experimental import pallas as pl
from jax.experimental.pallas import tpu as pltpu
from jax.sharding import PartitionSpec as P

SLOT = 10
LANES = 128
CHUNK = 256
LONG = 1024
MIB = 1024 * 1024
VMEM = pl.BlockSpec(memory_space=pltpu.VMEM)
SMEM = pl.BlockSpec(memory_space=pltpu.SMEM)
ANY = pl.BlockSpec(memory_space=pl.ANY)
F32 = jnp.float32
BF16 = jnp.bfloat16


def dot(left, right):
    return jnp.dot(left, right, preferred_element_type=F32)


def dot_rows(left, right):
    return lax.dot_general(left, right, (((1,), (1,)), ((), ())), preferred_element_type=F32)


def dot_cols(left, right):
    return lax.dot_general(left, right, (((0,), (0,)), ((), ())), preferred_element_type=F32)


def split3(array):
    high = array.astype(BF16)
    rest = array - high.astype(F32)
    middle = rest.astype(BF16)
    return high, middle, (rest - middle.astype(F32)).astype(BF16)


def span_finder(span_ref):
    slots = span_ref.shape[0]

    def span_of(chip, core, upper):
        place = chip * 2 + core
        return span_ref[slots - 1 - place if upper else place]

    return span_of


def pair_gradients(scale, queries, grads, norm, inner, keys, values, keys_t, visible):
    scores = dot_rows(keys, queries)
    probs = jnp.exp2(scores * (scale / math.log(2.0)) - norm)
    if visible is not None:
        probs = jnp.where(visible(scores.shape), probs, 0.0)
    dprobs = dot_rows(values, grads)
    dscores = (probs * (dprobs - inner)).astype(BF16)
    return dot(dscores, queries), dot(probs.astype(BF16), grads), dot(keys_t, dscores)


def near_kernel(
    scale, span_ref, q_own, q_got, d_own, d_got, stat_own, stat_got, kv_ref, dq_ref, sum_ref, stat_ref, keys_t, key_pos
):
    me = lax.axis_index("ctx")
    chip, core = me // 2, me % 2
    span_of = span_finder(span_ref)
    width = q_own.shape[1]
    count = kv_ref.shape[0]
    half = count // 8
    repeat = width // half

    stats = jnp.concatenate([stat_own[...], stat_got[...]], axis=0)
    rows = stats.shape[1]
    wide = rows * repeat
    spread = (
        lax.broadcasted_iota(jnp.int32, (rows, wide), 1) // repeat
        == lax.broadcasted_iota(jnp.int32, (rows, wide), 0)
    ).astype(F32).astype(BF16)
    high, middle, low = split3(stats)
    lanes = dot(high, spread) + (dot(middle, spread) + dot(low, spread))
    lanes = lanes.reshape(stats.shape[0] // repeat, repeat, wide)
    head = lax.broadcasted_iota(jnp.int32, lanes.shape, 1)
    lane_head = lax.broadcasted_iota(jnp.int32, lanes.shape, 2) % repeat
    lanes = jnp.sum(jnp.where(head == lane_head, lanes, 0.0), axis=1)
    is_norm = lax.broadcasted_iota(jnp.int32, lanes.shape, 0) % 2 == 0
    stat_ref[...] = jnp.where(is_norm, lanes * (1.0 / math.log(2.0)), lanes)

    keys_t[...] = kv_ref[:, :LANES].T
    for part in range(8):
        span = span_of(chip ^ (part // 4), part // 2 % 2, part % 2)
        at = slice(part * half, (part + 1) * half)
        key_pos[at, :] = span * half + lax.broadcasted_iota(jnp.int32, (half, LANES), 0)

    for index in range(4):
        upper = index % 2
        q_ref, d_ref, who = (q_own, d_own, core) if index < 2 else (q_got, d_got, 1 - core)
        line = 2 * (index // 2)
        span = span_of(chip, who, upper)

        def visible(shape):
            query_pos = span * half + lax.broadcasted_iota(jnp.int32, shape, 1) // repeat
            return jnp.concatenate([key_pos[...]] * (width // LANES), axis=1) <= query_pos

        at = slice(upper * width, (upper + 1) * width)
        dk, dv, dq = pair_gradients(
            scale,
            q_ref[upper],
            d_ref[upper],
            stat_ref[line : line + 1, at],
            stat_ref[line + 1 : line + 2, at],
            kv_ref[:, :LANES],
            kv_ref[:, LANES:],
            keys_t[...],
            visible,
        )
        dq_ref[index] = dq
        dk = dk * scale
        sum_ref[:, :LANES] = dk if index == 0 else sum_ref[:, :LANES] + dk
        sum_ref[:, LANES:] = dv if index == 0 else sum_ref[:, LANES:] + dv


def far_kernel(scale, kv_blocks, span_ref, q_own, q_got, d_own, d_got, stat_ref, dq_ref, *rest):
    kv_refs = rest[:kv_blocks]
    dq_own, dq_got = rest[kv_blocks : kv_blocks + 2]
    part_refs = rest[kv_blocks + 2 : 2 * kv_blocks + 2]
    keys, values, keys_t, dk_acc, dv_acc, dq_acc, before = rest[2 * kv_blocks + 2 :]
    me = lax.axis_index("ctx")
    chip, core = me // 2, me % 2
    span_of = span_finder(span_ref)
    slots = span_ref.shape[0]
    width = q_own.shape[1]
    half = kv_refs[0].shape[0] // 8

    for n in range(slots):
        before[n] = 0
    spans = [
        [span_of(chip ^ (2 * (block + 1) + part // 4), part // 2 % 2, part % 2) for part in range(8)]
        for block in range(kv_blocks)
    ]
    for line in spans:
        for span in line:
            before[span] = 1
    running = 0
    for n in range(slots):
        here = before[n]
        before[n] = running
        running = running + here

    def place(block, part):
        return pl.ds(pl.multiple_of(before[spans[block][part]] * half, half), half)

    for block in range(kv_blocks):
        for part in range(8):
            at = place(block, part)
            rows = kv_refs[block][part * half : (part + 1) * half, :]
            keys[at, :] = rows[:, :LANES]
            values[at, :] = rows[:, LANES:]
    for chunk in range(keys.shape[0] // CHUNK):
        at = slice(chunk * CHUNK, (chunk + 1) * CHUNK)
        keys_t[:, at] = keys[at, :].T
    dk_acc[...] = jnp.zeros_like(dk_acc)
    dv_acc[...] = jnp.zeros_like(dv_acc)

    for index in range(4):
        upper = index % 2
        q_ref, d_ref, out_ref, who = (q_own, d_own, dq_own, core) if index < 2 else (q_got, d_got, dq_got, 1 - core)
        line = 2 * (index // 2)
        lanes = slice(upper * width, (upper + 1) * width)
        queries = q_ref[upper]
        grads = d_ref[upper]
        norm = stat_ref[line : line + 1, lanes]
        inner = stat_ref[line + 1 : line + 2, lanes]
        dq_acc[...] = dq_ref[index]
        ahead = before[span_of(chip, who, upper)] * half

        def one(start, count, masked):
            at = pl.ds(pl.multiple_of(start, CHUNK), count)
            seen = lambda shape: start + lax.broadcasted_iota(jnp.int32, shape, 0) < ahead
            dk, dv, dq = pair_gradients(
                scale, queries, grads, norm, inner, keys[at, :], values[at, :], keys_t[:, at], seen if masked else None
            )
            dk_acc[at, :] += dk
            dv_acc[at, :] += dv
            dq_acc[...] += dq

        long = ahead // LONG * LONG
        tail = ahead // (LONG // 2) * (LONG // 2)

        @pl.when(long > 0)
        def _():
            one(0, LONG, False)

        @pl.when(tail > long)
        def _():
            one(long, LONG // 2, False)

        @pl.when(ahead - tail > CHUNK)
        def _():
            one(tail, LONG // 2, True)

        @pl.when((ahead > tail) & (ahead - tail <= CHUNK))
        def _():
            one(tail, CHUNK, True)

        out_ref[upper] = (dq_acc[...].T * scale).astype(BF16)

    for block in range(kv_blocks):
        for part in range(8):
            at = place(block, part)
            rows = slice(part * half, (part + 1) * half)
            part_refs[block][rows, :LANES] = (dk_acc[at, :] * scale).astype(BF16)
            part_refs[block][rows, LANES:] = dv_acc[at, :].astype(BF16)


def attention_near(span_order, q_own, q_got, d_own, d_got, stat_own, stat_got, kv, scale):
    count = kv.shape[0]
    halves, width, size = q_own.shape
    assert count * 2 == LONG
    return pl.pallas_call(
        functools.partial(near_kernel, scale),
        out_shape=(
            jax.ShapeDtypeStruct((2 * halves, size, width), F32),
            jax.ShapeDtypeStruct((count, 2 * LANES), F32),
            jax.ShapeDtypeStruct((4, halves * width), F32),
        ),
        in_specs=[SMEM] + [VMEM] * 7,
        out_specs=(VMEM,) * 3,
        scratch_shapes=[pltpu.VMEM((LANES, count), BF16), pltpu.VMEM((count, LANES), jnp.int32)],
        compiler_params=pltpu.CompilerParams(vmem_limit_bytes=16 * MIB),
        cost_estimate=pl.CostEstimate(
            flops=20 * halves * width * count * size,
            bytes_accessed=3 * MIB,
            transcendentals=2 * halves * width * count,
        ),
        name="attention_near",
    )(span_order, q_own, q_got, d_own, d_got, stat_own, stat_got, kv)


def attention_far(span_order, q_own, q_got, d_own, d_got, stats, dq_near, kv_list, scale):
    blocks = len(kv_list)
    rows = kv_list[0].shape[0]
    total = blocks * rows
    halves, width, size = q_own.shape
    assert total % LONG == LONG // 2
    part = jax.ShapeDtypeStruct((rows, 2 * LANES), BF16)
    return pl.pallas_call(
        functools.partial(far_kernel, scale, blocks),
        out_shape=(jax.ShapeDtypeStruct(q_own.shape, BF16),) * 2 + (part,) * blocks,
        in_specs=[SMEM] + [VMEM] * (6 + blocks),
        out_specs=(VMEM,) * (2 + blocks),
        scratch_shapes=[
            pltpu.VMEM((total, LANES), BF16),
            pltpu.VMEM((total, LANES), BF16),
            pltpu.VMEM((LANES, total), BF16),
            pltpu.VMEM((total, LANES), F32),
            pltpu.VMEM((total, LANES), F32),
            pltpu.VMEM((LANES, width), F32),
            pltpu.SMEM(span_order.shape, jnp.int32),
        ],
        compiler_params=pltpu.CompilerParams(vmem_limit_bytes=16 * MIB),
        cost_estimate=pl.CostEstimate(
            flops=20 * halves * width * total * size,
            bytes_accessed=6 * MIB,
            transcendentals=2 * halves * width * total,
        ),
        name="attention_far",
    )(span_order, q_own, q_got, d_own, d_got, stats, dq_near, *kv_list)


def slots_to_chunks(tiles, experts, blocks, chunk_ref, first):
    for expert in range(experts):
        for block in range(blocks):
            at = first + block * SLOT
            chunk_ref[expert, at : at + SLOT, :] = tiles[block, expert * SLOT : (expert + 1) * SLOT, :]


def dispatch_kernel(ids_ref, keep_ref, weight_ref, x_hbm, g_hbm, send_ref, combine_ref, x_ref, g_ref, tiles, chunks, sems):
    loads = [
        pltpu.make_async_copy(source, target, sems.at[i])
        for i, (source, target) in enumerate(((x_hbm, x_ref), (g_hbm, g_ref)))
    ]
    for load in loads:
        load.start()
    top, rows = ids_ref.shape
    experts = send_ref.shape[0]
    blocks = x_ref.shape[1] // LANES
    slots = experts * SLOT
    line = lax.broadcasted_iota(jnp.int32, (slots, rows), 0)
    expert_of = line // SLOT
    slot_of = line - expert_of * SLOT
    ids = jnp.where(keep_ref[...] == 1, ids_ref[...], -1)
    weights = weight_ref[...]
    hit = jnp.zeros((slots, rows), F32)
    weight = jnp.zeros((slots, rows), F32)
    for k in range(top):
        match = ids[k : k + 1, :] == expert_of
        hit = jnp.where(match, 1.0, hit)
        weight = jnp.where(match, weights[k : k + 1, :], weight)
    earlier = (
        lax.broadcasted_iota(jnp.int32, (rows, rows), 0)
        < lax.broadcasted_iota(jnp.int32, (rows, rows), 1)
    ).astype(F32).astype(BF16)
    rank = dot(hit.astype(BF16), earlier)
    chosen = jnp.where(rank == slot_of.astype(F32), hit, 0.0)
    combine_ref[...] = chosen * weight
    pick = chosen.astype(BF16)
    for load, source, first in ((loads[0], x_ref, 0), (loads[1], g_ref, blocks * SLOT)):
        load.wait()
        for pair in range(blocks // 2):
            both = dot(pick, source[:, pair * 2 * LANES : (pair + 1) * 2 * LANES])
            tiles[2 * pair] = both[:, :LANES]
            tiles[2 * pair + 1] = both[:, LANES:]
        slots_to_chunks(tiles, experts, blocks, chunks, first)
    send_ref[...] = chunks[...].astype(BF16)


def dispatch(ids, keep, weight, x, g, experts):
    rows = ids.shape[0]
    blocks = x.shape[1] // LANES
    slots = experts * SLOT
    return pl.pallas_call(
        dispatch_kernel,
        out_shape=(
            jax.ShapeDtypeStruct((experts, 2 * blocks * SLOT, LANES), BF16),
            jax.ShapeDtypeStruct((slots, rows), F32),
        ),
        in_specs=[VMEM] * 3 + [ANY] * 2,
        out_specs=(VMEM, VMEM),
        scratch_shapes=[
            pltpu.VMEM(x.shape, BF16),
            pltpu.VMEM(g.shape, BF16),
            pltpu.VMEM((blocks, slots, LANES), F32),
            pltpu.VMEM((experts, 2 * blocks * SLOT, LANES), F32),
            pltpu.SemaphoreType.DMA((2,)),
        ],
        compiler_params=pltpu.CompilerParams(vmem_limit_bytes=60 * MIB),
        name="dispatch",
    )(ids.T, keep.T, weight.T, x, g)


def mlp_kernel(in_ref, *rest):
    weights_hbm = rest[:3]
    out_ref = rest[3]
    weights = rest[4:7]
    chunks, tiles, x_rows, g_rows, sems = rest[7:]
    sources = in_ref.shape[0]
    blocks = x_rows.shape[1] // LANES
    hidden = weights[0].shape[1]
    tile = 256
    loads = []
    for step in range(hidden // tile):
        part = slice(step * tile, (step + 1) * tile)
        for i in range(3):
            at = (slice(None), part) if i < 2 else (part, slice(None))
            load = pltpu.make_async_copy(weights_hbm[i].at[(0,) + at], weights[i].at[at], sems.at[3 * step + i])
            load.start()
            loads.append(load)
    chunks[...] = in_ref[...].astype(F32)
    for rows_ref, first in ((x_rows, 0), (g_rows, blocks * SLOT)):
        for block in range(blocks):
            for source in range(sources):
                at = first + block * SLOT
                tiles[block, source * SLOT : (source + 1) * SLOT, :] = chunks[source, at : at + SLOT, :]
            rows_ref[:, block * LANES : (block + 1) * LANES] = tiles[block].astype(BF16)
    total = None
    for step in range(hidden // tile):
        for i in range(3):
            loads[3 * step + i].wait()
        part = slice(step * tile, (step + 1) * tile)
        gate_w, up_w = weights[0][:, part], weights[1][:, part]
        gate_pre = dot(x_rows[...], gate_w)
        up_pre = dot(x_rows[...], up_w)
        hidden_grad = dot_rows(g_rows[...], weights[2][part, :])
        sig = jax.nn.sigmoid(gate_pre)
        gate_grad = (hidden_grad * up_pre * sig * (1.0 + gate_pre * (1.0 - sig))).astype(BF16)
        up_grad = (hidden_grad * gate_pre * sig).astype(BF16)
        term = dot_rows(gate_grad, gate_w) + dot_rows(up_grad, up_w)
        for block in range(blocks):
            piece = term[:, block * LANES : (block + 1) * LANES]
            tiles[block] = piece if step == 0 else tiles[block] + piece
    slots_to_chunks(tiles, sources, blocks, chunks, 0)
    out_ref[...] = chunks[:, : blocks * SLOT, :].astype(BF16)


def mlp(received, w_gate, w_up, w_down):
    sources, chunk_rows, _ = received.shape
    _, width, hidden = w_gate.shape
    blocks = width // LANES
    slots = sources * SLOT
    return pl.pallas_call(
        mlp_kernel,
        out_shape=jax.ShapeDtypeStruct((sources, blocks * SLOT, LANES), BF16),
        in_specs=[VMEM] + [ANY] * 3,
        out_specs=VMEM,
        scratch_shapes=[
            pltpu.VMEM((width, hidden), BF16),
            pltpu.VMEM((width, hidden), BF16),
            pltpu.VMEM((hidden, width), BF16),
            pltpu.VMEM((sources, chunk_rows, LANES), F32),
            pltpu.VMEM((blocks, slots, LANES), F32),
            pltpu.VMEM((slots, width), BF16),
            pltpu.VMEM((slots, width), BF16),
            pltpu.SemaphoreType.DMA((9,)),
        ],
        compiler_params=pltpu.CompilerParams(vmem_limit_bytes=58 * MIB),
        cost_estimate=pl.CostEstimate(
            flops=10 * slots * width * hidden, bytes_accessed=11 * 1024 * 1024, transcendentals=slots * hidden
        ),
        name="experts",
    )(received, w_gate, w_up, w_down)


def combine_kernel(weight_ref, back_ref, out_ref, chunks, tiles):
    experts = back_ref.shape[0]
    blocks = out_ref.shape[1] // LANES
    chunks[...] = back_ref[...].astype(F32)
    weight = weight_ref[...].T
    high = weight.astype(BF16)
    rest = weight - high.astype(F32)
    middle = rest.astype(BF16)
    low = (rest - middle.astype(F32)).astype(BF16)
    for block in range(blocks):
        for expert in range(experts):
            at = block * SLOT
            tiles[block, expert * SLOT : (expert + 1) * SLOT, :] = chunks[expert, at : at + SLOT, :]
    for pair in range(blocks // 2):
        rows = jnp.concatenate([tiles[2 * pair], tiles[2 * pair + 1]], axis=1).astype(BF16)
        out = dot(high, rows) + (dot(middle, rows) + dot(low, rows))
        out_ref[:, pair * 2 * LANES : (pair + 1) * 2 * LANES] = out.astype(BF16)


def combine(weight, back):
    experts, chunk_rows, _ = back.shape
    slots, rows = weight.shape
    blocks = chunk_rows // SLOT
    return pl.pallas_call(
        combine_kernel,
        out_shape=jax.ShapeDtypeStruct((rows, blocks * LANES), BF16),
        in_specs=[VMEM, VMEM],
        out_specs=VMEM,
        scratch_shapes=[
            pltpu.VMEM((experts, chunk_rows, LANES), F32),
            pltpu.VMEM((blocks, slots, LANES), F32),
        ],
        compiler_params=pltpu.CompilerParams(vmem_limit_bytes=12 * MIB),
        name="combine",
    )(weight, back)


def on_device(
    queries,
    key_tensor,
    value_tensor,
    out_grad,
    log_norm,
    out_dot,
    span_order,
    moe_input,
    moe_grad,
    expert_ids,
    keep_mask,
    route_weight,
    w_gate,
    w_up,
    w_down,
):
    rows, heads, size = queries.shape
    group = heads // 2
    scale = 1.0 / math.sqrt(size)
    members = lax.axis_size("ctx")
    experts = lax.axis_size("exp")
    first = lax.axis_index("ctx") & 1 == 0
    chips = members // 2
    trade = lambda array, k: lax.ppermute(array, "ctx", [(i, i ^ k) for i in range(members)])

    kv = jnp.concatenate([key_tensor, value_tensor], axis=2)
    kv_own = jnp.where(first, kv[:, 0], kv[:, 1])
    kv_away = jnp.where(first, kv[:, 1], kv[:, 0])
    kv_own, kv_away, expert_ids = lax.optimization_barrier((kv_own, kv_away, expert_ids))
    kv_got = trade(kv_away, 1)
    kv_near, kv_cross = trade(kv_own, 2), trade(kv_away, 3)
    send, weight = dispatch(expert_ids, keep_mask, route_weight, moe_input, moe_grad, experts)
    ordered = lambda mine, other: [jnp.where(first, mine, other), jnp.where(first, other, mine)]
    kv_pair = jnp.concatenate(ordered(kv_own, kv_got) + ordered(kv_near, kv_cross), axis=0)
    send, kv_pair = lax.optimization_barrier((send, kv_pair))
    received = lax.all_to_all(send, "exp", split_axis=0, concat_axis=0, tiled=True)
    kv_list = [trade(kv_pair, 4 * k) for k in range(1, chips // 2)]

    kv_near, queries, out_grad, log_norm, out_dot = lax.optimization_barrier(
        (kv_near, queries, out_grad, log_norm, out_dot)
    )

    def halves(array, axis):
        low, high = jnp.split(array, 2, axis=axis)
        return jnp.where(first, low, high), jnp.where(first, high, low)

    q_own, q_away = halves(queries, 1)
    d_own, d_away = halves(out_grad, 1)
    stat_own, stat_away = halves(jnp.stack([log_norm.T, out_dot.T]), 1)
    q_got, d_got = trade(q_away, 1), trade(d_away, 1)
    stat_got = trade(stat_away, 1)

    spans = lambda array: array.reshape(2, rows // 2 * group, size)
    shared = (span_order, spans(q_own), spans(q_got), spans(d_own), spans(d_got))
    dq_near, own_sum, stats = attention_near(
        *shared, stat_own.reshape(2 * group, rows), stat_got.reshape(2 * group, rows), kv_pair, scale
    )
    dq_own, dq_got, *parts = attention_far(*shared, stats, dq_near, kv_list, scale)
    received, _ = lax.optimization_barrier((received, parts[0]))
    slot_grad = mlp(received, w_gate, w_up, w_down)
    returned = lax.all_to_all(slot_grad, "exp", split_axis=0, concat_axis=0, tiled=True)

    total, _ = lax.optimization_barrier((own_sum, slot_grad))
    for k in range(1, chips // 2):
        total = total + trade(parts[k - 1], 4 * k).astype(F32)
    blocks = [total[i * rows : (i + 1) * rows] for i in range(4)]
    mine, near = ordered(blocks[0], blocks[1]), ordered(blocks[2], blocks[3])
    own_head = mine[0] + trade(near[0].astype(BF16), 2).astype(F32)
    other_head = trade(mine[1].astype(BF16), 1).astype(F32) + trade(near[1].astype(BF16), 3).astype(F32)
    dq_got, _ = lax.optimization_barrier((dq_got, slot_grad))
    dq_back = trade(dq_got, 1)

    def joined(own, other):
        return jnp.concatenate(ordered(own, other), axis=1)

    grad_queries = joined(dq_own.reshape(rows, group, size), dq_back.reshape(rows, group, size))
    kv_grads = joined(own_head.astype(BF16)[:, None, :], other_head.astype(BF16)[:, None, :])
    grad_moe = combine(weight, returned)
    return grad_queries, kv_grads[:, :, :size], kv_grads[:, :, size:], grad_moe


def solution(mesh):
    rows = P(("ctx", "exp"))
    in_specs = (rows,) * 6 + (P(),) + (rows,) * 5 + (P("exp"),) * 3
    return jax.shard_map(
        on_device, mesh=mesh, in_specs=in_specs, out_specs=(rows,) * 4, check_vma=False
    )
```

```python
import functools
import math

import jax
import jax.numpy as jnp
from jax import lax
from jax.experimental import pallas as pl
from jax.experimental.pallas import tpu as pltpu
from jax.sharding import PartitionSpec as P

SLOT = 10
LANES = 128
CHUNK = 256
LONG = 1024
MIB = 1024 * 1024
VMEM = pl.BlockSpec(memory_space=pltpu.VMEM)
SMEM = pl.BlockSpec(memory_space=pltpu.SMEM)
ANY = pl.BlockSpec(memory_space=pl.ANY)
F32 = jnp.float32
BF16 = jnp.bfloat16


def dot(left, right):
    return jnp.dot(left, right, preferred_element_type=F32)


def dot_rows(left, right):
    return lax.dot_general(left, right, (((1,), (1,)), ((), ())), preferred_element_type=F32)


def dot_cols(left, right):
    return lax.dot_general(left, right, (((0,), (0,)), ((), ())), preferred_element_type=F32)


def split3(array):
    high = array.astype(BF16)
    rest = array - high.astype(F32)
    middle = rest.astype(BF16)
    return high, middle, (rest - middle.astype(F32)).astype(BF16)


def span_finder(span_ref):
    slots = span_ref.shape[0]

    def span_of(chip, core, upper):
        place = chip * 2 + core
        return span_ref[slots - 1 - place if upper else place]

    return span_of


def pair_gradients(scale, queries, grads, norm, inner, keys, values, keys_t, visible):
    scores = dot_rows(keys, queries)
    probs = jnp.exp2(scores * (scale / math.log(2.0)) - norm)
    if visible is not None:
        probs = jnp.where(visible(scores.shape), probs, 0.0)
    dprobs = dot_rows(values, grads)
    dscores = (probs * (dprobs - inner)).astype(BF16)
    return dot(dscores, queries), dot(probs.astype(BF16), grads), dot(keys_t, dscores)


def near_kernel(
    scale, span_ref, q_own, q_got, d_own, d_got, stat_own, stat_got, kv_ref, dq_ref, sum_ref, stat_ref, keys, values, keys_t, key_pos
):
    me = lax.axis_index("ctx")
    chip, core = me // 2, me % 2
    span_of = span_finder(span_ref)
    width = q_own.shape[1]
    count = kv_ref.shape[0] // 2
    half = count // 8
    repeat = width // half

    stats = jnp.concatenate([stat_own[...], stat_got[...]], axis=0)
    rows = stats.shape[1]
    wide = rows * repeat
    spread = (
        lax.broadcasted_iota(jnp.int32, (rows, wide), 1) // repeat
        == lax.broadcasted_iota(jnp.int32, (rows, wide), 0)
    ).astype(F32).astype(BF16)
    high, middle, low = split3(stats)
    lanes = dot(high, spread) + (dot(middle, spread) + dot(low, spread))
    lanes = lanes.reshape(stats.shape[0] // repeat, repeat, wide)
    head = lax.broadcasted_iota(jnp.int32, lanes.shape, 1)
    lane_head = lax.broadcasted_iota(jnp.int32, lanes.shape, 2) % repeat
    lanes = jnp.sum(jnp.where(head == lane_head, lanes, 0.0), axis=1)
    is_norm = lax.broadcasted_iota(jnp.int32, lanes.shape, 0) % 2 == 0
    stat_ref[...] = jnp.where(is_norm, lanes * (1.0 / math.log(2.0)), lanes)

    for device in range(4):
        at = slice(device * 2 * half, (device + 1) * 2 * half)
        keys[at, :] = kv_ref[device * 4 * half : device * 4 * half + 2 * half, :]
        values[at, :] = kv_ref[device * 4 * half + 2 * half : (device + 1) * 4 * half, :]
    keys_t[...] = keys[...].T
    for part in range(8):
        span = span_of(chip ^ (part // 4), part // 2 % 2, part % 2)
        at = slice(part * half, (part + 1) * half)
        key_pos[at, :] = span * half + lax.broadcasted_iota(jnp.int32, (half, LANES), 0)

    for index in range(4):
        upper = index % 2
        q_ref, d_ref, who = (q_own, d_own, core) if index < 2 else (q_got, d_got, 1 - core)
        line = 2 * (index // 2)
        span = span_of(chip, who, upper)

        def visible(shape):
            query_pos = span * half + lax.broadcasted_iota(jnp.int32, shape, 1) // repeat
            return jnp.concatenate([key_pos[...]] * (width // LANES), axis=1) <= query_pos

        at = slice(upper * width, (upper + 1) * width)
        dk, dv, dq = pair_gradients(
            scale,
            q_ref[upper],
            d_ref[upper],
            stat_ref[line : line + 1, at],
            stat_ref[line + 1 : line + 2, at],
            keys[...],
            values[...],
            keys_t[...],
            visible,
        )
        dq_ref[index] = dq
        dk = dk * scale
        sum_ref[:, :LANES] = dk if index == 0 else sum_ref[:, :LANES] + dk
        sum_ref[:, LANES:] = dv if index == 0 else sum_ref[:, LANES:] + dv


def far_kernel(scale, kv_blocks, span_ref, q_own, q_got, d_own, d_got, stat_ref, dq_ref, *rest):
    kv_refs = rest[:kv_blocks]
    dq_own, dq_got = rest[kv_blocks : kv_blocks + 2]
    part_refs = rest[kv_blocks + 2 : 2 * kv_blocks + 2]
    keys, values, keys_t, dk_acc, dv_acc, dq_acc, before = rest[2 * kv_blocks + 2 :]
    me = lax.axis_index("ctx")
    chip, core = me // 2, me % 2
    span_of = span_finder(span_ref)
    slots = span_ref.shape[0]
    width = q_own.shape[1]
    half = kv_refs[0].shape[0] // 16

    for n in range(slots):
        before[n] = 0
    spans = [
        [span_of(chip ^ (2 * (block + 1) + part // 4), part // 2 % 2, part % 2) for part in range(8)]
        for block in range(kv_blocks)
    ]
    for line in spans:
        for span in line:
            before[span] = 1
    running = 0
    for n in range(slots):
        here = before[n]
        before[n] = running
        running = running + here

    def place(block, part):
        return pl.ds(pl.multiple_of(before[spans[block][part]] * half, half), half)

    for block in range(kv_blocks):
        for part in range(8):
            at = place(block, part)
            first = (part // 2 * 4 + part % 2) * half
            keys[at, :] = kv_refs[block][first : first + half, :]
            values[at, :] = kv_refs[block][first + 2 * half : first + 3 * half, :]
    for chunk in range(keys.shape[0] // CHUNK):
        at = slice(chunk * CHUNK, (chunk + 1) * CHUNK)
        keys_t[:, at] = keys[at, :].T
    dk_acc[...] = jnp.zeros_like(dk_acc)
    dv_acc[...] = jnp.zeros_like(dv_acc)

    for index in range(4):
        upper = index % 2
        q_ref, d_ref, out_ref, who = (q_own, d_own, dq_own, core) if index < 2 else (q_got, d_got, dq_got, 1 - core)
        line = 2 * (index // 2)
        lanes = slice(upper * width, (upper + 1) * width)
        queries = q_ref[upper]
        grads = d_ref[upper]
        norm = stat_ref[line : line + 1, lanes]
        inner = stat_ref[line + 1 : line + 2, lanes]
        dq_acc[...] = dq_ref[index]
        ahead = before[span_of(chip, who, upper)] * half

        def one(start, count, masked):
            at = pl.ds(pl.multiple_of(start, CHUNK), count)
            seen = lambda shape: start + lax.broadcasted_iota(jnp.int32, shape, 0) < ahead
            dk, dv, dq = pair_gradients(
                scale, queries, grads, norm, inner, keys[at, :], values[at, :], keys_t[:, at], seen if masked else None
            )
            dk_acc[at, :] += dk
            dv_acc[at, :] += dv
            dq_acc[...] += dq

        long = ahead // LONG * LONG
        tail = ahead // (LONG // 2) * (LONG // 2)

        @pl.when(long > 0)
        def _():
            one(0, LONG, False)

        @pl.when(tail > long)
        def _():
            one(long, LONG // 2, False)

        @pl.when(ahead - tail > CHUNK)
        def _():
            one(tail, LONG // 2, True)

        @pl.when((ahead > tail) & (ahead - tail <= CHUNK))
        def _():
            one(tail, CHUNK, True)

        out_ref[upper] = (dq_acc[...].T * scale).astype(BF16)

    for block in range(kv_blocks):
        for part in range(8):
            at = place(block, part)
            rows = slice(part * half, (part + 1) * half)
            part_refs[block][rows, :LANES] = (dk_acc[at, :] * scale).astype(BF16)
            part_refs[block][rows, LANES:] = dv_acc[at, :].astype(BF16)


def attention_near(span_order, q_own, q_got, d_own, d_got, stat_own, stat_got, kv, scale):
    count = kv.shape[0] // 2
    halves, width, size = q_own.shape
    assert count * 2 == LONG
    return pl.pallas_call(
        functools.partial(near_kernel, scale),
        out_shape=(
            jax.ShapeDtypeStruct((2 * halves, size, width), F32),
            jax.ShapeDtypeStruct((count, 2 * LANES), F32),
            jax.ShapeDtypeStruct((4, halves * width), F32),
        ),
        in_specs=[SMEM] + [VMEM] * 7,
        out_specs=(VMEM,) * 3,
        scratch_shapes=[
            pltpu.VMEM((count, LANES), BF16),
            pltpu.VMEM((count, LANES), BF16),
            pltpu.VMEM((LANES, count), BF16),
            pltpu.VMEM((count, LANES), jnp.int32),
        ],
        compiler_params=pltpu.CompilerParams(vmem_limit_bytes=16 * MIB),
        cost_estimate=pl.CostEstimate(
            flops=20 * halves * width * count * size,
            bytes_accessed=3 * MIB,
            transcendentals=2 * halves * width * count,
        ),
        name="attention_near",
    )(span_order, q_own, q_got, d_own, d_got, stat_own, stat_got, kv)


def attention_far(span_order, q_own, q_got, d_own, d_got, stats, dq_near, kv_list, scale):
    blocks = len(kv_list)
    rows = kv_list[0].shape[0] // 2
    total = blocks * rows
    halves, width, size = q_own.shape
    assert total % LONG == LONG // 2
    part = jax.ShapeDtypeStruct((rows, 2 * LANES), BF16)
    return pl.pallas_call(
        functools.partial(far_kernel, scale, blocks),
        out_shape=(jax.ShapeDtypeStruct(q_own.shape, BF16),) * 2 + (part,) * blocks,
        in_specs=[SMEM] + [VMEM] * (6 + blocks),
        out_specs=(VMEM,) * (2 + blocks),
        scratch_shapes=[
            pltpu.VMEM((total, LANES), BF16),
            pltpu.VMEM((total, LANES), BF16),
            pltpu.VMEM((LANES, total), BF16),
            pltpu.VMEM((total, LANES), F32),
            pltpu.VMEM((total, LANES), F32),
            pltpu.VMEM((LANES, width), F32),
            pltpu.SMEM(span_order.shape, jnp.int32),
        ],
        compiler_params=pltpu.CompilerParams(vmem_limit_bytes=16 * MIB),
        cost_estimate=pl.CostEstimate(
            flops=20 * halves * width * total * size,
            bytes_accessed=6 * MIB,
            transcendentals=2 * halves * width * total,
        ),
        name="attention_far",
    )(span_order, q_own, q_got, d_own, d_got, stats, dq_near, *kv_list)


def slots_to_chunks(tiles, experts, blocks, chunk_ref, first):
    for expert in range(experts):
        for block in range(blocks):
            at = first + block * SLOT
            chunk_ref[expert, at : at + SLOT, :] = tiles[block, expert * SLOT : (expert + 1) * SLOT, :]


def dispatch_kernel(*refs):
    sources, (send_ref, combine_ref), targets, (tiles, chunks, sems) = refs[:5], refs[5:7], refs[7:12], refs[12:]
    ids_ref, keep_ref, weight_ref, x_ref, g_ref = targets
    loads = [pltpu.make_async_copy(*pair, sems.at[i]) for i, pair in enumerate(zip(sources, targets))]
    for load in loads:
        load.start()
    for load in loads[:3]:
        load.wait()
    top, rows = ids_ref.shape
    experts = send_ref.shape[0]
    blocks = x_ref.shape[1] // LANES
    slots = experts * SLOT
    line = lax.broadcasted_iota(jnp.int32, (slots, rows), 0)
    expert_of = line // SLOT
    slot_of = line - expert_of * SLOT
    ids = jnp.where(keep_ref[...] == 1, ids_ref[...], -1)
    weights = weight_ref[...]
    hit = jnp.zeros((slots, rows), F32)
    weight = jnp.zeros((slots, rows), F32)
    for k in range(top):
        match = ids[k : k + 1, :] == expert_of
        hit = jnp.where(match, 1.0, hit)
        weight = jnp.where(match, weights[k : k + 1, :], weight)
    earlier = (
        lax.broadcasted_iota(jnp.int32, (rows, rows), 0)
        < lax.broadcasted_iota(jnp.int32, (rows, rows), 1)
    ).astype(F32).astype(BF16)
    rank = dot(hit.astype(BF16), earlier)
    chosen = jnp.where(rank == slot_of.astype(F32), hit, 0.0)
    combine_ref[...] = chosen * weight
    pick = chosen.astype(BF16)
    for load, source, first in ((loads[3], x_ref, 0), (loads[4], g_ref, blocks * SLOT)):
        load.wait()
        for pair in range(blocks // 2):
            both = dot(pick, source[:, pair * 2 * LANES : (pair + 1) * 2 * LANES])
            tiles[2 * pair] = both[:, :LANES]
            tiles[2 * pair + 1] = both[:, LANES:]
        slots_to_chunks(tiles, experts, blocks, chunks, first)
    send_ref[...] = chunks[...].astype(BF16)


def dispatch(ids, keep, weight, x, g, experts):
    rows = ids.shape[0]
    blocks = x.shape[1] // LANES
    slots = experts * SLOT
    return pl.pallas_call(
        dispatch_kernel,
        out_shape=(
            jax.ShapeDtypeStruct((experts, 2 * blocks * SLOT, LANES), BF16),
            jax.ShapeDtypeStruct((slots, rows), F32),
        ),
        in_specs=[ANY] * 5,
        out_specs=(VMEM, VMEM),
        scratch_shapes=[
            pltpu.VMEM(ids.T.shape, ids.dtype),
            pltpu.VMEM(ids.T.shape, keep.dtype),
            pltpu.VMEM(ids.T.shape, weight.dtype),
            pltpu.VMEM(x.shape, BF16),
            pltpu.VMEM(g.shape, BF16),
            pltpu.VMEM((blocks, slots, LANES), F32),
            pltpu.VMEM((experts, 2 * blocks * SLOT, LANES), F32),
            pltpu.SemaphoreType.DMA((5,)),
        ],
        compiler_params=pltpu.CompilerParams(vmem_limit_bytes=60 * MIB),
        name="dispatch",
    )(ids.T, keep.T, weight.T, x, g)


def mlp_kernel(in_ref, *rest):
    weights_hbm = rest[:3]
    out_ref = rest[3]
    weights = rest[4:7]
    chunks, tiles, x_rows, g_rows, sems = rest[7:]
    sources = in_ref.shape[0]
    blocks = x_rows.shape[1] // LANES
    hidden = weights[0].shape[1]
    tile = 256
    loads = []
    edges = [0, tile // 2, hidden // 2, hidden]
    parts = [slice(low, high) for low, high in zip(edges, edges[1:])]
    for step, part in enumerate(parts):
        for i in range(3):
            at = (slice(None), part) if i < 2 else (part, slice(None))
            load = pltpu.make_async_copy(weights_hbm[i].at[(0,) + at], weights[i].at[at], sems.at[3 * step + i])
            loads.append(load)
    for load in loads[:3]:
        load.start()
    chunks[...] = in_ref[...].astype(F32)
    for rows_ref, first in ((x_rows, 0), (g_rows, blocks * SLOT)):
        for block in range(blocks):
            for source in range(sources):
                at = first + block * SLOT
                tiles[block, source * SLOT : (source + 1) * SLOT, :] = chunks[source, at : at + SLOT, :]
            rows_ref[:, block * LANES : (block + 1) * LANES] = tiles[block].astype(BF16)
    for load in loads[3:]:
        load.start()

    def back(part, gate_grad, up_grad, fresh):
        term = dot_rows(gate_grad, weights[0][:, part]) + dot_rows(up_grad, weights[1][:, part])
        for block in range(blocks):
            piece = term[:, block * LANES : (block + 1) * LANES]
            tiles[block] = piece if fresh else tiles[block] + piece

    waiting = None
    for step, part in enumerate(parts):
        for i in range(3):
            loads[3 * step + i].wait()
        gate_pre = dot(x_rows[...], weights[0][:, part])
        up_pre = dot(x_rows[...], weights[1][:, part])
        hidden_grad = dot_rows(g_rows[...], weights[2][part, :])
        if waiting is not None:
            back(*waiting, step == 1)
        sig = jax.nn.sigmoid(gate_pre)
        gate_grad = (hidden_grad * up_pre * sig * (1.0 + gate_pre * (1.0 - sig))).astype(BF16)
        up_grad = (hidden_grad * gate_pre * sig).astype(BF16)
        waiting = (part, gate_grad, up_grad)
    back(*waiting, False)
    slots_to_chunks(tiles, sources, blocks, chunks, 0)
    out_ref[...] = chunks[:, : blocks * SLOT, :].astype(BF16)


def mlp(received, w_gate, w_up, w_down):
    sources, chunk_rows, _ = received.shape
    _, width, hidden = w_gate.shape
    blocks = width // LANES
    slots = sources * SLOT
    return pl.pallas_call(
        mlp_kernel,
        out_shape=jax.ShapeDtypeStruct((sources, blocks * SLOT, LANES), BF16),
        in_specs=[VMEM] + [ANY] * 3,
        out_specs=VMEM,
        scratch_shapes=[
            pltpu.VMEM((width, hidden), BF16),
            pltpu.VMEM((width, hidden), BF16),
            pltpu.VMEM((hidden, width), BF16),
            pltpu.VMEM((sources, chunk_rows, LANES), F32),
            pltpu.VMEM((blocks, slots, LANES), F32),
            pltpu.VMEM((slots, width), BF16),
            pltpu.VMEM((slots, width), BF16),
            pltpu.SemaphoreType.DMA((9,)),
        ],
        compiler_params=pltpu.CompilerParams(vmem_limit_bytes=58 * MIB),
        cost_estimate=pl.CostEstimate(
            flops=10 * slots * width * hidden, bytes_accessed=11 * 1024 * 1024, transcendentals=slots * hidden
        ),
        name="experts",
    )(received, w_gate, w_up, w_down)


def combine_kernel(weight_ref, back_ref, out_ref, chunks, tiles):
    experts = back_ref.shape[0]
    blocks = out_ref.shape[1] // LANES
    chunks[...] = back_ref[...].astype(F32)
    weight = weight_ref[...].T
    high = weight.astype(BF16)
    rest = weight - high.astype(F32)
    middle = rest.astype(BF16)
    low = (rest - middle.astype(F32)).astype(BF16)
    for block in range(blocks):
        for expert in range(experts):
            at = block * SLOT
            tiles[block, expert * SLOT : (expert + 1) * SLOT, :] = chunks[expert, at : at + SLOT, :]
    for pair in range(blocks // 2):
        rows = jnp.concatenate([tiles[2 * pair], tiles[2 * pair + 1]], axis=1).astype(BF16)
        out = dot(high, rows) + (dot(middle, rows) + dot(low, rows))
        out_ref[:, pair * 2 * LANES : (pair + 1) * 2 * LANES] = out.astype(BF16)


def combine(weight, back):
    experts, chunk_rows, _ = back.shape
    slots, rows = weight.shape
    blocks = chunk_rows // SLOT
    return pl.pallas_call(
        combine_kernel,
        out_shape=jax.ShapeDtypeStruct((rows, blocks * LANES), BF16),
        in_specs=[VMEM, VMEM],
        out_specs=VMEM,
        scratch_shapes=[
            pltpu.VMEM((experts, chunk_rows, LANES), F32),
            pltpu.VMEM((blocks, slots, LANES), F32),
        ],
        compiler_params=pltpu.CompilerParams(vmem_limit_bytes=12 * MIB),
        name="combine",
    )(weight, back)


def on_device(
    queries,
    key_tensor,
    value_tensor,
    out_grad,
    log_norm,
    out_dot,
    span_order,
    moe_input,
    moe_grad,
    expert_ids,
    keep_mask,
    route_weight,
    w_gate,
    w_up,
    w_down,
):
    rows, heads, size = queries.shape
    group = heads // 2
    scale = 1.0 / math.sqrt(size)
    members = lax.axis_size("ctx")
    experts = lax.axis_size("exp")
    first = lax.axis_index("ctx") & 1 == 0
    chips = members // 2
    trade = lambda array, k: lax.ppermute(array, "ctx", [(i, i ^ k) for i in range(members)])

    kv = jnp.stack([key_tensor, value_tensor]).reshape(2 * rows, 2, size)
    kv_own = jnp.where(first, kv[:, 0], kv[:, 1])
    kv_away = jnp.where(first, kv[:, 1], kv[:, 0])
    kv_own, kv_away, expert_ids = lax.optimization_barrier((kv_own, kv_away, expert_ids))
    kv_got = trade(kv_away, 1)
    kv_near, kv_cross = trade(kv_own, 2), trade(kv_away, 3)
    send, weight = dispatch(expert_ids, keep_mask, route_weight, moe_input, moe_grad, experts)
    ordered = lambda mine, other: [jnp.where(first, mine, other), jnp.where(first, other, mine)]
    pieces = ordered(kv_own, kv_got) + ordered(kv_near, kv_cross)
    kv_pair = jnp.concatenate(pieces, axis=0)
    send, kv_pair = lax.optimization_barrier((send, kv_pair))
    received = lax.all_to_all(send, "exp", split_axis=0, concat_axis=0, tiled=True)
    kv_list = [trade(kv_pair, 4 * k) for k in range(1, chips // 2)]

    kv_near, queries, out_grad, log_norm, out_dot = lax.optimization_barrier(
        (kv_near, queries, out_grad, log_norm, out_dot)
    )

    def halves(array, axis):
        low, high = jnp.split(array, 2, axis=axis)
        return jnp.where(first, low, high), jnp.where(first, high, low)

    q_own, q_away = halves(queries, 1)
    d_own, d_away = halves(out_grad, 1)
    stat_own, stat_away = halves(jnp.stack([log_norm.T, out_dot.T]), 1)
    q_got, d_got = trade(q_away, 1), trade(d_away, 1)
    stat_got = trade(stat_away, 1)

    spans = lambda array: array.reshape(2, rows // 2 * group, size)
    shared = (span_order, spans(q_own), spans(q_got), spans(d_own), spans(d_got))
    dq_near, own_sum, stats = attention_near(
        *shared, stat_own.reshape(2 * group, rows), stat_got.reshape(2 * group, rows), kv_pair, scale
    )
    dq_own, dq_got, *parts = attention_far(*shared, stats, dq_near, kv_list, scale)
    received, _ = lax.optimization_barrier((received, parts[0]))
    slot_grad = mlp(received, w_gate, w_up, w_down)
    returned = lax.all_to_all(slot_grad, "exp", split_axis=0, concat_axis=0, tiled=True)

    total, _ = lax.optimization_barrier((own_sum, slot_grad))
    for k in range(1, chips // 2):
        total = total + trade(parts[k - 1], 4 * k).astype(F32)
    blocks = [total[i * rows : (i + 1) * rows] for i in range(4)]
    mine, near = ordered(blocks[0], blocks[1]), ordered(blocks[2], blocks[3])
    own_head = mine[0] + trade(near[0].astype(BF16), 2).astype(F32)
    other_head = trade(mine[1].astype(BF16), 1).astype(F32) + trade(near[1].astype(BF16), 3).astype(F32)
    dq_got, _ = lax.optimization_barrier((dq_got, slot_grad))
    dq_back = trade(dq_got, 1)

    def joined(own, other):
        return jnp.concatenate(ordered(own, other), axis=1)

    grad_queries = joined(dq_own.reshape(rows, group, size), dq_back.reshape(rows, group, size))
    kv_grads = joined(own_head.astype(BF16)[:, None, :], other_head.astype(BF16)[:, None, :])
    grad_moe = combine(weight, returned)
    return grad_queries, kv_grads[:, :, :size], kv_grads[:, :, size:], grad_moe


def solution(mesh):
    rows = P(("ctx", "exp"))
    in_specs = (rows,) * 6 + (P(),) + (rows,) * 5 + (P("exp"),) * 3
    return jax.shard_map(
        on_device, mesh=mesh, in_specs=in_specs, out_specs=(rows,) * 4, check_vma=False
    )
```

```python
import functools
import math

import jax
import jax.numpy as jnp
from jax import lax
from jax.experimental import pallas as pl
from jax.experimental.pallas import tpu as pltpu
from jax.sharding import PartitionSpec as P

SLOT = 10
LANES = 128
CHUNK = 256
LONG = 1024
MIB = 1024 * 1024
VMEM = pl.BlockSpec(memory_space=pltpu.VMEM)
SMEM = pl.BlockSpec(memory_space=pltpu.SMEM)
ANY = pl.BlockSpec(memory_space=pl.ANY)
F32 = jnp.float32
BF16 = jnp.bfloat16


def dot(left, right):
    return jnp.dot(left, right, preferred_element_type=F32)


def dot_rows(left, right):
    return lax.dot_general(left, right, (((1,), (1,)), ((), ())), preferred_element_type=F32)


def dot_cols(left, right):
    return lax.dot_general(left, right, (((0,), (0,)), ((), ())), preferred_element_type=F32)


def split3(array):
    high = array.astype(BF16)
    rest = array - high.astype(F32)
    middle = rest.astype(BF16)
    return high, middle, (rest - middle.astype(F32)).astype(BF16)


def span_finder(span_ref):
    slots = span_ref.shape[0]

    def span_of(chip, core, upper):
        place = chip * 2 + core
        return span_ref[slots - 1 - place if upper else place]

    return span_of


def pair_gradients(scale, queries, grads, norm, inner, keys, values, keys_t, visible):
    scores = dot_rows(keys, queries)
    probs = jnp.exp2(scores * (scale / math.log(2.0)) - norm)
    if visible is not None:
        probs = jnp.where(visible(scores.shape), probs, 0.0)
    dprobs = dot_rows(values, grads)
    dscores = (probs * (dprobs - inner)).astype(BF16)
    return dot(dscores, queries), dot(probs.astype(BF16), grads), dot(keys_t, dscores)


def near_kernel(
    scale, span_ref, q_own, q_got, d_own, d_got, stat_own, stat_got, kv_ref, dq_ref, sum_ref, stat_ref, keys, values, keys_t, key_pos
):
    me = lax.axis_index("ctx")
    chip, core = me // 2, me % 2
    span_of = span_finder(span_ref)
    width = q_own.shape[1]
    count = kv_ref.shape[0] // 2
    half = count // 8
    repeat = width // half

    stats = jnp.concatenate([stat_own[...], stat_got[...]], axis=0)
    rows = stats.shape[1]
    wide = rows * repeat
    spread = (
        lax.broadcasted_iota(jnp.int32, (rows, wide), 1) // repeat
        == lax.broadcasted_iota(jnp.int32, (rows, wide), 0)
    ).astype(F32).astype(BF16)
    high, middle, low = split3(stats)
    lanes = dot(high, spread) + (dot(middle, spread) + dot(low, spread))
    lanes = lanes.reshape(stats.shape[0] // repeat, repeat, wide)
    head = lax.broadcasted_iota(jnp.int32, lanes.shape, 1)
    lane_head = lax.broadcasted_iota(jnp.int32, lanes.shape, 2) % repeat
    lanes = jnp.sum(jnp.where(head == lane_head, lanes, 0.0), axis=1)
    is_norm = lax.broadcasted_iota(jnp.int32, lanes.shape, 0) % 2 == 0
    stat_ref[...] = jnp.where(is_norm, lanes * (1.0 / math.log(2.0)), lanes)

    for device in range(4):
        at = slice(device * 2 * half, (device + 1) * 2 * half)
        keys[at, :] = kv_ref[device * 4 * half : device * 4 * half + 2 * half, :]
        values[at, :] = kv_ref[device * 4 * half + 2 * half : (device + 1) * 4 * half, :]
    keys_t[...] = keys[...].T
    for part in range(8):
        span = span_of(chip ^ (part // 4), part // 2 % 2, part % 2)
        at = slice(part * half, (part + 1) * half)
        key_pos[at, :] = span * half + lax.broadcasted_iota(jnp.int32, (half, LANES), 0)

    for index in range(4):
        upper = index % 2
        q_ref, d_ref, who = (q_own, d_own, core) if index < 2 else (q_got, d_got, 1 - core)
        line = 2 * (index // 2)
        span = span_of(chip, who, upper)

        def visible(shape):
            query_pos = span * half + lax.broadcasted_iota(jnp.int32, shape, 1) // repeat
            return jnp.concatenate([key_pos[...]] * (width // LANES), axis=1) <= query_pos

        at = slice(upper * width, (upper + 1) * width)
        dk, dv, dq = pair_gradients(
            scale,
            q_ref[upper],
            d_ref[upper],
            stat_ref[line : line + 1, at],
            stat_ref[line + 1 : line + 2, at],
            keys[...],
            values[...],
            keys_t[...],
            visible,
        )
        dq_ref[index] = dq
        dk = dk * scale
        sum_ref[:, :LANES] = dk if index == 0 else sum_ref[:, :LANES] + dk
        sum_ref[:, LANES:] = dv if index == 0 else sum_ref[:, LANES:] + dv


def far_kernel(scale, kv_blocks, span_ref, q_own, q_got, d_own, d_got, stat_ref, dq_ref, *rest):
    kv_refs = rest[:kv_blocks]
    dq_own, dq_got = rest[kv_blocks : kv_blocks + 2]
    part_refs = rest[kv_blocks + 2 : 2 * kv_blocks + 2]
    keys, values, keys_t, dk_acc, dv_acc, dq_acc, before = rest[2 * kv_blocks + 2 :]
    me = lax.axis_index("ctx")
    chip, core = me // 2, me % 2
    span_of = span_finder(span_ref)
    slots = span_ref.shape[0]
    width = q_own.shape[1]
    half = kv_refs[0].shape[0] // 16

    for n in range(slots):
        before[n] = 0
    spans = [
        [span_of(chip ^ (2 * (block + 1) + part // 4), part // 2 % 2, part % 2) for part in range(8)]
        for block in range(kv_blocks)
    ]
    for line in spans:
        for span in line:
            before[span] = 1
    running = 0
    for n in range(slots):
        here = before[n]
        before[n] = running
        running = running + here

    def place(block, part):
        return pl.ds(pl.multiple_of(before[spans[block][part]] * half, half), half)

    for block in range(kv_blocks):
        for part in range(8):
            at = place(block, part)
            first = (part // 2 * 4 + part % 2) * half
            keys[at, :] = kv_refs[block][first : first + half, :]
            values[at, :] = kv_refs[block][first + 2 * half : first + 3 * half, :]
    for chunk in range(keys.shape[0] // CHUNK):
        at = slice(chunk * CHUNK, (chunk + 1) * CHUNK)
        keys_t[:, at] = keys[at, :].T
    dk_acc[...] = jnp.zeros_like(dk_acc)
    dv_acc[...] = jnp.zeros_like(dv_acc)

    for index in range(4):
        upper = index % 2
        q_ref, d_ref, out_ref, who = (q_own, d_own, dq_own, core) if index < 2 else (q_got, d_got, dq_got, 1 - core)
        line = 2 * (index // 2)
        lanes = slice(upper * width, (upper + 1) * width)
        queries = q_ref[upper]
        grads = d_ref[upper]
        norm = stat_ref[line : line + 1, lanes]
        inner = stat_ref[line + 1 : line + 2, lanes]
        dq_acc[...] = dq_ref[index]
        ahead = before[span_of(chip, who, upper)] * half

        def one(start, count, masked):
            at = pl.ds(pl.multiple_of(start, CHUNK), count)
            seen = lambda shape: start + lax.broadcasted_iota(jnp.int32, shape, 0) < ahead
            dk, dv, dq = pair_gradients(
                scale, queries, grads, norm, inner, keys[at, :], values[at, :], keys_t[:, at], seen if masked else None
            )
            dk_acc[at, :] += dk
            dv_acc[at, :] += dv
            dq_acc[...] += dq

        long = ahead // LONG * LONG
        tail = ahead // (LONG // 2) * (LONG // 2)

        @pl.when(long > 0)
        def _():
            one(0, LONG, False)

        @pl.when(tail > long)
        def _():
            one(long, LONG // 2, False)

        @pl.when(ahead - tail > CHUNK)
        def _():
            one(tail, LONG // 2, True)

        @pl.when((ahead > tail) & (ahead - tail <= CHUNK))
        def _():
            one(tail, CHUNK, True)

        out_ref[upper] = (dq_acc[...].T * scale).astype(BF16)

    for block in range(kv_blocks):
        for part in range(8):
            at = place(block, part)
            rows = slice(part * half, (part + 1) * half)
            part_refs[block][rows, :LANES] = (dk_acc[at, :] * scale).astype(BF16)
            part_refs[block][rows, LANES:] = dv_acc[at, :].astype(BF16)


def attention_near(span_order, q_own, q_got, d_own, d_got, stat_own, stat_got, kv, scale):
    count = kv.shape[0] // 2
    halves, width, size = q_own.shape
    assert count * 2 == LONG
    return pl.pallas_call(
        functools.partial(near_kernel, scale),
        out_shape=(
            jax.ShapeDtypeStruct((2 * halves, size, width), F32),
            jax.ShapeDtypeStruct((count, 2 * LANES), F32),
            jax.ShapeDtypeStruct((4, halves * width), F32),
        ),
        in_specs=[SMEM] + [VMEM] * 7,
        out_specs=(VMEM,) * 3,
        scratch_shapes=[
            pltpu.VMEM((count, LANES), BF16),
            pltpu.VMEM((count, LANES), BF16),
            pltpu.VMEM((LANES, count), BF16),
            pltpu.VMEM((count, LANES), jnp.int32),
        ],
        compiler_params=pltpu.CompilerParams(vmem_limit_bytes=16 * MIB),
        cost_estimate=pl.CostEstimate(
            flops=20 * halves * width * count * size,
            bytes_accessed=3 * MIB,
            transcendentals=2 * halves * width * count,
        ),
        name="attention_near",
    )(span_order, q_own, q_got, d_own, d_got, stat_own, stat_got, kv)


def attention_far(span_order, q_own, q_got, d_own, d_got, stats, dq_near, kv_list, scale):
    blocks = len(kv_list)
    rows = kv_list[0].shape[0] // 2
    total = blocks * rows
    halves, width, size = q_own.shape
    assert total % LONG == LONG // 2
    part = jax.ShapeDtypeStruct((rows, 2 * LANES), BF16)
    return pl.pallas_call(
        functools.partial(far_kernel, scale, blocks),
        out_shape=(jax.ShapeDtypeStruct(q_own.shape, BF16),) * 2 + (part,) * blocks,
        in_specs=[SMEM] + [VMEM] * (6 + blocks),
        out_specs=(VMEM,) * (2 + blocks),
        scratch_shapes=[
            pltpu.VMEM((total, LANES), BF16),
            pltpu.VMEM((total, LANES), BF16),
            pltpu.VMEM((LANES, total), BF16),
            pltpu.VMEM((total, LANES), F32),
            pltpu.VMEM((total, LANES), F32),
            pltpu.VMEM((LANES, width), F32),
            pltpu.SMEM(span_order.shape, jnp.int32),
        ],
        compiler_params=pltpu.CompilerParams(vmem_limit_bytes=16 * MIB),
        cost_estimate=pl.CostEstimate(
            flops=20 * halves * width * total * size,
            bytes_accessed=6 * MIB,
            transcendentals=2 * halves * width * total,
        ),
        name="attention_far",
    )(span_order, q_own, q_got, d_own, d_got, stats, dq_near, *kv_list)


def slots_to_chunks(tiles, experts, blocks, chunk_ref, first):
    for expert in range(experts):
        for block in range(blocks):
            at = first + block * SLOT
            chunk_ref[expert, at : at + SLOT, :] = tiles[block, expert * SLOT : (expert + 1) * SLOT, :]


def dispatch_kernel(*refs):
    sources, (send_ref, combine_ref), targets, (tiles, chunks, sems) = refs[:5], refs[5:7], refs[7:12], refs[12:]
    ids_ref, keep_ref, weight_ref, x_ref, g_ref = targets
    loads = [pltpu.make_async_copy(*pair, sems.at[i]) for i, pair in enumerate(zip(sources, targets))]
    for load in loads:
        load.start()
    for load in loads[:3]:
        load.wait()
    top, rows = ids_ref.shape
    experts = send_ref.shape[0]
    blocks = x_ref.shape[1] // LANES
    slots = experts * SLOT
    line = lax.broadcasted_iota(jnp.int32, (slots, rows), 0)
    expert_of = line // SLOT
    slot_of = line - expert_of * SLOT
    ids = jnp.where(keep_ref[...] == 1, ids_ref[...], -1)
    weights = weight_ref[...]
    hit = jnp.zeros((slots, rows), F32)
    weight = jnp.zeros((slots, rows), F32)
    for k in range(top):
        match = ids[k : k + 1, :] == expert_of
        hit = jnp.where(match, 1.0, hit)
        weight = jnp.where(match, weights[k : k + 1, :], weight)
    earlier = (
        lax.broadcasted_iota(jnp.int32, (rows, rows), 0)
        < lax.broadcasted_iota(jnp.int32, (rows, rows), 1)
    ).astype(F32).astype(BF16)
    rank = dot(hit.astype(BF16), earlier)
    chosen = jnp.where(rank == slot_of.astype(F32), hit, 0.0)
    combine_ref[...] = chosen * weight
    pick = chosen.astype(BF16)
    for load, source, first in ((loads[3], x_ref, 0), (loads[4], g_ref, blocks * SLOT)):
        load.wait()
        for pair in range(blocks // 2):
            both = dot(pick, source[:, pair * 2 * LANES : (pair + 1) * 2 * LANES])
            tiles[2 * pair] = both[:, :LANES]
            tiles[2 * pair + 1] = both[:, LANES:]
        slots_to_chunks(tiles, experts, blocks, chunks, first)
    send_ref[...] = chunks[...].astype(BF16)


def dispatch(ids, keep, weight, x, g, experts):
    rows = ids.shape[0]
    blocks = x.shape[1] // LANES
    slots = experts * SLOT
    return pl.pallas_call(
        dispatch_kernel,
        out_shape=(
            jax.ShapeDtypeStruct((experts, 2 * blocks * SLOT, LANES), BF16),
            jax.ShapeDtypeStruct((slots, rows), F32),
        ),
        in_specs=[ANY] * 5,
        out_specs=(VMEM, VMEM),
        scratch_shapes=[
            pltpu.VMEM(ids.T.shape, ids.dtype),
            pltpu.VMEM(ids.T.shape, keep.dtype),
            pltpu.VMEM(ids.T.shape, weight.dtype),
            pltpu.VMEM(x.shape, BF16),
            pltpu.VMEM(g.shape, BF16),
            pltpu.VMEM((blocks, slots, LANES), F32),
            pltpu.VMEM((experts, 2 * blocks * SLOT, LANES), F32),
            pltpu.SemaphoreType.DMA((5,)),
        ],
        compiler_params=pltpu.CompilerParams(vmem_limit_bytes=60 * MIB),
        name="dispatch",
    )(ids.T, keep.T, weight.T, x, g)


def mlp_kernel(in_ref, *rest):
    weights_hbm = rest[:3]
    out_ref = rest[3]
    weights = rest[4:7]
    chunks, tiles, x_rows, g_rows, sems = rest[7:]
    sources = in_ref.shape[0]
    blocks = x_rows.shape[1] // LANES
    hidden = weights[0].shape[1]
    tile = 256
    loads = []
    edges = [0, tile // 2, hidden // 2, hidden]
    parts = [slice(low, high) for low, high in zip(edges, edges[1:])]
    for step, part in enumerate(parts):
        for i in range(3):
            at = (slice(None), part) if i < 2 else (part, slice(None))
            load = pltpu.make_async_copy(weights_hbm[i].at[(0,) + at], weights[i].at[at], sems.at[3 * step + i])
            loads.append(load)
    for load in loads[:3]:
        load.start()
    chunks[...] = in_ref[...].astype(F32)
    for rows_ref, first in ((x_rows, 0), (g_rows, blocks * SLOT)):
        for block in range(blocks):
            for source in range(sources):
                at = first + block * SLOT
                tiles[block, source * SLOT : (source + 1) * SLOT, :] = chunks[source, at : at + SLOT, :]
            rows_ref[:, block * LANES : (block + 1) * LANES] = tiles[block].astype(BF16)
    for load in loads[3:]:
        load.start()

    def back(part, gate_grad, up_grad, fresh):
        term = dot_rows(gate_grad, weights[0][:, part]) + dot_rows(up_grad, weights[1][:, part])
        for block in range(blocks):
            piece = term[:, block * LANES : (block + 1) * LANES]
            tiles[block] = piece if fresh else tiles[block] + piece

    waiting = None
    for step, part in enumerate(parts):
        for i in range(3):
            loads[3 * step + i].wait()
        gate_pre = dot(x_rows[...], weights[0][:, part])
        up_pre = dot(x_rows[...], weights[1][:, part])
        hidden_grad = dot_rows(g_rows[...], weights[2][part, :])
        if waiting is not None:
            back(*waiting, step == 1)
        sig = jax.nn.sigmoid(gate_pre)
        gate_grad = (hidden_grad * up_pre * sig * (1.0 + gate_pre * (1.0 - sig))).astype(BF16)
        up_grad = (hidden_grad * gate_pre * sig).astype(BF16)
        waiting = (part, gate_grad, up_grad)
    back(*waiting, False)
    slots_to_chunks(tiles, sources, blocks, chunks, 0)
    out_ref[...] = chunks[:, : blocks * SLOT, :].astype(BF16)


def mlp(received, w_gate, w_up, w_down):
    sources, chunk_rows, _ = received.shape
    _, width, hidden = w_gate.shape
    blocks = width // LANES
    slots = sources * SLOT
    return pl.pallas_call(
        mlp_kernel,
        out_shape=jax.ShapeDtypeStruct((sources, blocks * SLOT, LANES), BF16),
        in_specs=[VMEM] + [ANY] * 3,
        out_specs=VMEM,
        scratch_shapes=[
            pltpu.VMEM((width, hidden), BF16),
            pltpu.VMEM((width, hidden), BF16),
            pltpu.VMEM((hidden, width), BF16),
            pltpu.VMEM((sources, chunk_rows, LANES), F32),
            pltpu.VMEM((blocks, slots, LANES), F32),
            pltpu.VMEM((slots, width), BF16),
            pltpu.VMEM((slots, width), BF16),
            pltpu.SemaphoreType.DMA((9,)),
        ],
        compiler_params=pltpu.CompilerParams(vmem_limit_bytes=58 * MIB),
        cost_estimate=pl.CostEstimate(
            flops=10 * slots * width * hidden, bytes_accessed=11 * 1024 * 1024, transcendentals=slots * hidden
        ),
        name="experts",
    )(received, w_gate, w_up, w_down)


def combine_kernel(weight_ref, back_ref, out_ref, chunks, tiles):
    experts = back_ref.shape[0]
    blocks = out_ref.shape[1] // LANES
    chunks[...] = back_ref[...].astype(F32)
    weight = weight_ref[...].T
    high, middle, _ = split3(weight)
    for block in range(blocks):
        for expert in range(experts):
            at = block * SLOT
            tiles[block, expert * SLOT : (expert + 1) * SLOT, :] = chunks[expert, at : at + SLOT, :]
    for pair in range(blocks // 2):
        rows = jnp.concatenate([tiles[2 * pair], tiles[2 * pair + 1]], axis=1).astype(BF16)
        out = dot(high, rows) + dot(middle, rows)
        out_ref[:, pair * 2 * LANES : (pair + 1) * 2 * LANES] = out.astype(BF16)


def combine(weight, back):
    experts, chunk_rows, _ = back.shape
    slots, rows = weight.shape
    blocks = chunk_rows // SLOT
    return pl.pallas_call(
        combine_kernel,
        out_shape=jax.ShapeDtypeStruct((rows, blocks * LANES), BF16),
        in_specs=[VMEM, VMEM],
        out_specs=VMEM,
        scratch_shapes=[
            pltpu.VMEM((experts, chunk_rows, LANES), F32),
            pltpu.VMEM((blocks, slots, LANES), F32),
        ],
        compiler_params=pltpu.CompilerParams(vmem_limit_bytes=12 * MIB),
        name="combine",
    )(weight, back)


def on_device(
    queries,
    key_tensor,
    value_tensor,
    out_grad,
    log_norm,
    out_dot,
    span_order,
    moe_input,
    moe_grad,
    expert_ids,
    keep_mask,
    route_weight,
    w_gate,
    w_up,
    w_down,
):
    rows, heads, size = queries.shape
    group = heads // 2
    scale = 1.0 / math.sqrt(size)
    members = lax.axis_size("ctx")
    experts = lax.axis_size("exp")
    first = lax.axis_index("ctx") & 1 == 0
    chips = members // 2
    trade = lambda array, k: lax.ppermute(array, "ctx", [(i, i ^ k) for i in range(members)])

    kv = jnp.stack([key_tensor, value_tensor]).reshape(2 * rows, 2, size)
    kv_own = jnp.where(first, kv[:, 0], kv[:, 1])
    kv_away = jnp.where(first, kv[:, 1], kv[:, 0])
    kv_own, kv_away, expert_ids = lax.optimization_barrier((kv_own, kv_away, expert_ids))
    kv_got = trade(kv_away, 1)
    kv_near, kv_cross = trade(kv_own, 2), trade(kv_away, 3)
    send, weight = dispatch(expert_ids, keep_mask, route_weight, moe_input, moe_grad, experts)
    ordered = lambda mine, other: [jnp.where(first, mine, other), jnp.where(first, other, mine)]
    pieces = ordered(kv_own, kv_got) + ordered(kv_near, kv_cross)
    kv_pair = jnp.concatenate(pieces, axis=0)
    send, _ = lax.optimization_barrier((send, kv_got))
    received = lax.all_to_all(send, "exp", split_axis=0, concat_axis=0, tiled=True)
    kv_list = [trade(kv_pair, 4 * k) for k in range(1, chips // 2)]

    kv_near, queries, out_grad, log_norm, out_dot = lax.optimization_barrier(
        (kv_near, queries, out_grad, log_norm, out_dot)
    )

    def halves(array, axis):
        low, high = jnp.split(array, 2, axis=axis)
        return jnp.where(first, low, high), jnp.where(first, high, low)

    q_own, q_away = halves(queries, 1)
    d_own, d_away = halves(out_grad, 1)
    stat_own, stat_away = halves(jnp.stack([log_norm.T, out_dot.T]), 1)
    q_got, d_got = trade(q_away, 1), trade(d_away, 1)
    stat_got = trade(stat_away, 1)

    spans = lambda array: array.reshape(2, rows // 2 * group, size)
    shared = (span_order, spans(q_own), spans(q_got), spans(d_own), spans(d_got))
    dq_near, own_sum, stats = attention_near(
        *shared, stat_own.reshape(2 * group, rows), stat_got.reshape(2 * group, rows), kv_pair, scale
    )
    dq_own, dq_got, *parts = attention_far(*shared, stats, dq_near, kv_list, scale)
    received, _ = lax.optimization_barrier((received, parts[0]))
    slot_grad = mlp(received, w_gate, w_up, w_down)
    returned = lax.all_to_all(slot_grad, "exp", split_axis=0, concat_axis=0, tiled=True)

    total, _ = lax.optimization_barrier((own_sum, slot_grad))
    for k in range(1, chips // 2):
        total = total + trade(parts[k - 1], 4 * k).astype(F32)
    blocks = [total[i * rows : (i + 1) * rows] for i in range(4)]
    mine, near = ordered(blocks[0], blocks[1]), ordered(blocks[2], blocks[3])
    own_head = mine[0] + trade(near[0].astype(BF16), 2).astype(F32)
    other_head = trade(mine[1].astype(BF16), 1).astype(F32) + trade(near[1].astype(BF16), 3).astype(F32)
    dq_got, _ = lax.optimization_barrier((dq_got, slot_grad))
    dq_back = trade(dq_got, 1)

    def joined(own, other):
        return jnp.concatenate(ordered(own, other), axis=1)

    grad_queries = joined(dq_own.reshape(rows, group, size), dq_back.reshape(rows, group, size))
    kv_grads = joined(own_head.astype(BF16)[:, None, :], other_head.astype(BF16)[:, None, :])
    grad_moe = combine(weight, returned)
    return grad_queries, kv_grads[:, :, :size], kv_grads[:, :, size:], grad_moe


def solution(mesh):
    rows = P(("ctx", "exp"))
    in_specs = (rows,) * 6 + (P(),) + (rows,) * 5 + (P("exp"),) * 3
    return jax.shard_map(
        on_device, mesh=mesh, in_specs=in_specs, out_specs=(rows,) * 4, check_vma=False
    )
```

```python
import functools
import math

import jax
import jax.numpy as jnp
from jax import lax
from jax.experimental import pallas as pl
from jax.experimental.pallas import tpu as pltpu
from jax.sharding import PartitionSpec as P

SLOT = 10
LANES = 128
CHUNK = 256
LONG = 1024
MIB = 1024 * 1024
VMEM = pl.BlockSpec(memory_space=pltpu.VMEM)
SMEM = pl.BlockSpec(memory_space=pltpu.SMEM)
ANY = pl.BlockSpec(memory_space=pl.ANY)
F32 = jnp.float32
BF16 = jnp.bfloat16


def dot(left, right):
    return jnp.dot(left, right, preferred_element_type=F32)


def dot_rows(left, right):
    return lax.dot_general(left, right, (((1,), (1,)), ((), ())), preferred_element_type=F32)


def dot_cols(left, right):
    return lax.dot_general(left, right, (((0,), (0,)), ((), ())), preferred_element_type=F32)


def split3(array):
    high = array.astype(BF16)
    rest = array - high.astype(F32)
    middle = rest.astype(BF16)
    return high, middle, (rest - middle.astype(F32)).astype(BF16)


def span_finder(span_ref):
    slots = span_ref.shape[0]

    def span_of(chip, core, upper):
        place = chip * 2 + core
        return span_ref[slots - 1 - place if upper else place]

    return span_of


def pair_gradients(scale, queries, grads, norm, inner, keys, values, keys_t, visible):
    scores = dot_rows(keys, queries)
    probs = jnp.exp2(scores * (scale / math.log(2.0)) - norm)
    if visible is not None:
        probs = jnp.where(visible(scores.shape), probs, 0.0)
    dprobs = dot_rows(values, grads)
    dscores = (probs * (dprobs - inner)).astype(BF16)
    return dot(dscores, queries), dot(probs.astype(BF16), grads), dot(keys_t, dscores)


def near_kernel(
    scale, span_ref, q_own, q_got, d_own, d_got, stat_own, stat_got, kv_ref, dq_ref, sum_ref, stat_ref, keys, values, keys_t, key_pos
):
    me = lax.axis_index("ctx")
    chip, core = me // 2, me % 2
    span_of = span_finder(span_ref)
    width = q_own.shape[1]
    count = kv_ref.shape[0] // 2
    half = count // 8
    repeat = width // half

    stats = jnp.concatenate([stat_own[...], stat_got[...]], axis=0)
    rows = stats.shape[1]
    wide = rows * repeat
    spread = (
        lax.broadcasted_iota(jnp.int32, (rows, wide), 1) // repeat
        == lax.broadcasted_iota(jnp.int32, (rows, wide), 0)
    ).astype(F32).astype(BF16)
    high, middle, low = split3(stats)
    lanes = dot(high, spread) + (dot(middle, spread) + dot(low, spread))
    lanes = lanes.reshape(stats.shape[0] // repeat, repeat, wide)
    head = lax.broadcasted_iota(jnp.int32, lanes.shape, 1)
    lane_head = lax.broadcasted_iota(jnp.int32, lanes.shape, 2) % repeat
    lanes = jnp.sum(jnp.where(head == lane_head, lanes, 0.0), axis=1)
    is_norm = lax.broadcasted_iota(jnp.int32, lanes.shape, 0) % 2 == 0
    stat_ref[...] = jnp.where(is_norm, lanes * (1.0 / math.log(2.0)), lanes)

    for device in range(4):
        at = slice(device * 2 * half, (device + 1) * 2 * half)
        keys[at, :] = kv_ref[device * 4 * half : device * 4 * half + 2 * half, :]
        values[at, :] = kv_ref[device * 4 * half + 2 * half : (device + 1) * 4 * half, :]
    keys_t[...] = keys[...].T
    for part in range(8):
        span = span_of(chip ^ (part // 4), part // 2 % 2, part % 2)
        at = slice(part * half, (part + 1) * half)
        key_pos[at, :] = span * half + lax.broadcasted_iota(jnp.int32, (half, LANES), 0)

    for index in range(4):
        upper = index % 2
        q_ref, d_ref, who = (q_own, d_own, core) if index < 2 else (q_got, d_got, 1 - core)
        line = 2 * (index // 2)
        span = span_of(chip, who, upper)

        def visible(shape):
            query_pos = span * half + lax.broadcasted_iota(jnp.int32, shape, 1) // repeat
            return jnp.concatenate([key_pos[...]] * (width // LANES), axis=1) <= query_pos

        at = slice(upper * width, (upper + 1) * width)
        dk, dv, dq = pair_gradients(
            scale,
            q_ref[upper],
            d_ref[upper],
            stat_ref[line : line + 1, at],
            stat_ref[line + 1 : line + 2, at],
            keys[...],
            values[...],
            keys_t[...],
            visible,
        )
        dq_ref[index] = dq
        dk = dk * scale
        sum_ref[:, :LANES] = dk if index == 0 else sum_ref[:, :LANES] + dk
        sum_ref[:, LANES:] = dv if index == 0 else sum_ref[:, LANES:] + dv


def far_kernel(scale, kv_blocks, span_ref, q_own, q_got, d_own, d_got, stat_ref, dq_ref, *rest):
    kv_refs = rest[:kv_blocks]
    dq_own, dq_got = rest[kv_blocks : kv_blocks + 2]
    part_refs = rest[kv_blocks + 2 : 2 * kv_blocks + 2]
    keys, values, keys_t, dk_acc, dv_acc, dq_acc, before = rest[2 * kv_blocks + 2 :]
    me = lax.axis_index("ctx")
    chip, core = me // 2, me % 2
    span_of = span_finder(span_ref)
    slots = span_ref.shape[0]
    width = q_own.shape[1]
    half = kv_refs[0].shape[0] // 16

    for n in range(slots):
        before[n] = 0
    spans = [
        [span_of(chip ^ (2 * (block + 1) + part // 4), part // 2 % 2, part % 2) for part in range(8)]
        for block in range(kv_blocks)
    ]
    for line in spans:
        for span in line:
            before[span] = 1
    running = 0
    for n in range(slots):
        here = before[n]
        before[n] = running
        running = running + here

    def place(block, part):
        return pl.ds(pl.multiple_of(before[spans[block][part]] * half, half), half)

    for block in range(kv_blocks):
        for part in range(8):
            at = place(block, part)
            first = (part // 2 * 4 + part % 2) * half
            keys[at, :] = kv_refs[block][first : first + half, :]
            values[at, :] = kv_refs[block][first + 2 * half : first + 3 * half, :]
    for chunk in range(keys.shape[0] // CHUNK):
        at = slice(chunk * CHUNK, (chunk + 1) * CHUNK)
        keys_t[:, at] = keys[at, :].T
    dk_acc[...] = jnp.zeros_like(dk_acc)
    dv_acc[...] = jnp.zeros_like(dv_acc)

    for index in range(4):
        upper = index % 2
        q_ref, d_ref, out_ref, who = (q_own, d_own, dq_own, core) if index < 2 else (q_got, d_got, dq_got, 1 - core)
        line = 2 * (index // 2)
        lanes = slice(upper * width, (upper + 1) * width)
        queries = q_ref[upper]
        grads = d_ref[upper]
        norm = stat_ref[line : line + 1, lanes]
        inner = stat_ref[line + 1 : line + 2, lanes]
        dq_acc[...] = dq_ref[index]
        ahead = before[span_of(chip, who, upper)] * half

        def one(start, count, masked):
            at = pl.ds(pl.multiple_of(start, CHUNK), count)
            seen = lambda shape: start + lax.broadcasted_iota(jnp.int32, shape, 0) < ahead
            dk, dv, dq = pair_gradients(
                scale, queries, grads, norm, inner, keys[at, :], values[at, :], keys_t[:, at], seen if masked else None
            )
            dk_acc[at, :] += dk
            dv_acc[at, :] += dv
            dq_acc[...] += dq

        long = ahead // LONG * LONG
        tail = ahead // (LONG // 2) * (LONG // 2)

        @pl.when(long > 0)
        def _():
            one(0, LONG, False)

        @pl.when(tail > long)
        def _():
            one(long, LONG // 2, False)

        @pl.when(ahead - tail > CHUNK)
        def _():
            one(tail, LONG // 2, True)

        @pl.when((ahead > tail) & (ahead - tail <= CHUNK))
        def _():
            one(tail, CHUNK, True)

        out_ref[upper] = (dq_acc[...].T * scale).astype(BF16)

    for block in range(kv_blocks):
        for part in range(8):
            at = place(block, part)
            rows = slice(part * half, (part + 1) * half)
            part_refs[block][rows, :LANES] = (dk_acc[at, :] * scale).astype(BF16)
            part_refs[block][rows, LANES:] = dv_acc[at, :].astype(BF16)


def attention_near(span_order, q_own, q_got, d_own, d_got, stat_own, stat_got, kv, scale):
    count = kv.shape[0] // 2
    halves, width, size = q_own.shape
    assert count * 2 == LONG
    return pl.pallas_call(
        functools.partial(near_kernel, scale),
        out_shape=(
            jax.ShapeDtypeStruct((2 * halves, size, width), F32),
            jax.ShapeDtypeStruct((count, 2 * LANES), F32),
            jax.ShapeDtypeStruct((4, halves * width), F32),
        ),
        in_specs=[SMEM] + [VMEM] * 7,
        out_specs=(VMEM,) * 3,
        scratch_shapes=[
            pltpu.VMEM((count, LANES), BF16),
            pltpu.VMEM((count, LANES), BF16),
            pltpu.VMEM((LANES, count), BF16),
            pltpu.VMEM((count, LANES), jnp.int32),
        ],
        compiler_params=pltpu.CompilerParams(vmem_limit_bytes=16 * MIB),
        cost_estimate=pl.CostEstimate(
            flops=20 * halves * width * count * size,
            bytes_accessed=3 * MIB,
            transcendentals=2 * halves * width * count,
        ),
        name="attention_near",
    )(span_order, q_own, q_got, d_own, d_got, stat_own, stat_got, kv)


def attention_far(span_order, q_own, q_got, d_own, d_got, stats, dq_near, kv_list, scale):
    blocks = len(kv_list)
    rows = kv_list[0].shape[0] // 2
    total = blocks * rows
    halves, width, size = q_own.shape
    assert total % LONG == LONG // 2
    part = jax.ShapeDtypeStruct((rows, 2 * LANES), BF16)
    return pl.pallas_call(
        functools.partial(far_kernel, scale, blocks),
        out_shape=(jax.ShapeDtypeStruct(q_own.shape, BF16),) * 2 + (part,) * blocks,
        in_specs=[SMEM] + [VMEM] * (6 + blocks),
        out_specs=(VMEM,) * (2 + blocks),
        scratch_shapes=[
            pltpu.VMEM((total, LANES), BF16),
            pltpu.VMEM((total, LANES), BF16),
            pltpu.VMEM((LANES, total), BF16),
            pltpu.VMEM((total, LANES), F32),
            pltpu.VMEM((total, LANES), F32),
            pltpu.VMEM((LANES, width), F32),
            pltpu.SMEM(span_order.shape, jnp.int32),
        ],
        compiler_params=pltpu.CompilerParams(vmem_limit_bytes=16 * MIB),
        cost_estimate=pl.CostEstimate(
            flops=20 * halves * width * total * size,
            bytes_accessed=6 * MIB,
            transcendentals=2 * halves * width * total,
        ),
        name="attention_far",
    )(span_order, q_own, q_got, d_own, d_got, stats, dq_near, *kv_list)


def slots_to_chunks(tiles, experts, blocks, chunk_ref, first):
    for expert in range(experts):
        for block in range(blocks):
            at = first + block * SLOT
            chunk_ref[expert, at : at + SLOT, :] = tiles[block, expert * SLOT : (expert + 1) * SLOT, :]


def dispatch_kernel(*refs):
    sources, (send_ref, combine_ref), targets, (tiles, chunks, sems) = refs[:5], refs[5:7], refs[7:12], refs[12:]
    ids_ref, keep_ref, weight_ref, x_ref, g_ref = targets
    loads = [pltpu.make_async_copy(*pair, sems.at[i]) for i, pair in enumerate(zip(sources, targets))]
    for load in loads:
        load.start()
    for load in loads[:3]:
        load.wait()
    top, rows = ids_ref.shape
    experts = send_ref.shape[0]
    blocks = x_ref.shape[1] // LANES
    slots = experts * SLOT
    line = lax.broadcasted_iota(jnp.int32, (slots, rows), 0)
    expert_of = line // SLOT
    slot_of = line - expert_of * SLOT
    ids = jnp.where(keep_ref[...] == 1, ids_ref[...], -1)
    weights = weight_ref[...]
    hit = jnp.zeros((slots, rows), F32)
    weight = jnp.zeros((slots, rows), F32)
    for k in range(top):
        match = ids[k : k + 1, :] == expert_of
        hit = jnp.where(match, 1.0, hit)
        weight = jnp.where(match, weights[k : k + 1, :], weight)
    earlier = (
        lax.broadcasted_iota(jnp.int32, (rows, rows), 0)
        < lax.broadcasted_iota(jnp.int32, (rows, rows), 1)
    ).astype(F32).astype(BF16)
    rank = dot(hit.astype(BF16), earlier)
    chosen = jnp.where(rank == slot_of.astype(F32), hit, 0.0)
    combine_ref[...] = chosen * weight
    pick = chosen.astype(BF16)
    for load, source, first in ((loads[3], x_ref, 0), (loads[4], g_ref, blocks * SLOT)):
        load.wait()
        for pair in range(blocks // 2):
            both = dot(pick, source[:, pair * 2 * LANES : (pair + 1) * 2 * LANES])
            tiles[2 * pair] = both[:, :LANES]
            tiles[2 * pair + 1] = both[:, LANES:]
        slots_to_chunks(tiles, experts, blocks, chunks, first)
    send_ref[...] = chunks[...].astype(BF16)


def dispatch(ids, keep, weight, x, g, experts):
    rows = ids.shape[0]
    blocks = x.shape[1] // LANES
    slots = experts * SLOT
    return pl.pallas_call(
        dispatch_kernel,
        out_shape=(
            jax.ShapeDtypeStruct((experts, 2 * blocks * SLOT, LANES), BF16),
            jax.ShapeDtypeStruct((slots, rows), F32),
        ),
        in_specs=[ANY] * 5,
        out_specs=(VMEM, VMEM),
        scratch_shapes=[
            pltpu.VMEM(ids.T.shape, ids.dtype),
            pltpu.VMEM(ids.T.shape, keep.dtype),
            pltpu.VMEM(ids.T.shape, weight.dtype),
            pltpu.VMEM(x.shape, BF16),
            pltpu.VMEM(g.shape, BF16),
            pltpu.VMEM((blocks, slots, LANES), F32),
            pltpu.VMEM((experts, 2 * blocks * SLOT, LANES), F32),
            pltpu.SemaphoreType.DMA((5,)),
        ],
        compiler_params=pltpu.CompilerParams(vmem_limit_bytes=60 * MIB),
        name="dispatch",
    )(ids.T, keep.T, weight.T, x, g)


def mlp_kernel(in_ref, *rest):
    weights_hbm = rest[:3]
    out_ref = rest[3]
    weights = rest[4:7]
    chunks, tiles, x_rows, g_rows, sems = rest[7:]
    sources = in_ref.shape[0]
    blocks = x_rows.shape[1] // LANES
    hidden = weights[0].shape[1]
    tile = 256
    loads = []
    edges = [0, tile // 2, hidden // 2, hidden]
    parts = [slice(low, high) for low, high in zip(edges, edges[1:])]
    for step, part in enumerate(parts):
        for i in range(3):
            at = (slice(None), part) if i < 2 else (part, slice(None))
            load = pltpu.make_async_copy(weights_hbm[i].at[(0,) + at], weights[i].at[at], sems.at[3 * step + i])
            loads.append(load)
    for load in loads[:3]:
        load.start()
    chunks[...] = in_ref[...].astype(F32)
    for rows_ref, first in ((x_rows, 0), (g_rows, blocks * SLOT)):
        for block in range(blocks):
            for source in range(sources):
                at = first + block * SLOT
                tiles[block, source * SLOT : (source + 1) * SLOT, :] = chunks[source, at : at + SLOT, :]
            rows_ref[:, block * LANES : (block + 1) * LANES] = tiles[block].astype(BF16)
    for load in loads[3:]:
        load.start()

    def back(part, gate_grad, up_grad, fresh):
        term = dot_rows(gate_grad, weights[0][:, part]) + dot_rows(up_grad, weights[1][:, part])
        for block in range(blocks):
            piece = term[:, block * LANES : (block + 1) * LANES]
            tiles[block] = piece if fresh else tiles[block] + piece

    waiting = None
    for step, part in enumerate(parts):
        for i in range(3):
            loads[3 * step + i].wait()
        gate_pre = dot(x_rows[...], weights[0][:, part])
        up_pre = dot(x_rows[...], weights[1][:, part])
        hidden_grad = dot_rows(g_rows[...], weights[2][part, :])
        if waiting is not None:
            back(*waiting, step == 1)
        sig = jax.nn.sigmoid(gate_pre)
        gate_grad = (hidden_grad * up_pre * sig * (1.0 + gate_pre * (1.0 - sig))).astype(BF16)
        up_grad = (hidden_grad * gate_pre * sig).astype(BF16)
        waiting = (part, gate_grad, up_grad)
    back(*waiting, False)
    slots_to_chunks(tiles, sources, blocks, chunks, 0)
    out_ref[...] = chunks[:, : blocks * SLOT, :].astype(BF16)


def mlp(received, w_gate, w_up, w_down):
    sources, chunk_rows, _ = received.shape
    _, width, hidden = w_gate.shape
    blocks = width // LANES
    slots = sources * SLOT
    return pl.pallas_call(
        mlp_kernel,
        out_shape=jax.ShapeDtypeStruct((sources, blocks * SLOT, LANES), BF16),
        in_specs=[VMEM] + [ANY] * 3,
        out_specs=VMEM,
        scratch_shapes=[
            pltpu.VMEM((width, hidden), BF16),
            pltpu.VMEM((width, hidden), BF16),
            pltpu.VMEM((hidden, width), BF16),
            pltpu.VMEM((sources, chunk_rows, LANES), F32),
            pltpu.VMEM((blocks, slots, LANES), F32),
            pltpu.VMEM((slots, width), BF16),
            pltpu.VMEM((slots, width), BF16),
            pltpu.SemaphoreType.DMA((9,)),
        ],
        compiler_params=pltpu.CompilerParams(vmem_limit_bytes=58 * MIB),
        cost_estimate=pl.CostEstimate(
            flops=10 * slots * width * hidden, bytes_accessed=11 * 1024 * 1024, transcendentals=slots * hidden
        ),
        name="experts",
    )(received, w_gate, w_up, w_down)


def combine_kernel(weight_ref, back_ref, out_ref, chunks, tiles):
    experts = back_ref.shape[0]
    blocks = out_ref.shape[1] // LANES
    chunks[...] = back_ref[...].astype(F32)
    weight = weight_ref[...].T
    high, middle, _ = split3(weight)
    for block in range(blocks):
        for expert in range(experts):
            at = block * SLOT
            tiles[block, expert * SLOT : (expert + 1) * SLOT, :] = chunks[expert, at : at + SLOT, :]
    for pair in range(blocks // 2):
        rows = jnp.concatenate([tiles[2 * pair], tiles[2 * pair + 1]], axis=1).astype(BF16)
        out = dot(high, rows) + dot(middle, rows)
        out_ref[:, pair * 2 * LANES : (pair + 1) * 2 * LANES] = out.astype(BF16)


def combine(weight, back):
    experts, chunk_rows, _ = back.shape
    slots, rows = weight.shape
    blocks = chunk_rows // SLOT
    return pl.pallas_call(
        combine_kernel,
        out_shape=jax.ShapeDtypeStruct((rows, blocks * LANES), BF16),
        in_specs=[VMEM, VMEM],
        out_specs=VMEM,
        scratch_shapes=[
            pltpu.VMEM((experts, chunk_rows, LANES), F32),
            pltpu.VMEM((blocks, slots, LANES), F32),
        ],
        compiler_params=pltpu.CompilerParams(vmem_limit_bytes=12 * MIB),
        name="combine",
    )(weight, back)


def on_device(
    queries,
    key_tensor,
    value_tensor,
    out_grad,
    log_norm,
    out_dot,
    span_order,
    moe_input,
    moe_grad,
    expert_ids,
    keep_mask,
    route_weight,
    w_gate,
    w_up,
    w_down,
):
    rows, heads, size = queries.shape
    group = heads // 2
    scale = 1.0 / math.sqrt(size)
    members = lax.axis_size("ctx")
    experts = lax.axis_size("exp")
    first = lax.axis_index("ctx") & 1 == 0
    chips = members // 2
    trade = lambda array, k: lax.ppermute(array, "ctx", [(i, i ^ k) for i in range(members)])

    kv = jnp.stack([key_tensor, value_tensor]).reshape(2 * rows, 2, size)
    kv_own = jnp.where(first, kv[:, 0], kv[:, 1])
    kv_away = jnp.where(first, kv[:, 1], kv[:, 0])
    kv_own, kv_away, expert_ids = lax.optimization_barrier((kv_own, kv_away, expert_ids))
    kv_got = trade(kv_away, 1)
    kv_near, kv_cross = trade(kv_own, 2), trade(kv_away, 3)
    send, weight = dispatch(expert_ids, keep_mask, route_weight, moe_input, moe_grad, experts)
    ordered = lambda mine, other: [jnp.where(first, mine, other), jnp.where(first, other, mine)]
    pieces = ordered(kv_own, kv_got) + ordered(kv_near, kv_cross)
    kv_pair = jnp.concatenate(pieces, axis=0)
    send, kv_pair = lax.optimization_barrier((send, kv_pair))
    received = lax.all_to_all(send, "exp", split_axis=0, concat_axis=0, tiled=True)
    by_y = {k: trade(kv_pair, 4 * k) for k in sorted(range(1, chips // 2), key=lambda k: k == chips // 4)}
    kv_list = [by_y[k] for k in range(1, chips // 2)]

    kv_near, queries, out_grad, log_norm, out_dot = lax.optimization_barrier(
        (kv_near, queries, out_grad, log_norm, out_dot)
    )

    def halves(array, axis):
        low, high = jnp.split(array, 2, axis=axis)
        return jnp.where(first, low, high), jnp.where(first, high, low)

    q_own, q_away = halves(queries, 1)
    d_own, d_away = halves(out_grad, 1)
    stat_own, stat_away = halves(jnp.stack([log_norm.T, out_dot.T]), 1)
    q_got, d_got = trade(q_away, 1), trade(d_away, 1)
    stat_got = trade(stat_away, 1)

    spans = lambda array: array.reshape(2, rows // 2 * group, size)
    shared = (span_order, spans(q_own), spans(q_got), spans(d_own), spans(d_got))
    dq_near, own_sum, stats = attention_near(
        *shared, stat_own.reshape(2 * group, rows), stat_got.reshape(2 * group, rows), kv_pair, scale
    )
    dq_own, dq_got, *parts = attention_far(*shared, stats, dq_near, kv_list, scale)
    received, _ = lax.optimization_barrier((received, parts[0]))
    slot_grad = mlp(received, w_gate, w_up, w_down)
    returned = lax.all_to_all(slot_grad, "exp", split_axis=0, concat_axis=0, tiled=True)

    total, _ = lax.optimization_barrier((own_sum, slot_grad))
    for k in range(1, chips // 2):
        total = total + trade(parts[k - 1], 4 * k).astype(F32)
    blocks = [total[i * rows : (i + 1) * rows] for i in range(4)]
    mine, near = ordered(blocks[0], blocks[1]), ordered(blocks[2], blocks[3])
    own_head = mine[0] + trade(near[0].astype(BF16), 2).astype(F32)
    other_head = trade(mine[1].astype(BF16), 1).astype(F32) + trade(near[1].astype(BF16), 3).astype(F32)
    dq_got, _ = lax.optimization_barrier((dq_got, slot_grad))
    dq_back = trade(dq_got, 1)

    def joined(own, other):
        return jnp.concatenate(ordered(own, other), axis=1)

    grad_queries = joined(dq_own.reshape(rows, group, size), dq_back.reshape(rows, group, size))
    kv_grads = joined(own_head.astype(BF16)[:, None, :], other_head.astype(BF16)[:, None, :])
    grad_moe = combine(weight, returned)
    return grad_queries, kv_grads[:, :, :size], kv_grads[:, :, size:], grad_moe


def solution(mesh):
    rows = P(("ctx", "exp"))
    in_specs = (rows,) * 6 + (P(),) + (rows,) * 5 + (P("exp"),) * 3
    return jax.shard_map(
        on_device, mesh=mesh, in_specs=in_specs, out_specs=(rows,) * 4, check_vma=False
    )
```
